256 devices in a mesh: queue: 64 (over x, z_hi, y), space: 4 (over z_lo, core).
Axes of the slice: x: 4, y: 4, z: 8 (z_hi: 4, z_lo: 2; z = z_hi * 2 + z_lo), core: 2. Of those that a mesh axis runs over, the one named last changes fastest.
Arguments:
- latents: float32 [128, 2048], P('queue', 'space'), may hold values from -6 to 6
- fresh_noise: float32 [2, 2, 2048], P(None, None, 'space'), may hold values from -6 to 6
- level_index: int32 [64, 2], P('queue'), may hold values from 0 to 29
- step_sizes: float32 [30], replicated, may hold values from 0.1 to 0.6
- time_table: float32 [30, 2, 1152], replicated, may hold values from -2 to 2
- embed_in: float32 [16, 1152], replicated, may hold values from -1.5 to 1.5
- spatial_qkv: bfloat16 [1152, 3, 1152], P('queue', None, 'space'), as said below
- spatial_out: bfloat16 [1152, 1152], P('space', 'queue'), may hold values from -0.1875 to 0.1875
- temporal_qkv: bfloat16 [1152, 3, 1152], P('queue', None, 'space'), as said below
- temporal_out: bfloat16 [1152, 1152], P('space', 'queue'), may hold values from -0.1875 to 0.1875
- embed_out: float32 [1152, 16], replicated, may hold values from -0.1875 to 0.1875
Outputs:
- queue_state: float32 [128, 2048], P('queue', 'space')
The draws below stay inside these ranges and needn't reach their ends.
Inputs may be any that keep to these rules, and one draw needn't show every extreme that they name: `spatial_qkv`: query and value weights of order 1152 ** -0.5; key weights of that order or larger. `temporal_qkv`: query and value weights of order 1152 ** -0.5; key weights of that order or larger.
All inputs are finite; a program needn't handle non-finite values.
Results may differ from the reference program's by a relative error of at most 0.0065.
Values may be sent and summed in bfloat16 or wider, within the bound.
A program may use at most 128 MiB of HBM per device.

```python
import math
import jax
import jax.numpy as jnp
from jax import lax

D = 1152
HEADS = 16
PATCH = 16
FRAMES = 2
SPATIAL = 128
REACH = 1
LEVELS = 30
STEPS = 2
SPANS = 64
QFRAMES = 128


def draw_spatial_qkv(key, part):
    key = jax.random.fold_in(key, 11)
    weights = jax.random.normal(jax.random.fold_in(key, 1), (D, 3, D), jnp.float32) * (1.0 / math.sqrt(D))
    return weights.astype(jnp.bfloat16)


def draw_temporal_qkv(key, part):
    key = jax.random.fold_in(key, 23)
    weights = jax.random.normal(jax.random.fold_in(key, 1), (D, 3, D), jnp.float32) * (1.0 / math.sqrt(D))
    return weights.astype(jnp.bfloat16)


def plant(result, rng, least, top_value):
    longest = result.shape.index(max(result.shape))
    spots = []
    for shift in (0, 1):
        where = [jax.random.randint(jax.random.fold_in(rng, axis), (), 0, length) for axis, length in enumerate(result.shape)]
        where[longest] = (where[longest] + shift) % result.shape[longest]
        spots.append(tuple(where))
    return result.at[spots[0]].set(least).at[spots[1]].set(top_value)


def steps_of(key, shape, split, low, high):
    def one(dim, shards_of):
        heights = jax.random.uniform(jax.random.fold_in(jax.random.fold_in(key, 6), dim), (shards_of,), jnp.float32, low / len(split), high / len(split))
        return jnp.repeat(jnp.exp(heights), shape[dim] // shards_of).reshape((-1,) + (1,) * (len(shape) - dim - 1))

    loudness = one(*split[0])
    for cut in split[1:]:
        loudness = loudness * one(*cut)
    return loudness


def bell_draw(own_key, extent, deviation, most, pieces=(), held_as=jnp.bfloat16):
    array = deviation * jax.random.normal(own_key, extent, jnp.float32)
    if pieces:
        array = array * steps_of(own_key, extent, pieces, -0.22, 0.18)
    return jnp.clip(array, -most, most).astype(held_as)


def setup_inputs(seed: int = 0) -> dict:
    key_list = jax.random.split(jax.random.key(seed), 12)
    return {
        "latents": bell_draw(key_list[0], (QFRAMES, SPATIAL * PATCH), 1.0, 6.0, ((0, 64), (1, 4)), jnp.float32),
        "fresh_noise": bell_draw(key_list[1], (STEPS, FRAMES, SPATIAL * PATCH), 1.0, 6.0, ((2, 4),), jnp.float32),
        "level_index": plant(jax.random.randint(key_list[2], (SPANS, STEPS), 0, LEVELS), jax.random.fold_in(key_list[2], 1), 0, LEVELS - 1).astype(jnp.int32),
        "step_sizes": jnp.clip(jnp.exp(jax.random.uniform(key_list[3], (LEVELS,), jnp.float32, math.log(0.1), math.log(0.6))), 0.1, 0.6),
        "time_table": bell_draw(key_list[4], (LEVELS, 2, D), 0.3, 2.0, (), jnp.float32),
        "embed_in": bell_draw(key_list[5], (PATCH, D), PATCH ** -0.5, 1.5, (), jnp.float32),
        "spatial_qkv": draw_spatial_qkv(jax.random.fold_in(key_list[11], 71), 0),
        "spatial_out": bell_draw(key_list[7], (D, D), D ** -0.5, 0.1875, ((0, 4), (1, 64))),
        "temporal_qkv": draw_temporal_qkv(jax.random.fold_in(key_list[11], 71), 0),
        "temporal_out": bell_draw(key_list[9], (D, D), D ** -0.5, 0.1875, ((0, 4), (1, 64))),
        "embed_out": bell_draw(key_list[10], (D, PATCH), D ** -0.5, 0.1875, (), jnp.float32),
    }


def rms_scale(values):
    return values * lax.rsqrt(lax.optimization_barrier(jnp.mean(values * values, axis=-1, keepdims=True)) + 1e-06)

def widen(values):
    return lax.optimization_barrier(values).astype(jnp.float32)

def project(normed, weights):
    flat = widen(normed).reshape(QFRAMES * SPATIAL, D)
    product = jnp.dot(flat, weights.astype(jnp.float32).reshape(D, 3 * D), precision=lax.Precision.HIGHEST)
    return product.astype(jnp.bfloat16).reshape(QFRAMES, SPATIAL, 3, HEADS, D // HEADS)

def out_project(mixed, weights):
    flat = widen(mixed).reshape(QFRAMES * SPATIAL, D)
    product = jnp.dot(flat, weights.astype(jnp.float32), precision=lax.Precision.HIGHEST)
    return product.reshape(QFRAMES, SPATIAL, D)

def reference(latents, fresh_noise, level_index, step_sizes, time_table, embed_in, spatial_qkv, spatial_out, temporal_qkv, temporal_out, embed_out):
    head_dim = D // HEADS
    inverse = 1.0 / head_dim ** 0.5
    table = time_table.reshape(LEVELS, 2 * D)
    frame_ids = jnp.arange(QFRAMES, dtype=jnp.int32)
    lat = latents
    for step in range(STEPS):
        levels_now = jnp.repeat(level_index[:, step], FRAMES)
        onehot = (levels_now[:, None] == jnp.arange(LEVELS, dtype=jnp.int32)[None, :]).astype(jnp.float32)
        modulation = jnp.dot(onehot, table, precision=lax.Precision.HIGHEST)
        shift_vec = modulation[:, None, :D]
        scale_vec = modulation[:, None, D:]
        size_now = jnp.dot(onehot, step_sizes, precision=lax.Precision.HIGHEST)
        hidden = jnp.dot(lat.reshape(QFRAMES * SPATIAL, PATCH), embed_in, precision=lax.Precision.HIGHEST)
        hidden = hidden.reshape(QFRAMES, SPATIAL, D)
        normed = (rms_scale(hidden) * (1.0 + scale_vec) + shift_vec).astype(jnp.bfloat16)
        qkv = project(normed, spatial_qkv)
        query, keys, values = (widen(qkv[:, :, 0]), widen(qkv[:, :, 1]), widen(qkv[:, :, 2]))
        scores = jnp.einsum('fshe,fthe->fhst', query, keys, precision=lax.Precision.HIGHEST) * inverse
        scores = jnp.exp(scores - lax.optimization_barrier(jnp.max(scores, axis=-1, keepdims=True)))
        probs = (scores / lax.optimization_barrier(jnp.sum(scores, axis=-1, keepdims=True))).astype(jnp.bfloat16)
        mixed = jnp.einsum('fhst,fthe->fshe', widen(probs), values, precision=lax.Precision.HIGHEST)
        mixed = mixed.astype(jnp.bfloat16).reshape(QFRAMES, SPATIAL, D)
        hidden = hidden + out_project(mixed, spatial_out)
        normed = (rms_scale(hidden) * (1.0 + scale_vec) + shift_vec).astype(jnp.bfloat16)
        qkv = project(normed, temporal_qkv)
        query, keys, values = (widen(qkv[:, :, 0]), widen(qkv[:, :, 1]), widen(qkv[:, :, 2]))
        padding = ((REACH, REACH), (0, 0), (0, 0), (0, 0))
        keys_pad = jnp.pad(keys, padding)
        values_pad = jnp.pad(values, padding)
        score_list = []
        for offset in range(2 * REACH + 1):
            band = lax.optimization_barrier(jnp.sum(query * keys_pad[offset:offset + QFRAMES], axis=-1)) * inverse
            source = frame_ids + offset - REACH
            inside = (source >= 0) & (source < QFRAMES)
            score_list.append(jnp.where(inside[:, None, None], band, jnp.float32(-1e+30)))
        scores = jnp.stack(score_list, axis=0)
        scores = jnp.exp(scores - lax.optimization_barrier(jnp.max(scores, axis=0, keepdims=True)))
        probs = widen((scores / lax.optimization_barrier(jnp.sum(scores, axis=0, keepdims=True))).astype(jnp.bfloat16))
        mixed = jnp.zeros((QFRAMES, SPATIAL, HEADS, head_dim), jnp.float32)
        for offset in range(2 * REACH + 1):
            mixed = mixed + probs[offset][..., None] * values_pad[offset:offset + QFRAMES]
        mixed = mixed.astype(jnp.bfloat16).reshape(QFRAMES, SPATIAL, D)
        hidden = hidden + out_project(mixed, temporal_out)
        velocity = jnp.dot(rms_scale(hidden).reshape(QFRAMES * SPATIAL, D), embed_out, precision=lax.Precision.HIGHEST)
        lat = lat - size_now[:, None] * velocity.reshape(QFRAMES, SPATIAL * PATCH)
        lat = jnp.concatenate([fresh_noise[step], lat[:QFRAMES - FRAMES]], axis=0)
    return lat
```

```python
import functools

import jax
import jax.numpy as jnp
from jax import lax
from jax.experimental import pallas as pl
from jax.experimental.pallas import tpu as pltpu
from jax.sharding import PartitionSpec as P

HEADS = 16
STEPS = 2
RING = 4
BF = jnp.bfloat16
F32 = jnp.float32


class Place:
    def __init__(self):
        q, s = lax.axis_index("queue"), lax.axis_index("space")
        self.q, self.s = q, s
        self.x, self.zh, self.y = q // 16, (q // 4) % 4, q % 4
        self.zl, self.c = s // 2, s % 2
        self.v = (1 - self.c) * self.y + self.c * self.x
        self.w = (1 - self.c) * self.x + self.c * self.y

    def cell(self, v, w):
        x = self.c * v + (1 - self.c) * w
        y = (1 - self.c) * v + self.c * w
        return x * 4 + y

    def ring(self, v, w):
        x = self.c * v + (1 - self.c) * w
        y = (1 - self.c) * v + self.c * w
        return ((x * 4 + self.zh) * 4 + y, self.s)

    def up(self, dz):
        return ((self.x * 4 + (self.zh + dz) % 4) * 4 + self.y, self.s)


def greet(partners):
    barrier = pltpu.get_barrier_semaphore()
    for partner in partners:
        pl.semaphore_signal(barrier, inc=1, device_id=partner, device_id_type=pl.DeviceIdType.MESH)
    pl.semaphore_wait(barrier, len(partners))


class Stream:
    def __init__(self, place, buf, send, recv, base):
        self.p, self.buf, self.send, self.recv, self.base = place, buf, send, recv, base
        self.ops = {}

    def copy(self, key, rows, count, target):
        i = self.base + len(self.ops)
        rows = pl.multiple_of(rows, 16)
        part = self.buf.at[pl.ds(rows, count)]
        op = pltpu.make_async_remote_copy(
            src_ref=part,
            dst_ref=part,
            send_sem=self.send.at[i],
            recv_sem=self.recv.at[i],
            device_id=target,
            device_id_type=pl.DeviceIdType.MESH,
        )
        op.start()
        self.ops[key] = op

    def z(self, piece):
        p = self.p
        row = pl.multiple_of((p.cell(p.v, p.w) * 4 + p.zh) * 16, 16)
        self.buf[pl.ds(row, 16), :] = piece[...]
        for d in (1, 3, 2):
            self.copy(("z", d), row, 16, p.up(d))

    def both(self, key, v, w, right, left):
        rows = self.p.cell(v, w) * 64
        self.copy((key, "R"), rows, 64, right)
        self.copy((key, "L"), rows, 64, left)

    def w_sends(self, k):
        p = self.p
        v = (p.v + (0, 3, 1, 2)[k]) % 4
        self.both(("w", k), v, p.w, p.ring(p.v, (p.w + 1) % 4), p.ring(p.v, (p.w + 3) % 4))

    def v1(self):
        p = self.p
        for d in (1, 3, 2):
            self.ops["z", d].wait_recv()
        self.both("v", p.v, p.w, p.ring((p.v + 1) % 4, p.w), p.ring((p.v + 3) % 4, p.w))
        self.w_sends(0)

    def v2(self):
        p = self.p
        self.ops["v", "R"].wait_recv()
        self.copy("vfR", p.cell((p.v + 3) % 4, p.w) * 64, 32, p.ring((p.v + 1) % 4, p.w))
        self.w_sends(1)
        self.ops["v", "L"].wait_recv()
        self.copy("vfL", p.cell((p.v + 1) % 4, p.w) * 64 + 32, 32, p.ring((p.v + 3) % 4, p.w))
        self.w_sends(2)

    def w_forward(self, k):
        p = self.p
        v = (p.v + (0, 3, 1, 2)[k]) % 4
        self.ops[("w", k), "R"].wait_recv()
        self.copy(("wfR", k), p.cell(v, (p.w + 3) % 4) * 64, 32, p.ring(p.v, (p.w + 1) % 4))
        self.ops[("w", k), "L"].wait_recv()
        self.copy(("wfL", k), p.cell(v, (p.w + 1) % 4) * 64 + 32, 32, p.ring(p.v, (p.w + 3) % 4))

    def v3(self):
        self.ops["vfR"].wait_recv()
        self.ops["vfL"].wait_recv()
        self.w_sends(3)

    def end(self):
        for k in range(4):
            self.ops["wfR", k].wait_recv()
            self.ops["wfL", k].wait_recv()

    def drain(self):
        for op in self.ops.values():
            op.wait_send()


COPIES = 23


def gather_kernel(g1_in, g2_in, g3_in, g4_in, g1, g2, g3, g4, send, recv):
    p = Place()
    partners = [p.up(d) for d in (1, 2, 3)]
    partners += [p.ring((p.v + d) % 4, p.w) for d in (1, 3)]
    partners += [p.ring(p.v, (p.w + d) % 4) for d in (1, 3)]
    greet(partners)
    streams = [
        Stream(p, buf, send, recv, COPIES * i) for i, buf in enumerate((g1, g2, g3, g4))
    ]
    for stream, piece in zip(streams, (g1_in, g2_in, g3_in, g4_in)):
        stream.z(piece)
    a, b, c, d = streams
    a.v1()
    a.v2()
    b.v1()
    a.w_forward(0)
    a.v3()
    b.v2()
    a.w_forward(1)
    a.w_forward(2)
    b.w_forward(0)
    b.v3()
    a.w_forward(3)
    c.v1()
    b.w_forward(1)
    b.w_forward(2)
    c.v2()
    b.w_forward(3)
    a.end()
    c.w_forward(0)
    c.v3()
    d.v1()
    c.w_forward(1)
    c.w_forward(2)
    d.v2()
    c.w_forward(3)
    b.end()
    d.w_forward(0)
    d.v3()
    d.w_forward(1)
    d.w_forward(2)
    d.w_forward(3)
    c.end()
    d.end()
    for stream in streams:
        stream.drain()


def gathered(*pieces):
    return pl.pallas_call(
        gather_kernel,
        out_shape=[jax.ShapeDtypeStruct((1024, a.shape[1]), a.dtype) for a in pieces],
        in_specs=[pl.BlockSpec(memory_space=pltpu.VMEM)] * 4,
        out_specs=[pl.BlockSpec(memory_space=pltpu.VMEM)] * 4,
        scratch_shapes=[
            pltpu.SemaphoreType.DMA((4 * COPIES,)),
            pltpu.SemaphoreType.DMA((4 * COPIES,)),
        ],
        compiler_params=pltpu.CompilerParams(
            collective_id=0, has_side_effects=True, vmem_limit_bytes=48 * 2**20
        ),
        name="gather_weights",
    )(*pieces)


def permuted(array):
    lead = array.shape[:-1]
    split = array.reshape(*lead, 4, 4, 4, 18)
    split = jnp.swapaxes(split, -2, -3)
    main, rest = split[..., :16], split[..., 16:]
    return jnp.concatenate([main.reshape(*lead, 1024), rest.reshape(*lead, 128)], axis=-1)


def pieces_of(spatial_qkv, spatial_out, temporal_qkv, temporal_out):
    qs, qt = spatial_qkv.reshape(18, 864), temporal_qkv.reshape(18, 864)
    os, ot = spatial_out.T, temporal_out.T
    rest = jnp.stack([qs[16], qs[17], qt[16], qt[17]]).reshape(4, 3, 288)
    rest_out = jnp.stack([os[16], os[17], ot[16], ot[17]]).reshape(4, 1, 288)
    rest = jnp.concatenate([rest, rest_out], axis=1).reshape(16, 288)
    pad = lambda a, n: jnp.pad(a, ((0, 0), (0, n - a.shape[1])))
    g1 = jnp.concatenate([pad(qs[:16], 896), pad(rest, 384)], axis=1)
    return g1, pad(os[:16], 384), pad(qt[:16], 896), pad(ot[:16], 384)


def rms_scale(values):
    return values * lax.rsqrt(jnp.mean(values * values, axis=-1, keepdims=True) + 1e-06)


def spatial_attend(query, keys, values, head_dim):
    frames, queries, columns = query.shape
    heads = columns // head_dim
    query = query.reshape(frames, queries, heads, head_dim)
    keys = keys.reshape(frames, keys.shape[1], heads, head_dim)
    values = values.reshape(frames, values.shape[1], heads, head_dim)
    scores = jnp.einsum("fshe,fthe->fhst", query, keys, preferred_element_type=jnp.float32) * (
        1.0 / head_dim**0.5
    )
    scores = jnp.exp(scores - jnp.max(scores, axis=-1, keepdims=True))
    probs = (scores / jnp.sum(scores, axis=-1, keepdims=True)).astype(jnp.bfloat16)
    mixed = jnp.einsum("fhst,fthe->fshe", probs, values, preferred_element_type=jnp.float32)
    return mixed.astype(jnp.bfloat16).reshape(frames, queries, columns)


def temporal_attend(query, keys, values, inside, head_dim):
    frames, tokens, columns = query.shape
    heads = columns // head_dim
    padded = keys.shape[0]
    query = query.reshape(frames, tokens, heads, head_dim)
    keys = keys.reshape(padded, tokens, heads, head_dim)
    values = values.reshape(padded, tokens, heads, head_dim)
    scores = jnp.einsum("fshe,gshe->fghs", query, keys, preferred_element_type=jnp.float32) * (
        1.0 / head_dim**0.5
    )
    scores = jnp.where(inside[:, :, None, None], scores, jnp.float32(-1e30))
    scores = jnp.exp(scores - jnp.max(scores, axis=1, keepdims=True))
    probs = (scores / jnp.sum(scores, axis=1, keepdims=True)).astype(jnp.bfloat16)
    mixed = jnp.einsum("fghs,gshe->fshe", probs, values, preferred_element_type=jnp.float32)
    return mixed.astype(jnp.bfloat16).reshape(frames, tokens, columns)


def per_device(
    latents,
    fresh_noise,
    level_index,
    step_sizes,
    time_table,
    embed_in,
    spatial_qkv,
    spatial_out,
    temporal_qkv,
    temporal_out,
    embed_out,
):
    frames = latents.shape[0]
    width = embed_in.shape[1]
    levels = step_sizes.shape[0]
    head_dim = width // HEADS
    queue_count = lax.axis_size("queue")
    position = lax.axis_index("queue")
    share = lax.axis_index("space")
    g1, g2, g3, g4 = gathered(*pieces_of(spatial_qkv, spatial_out, temporal_qkv, temporal_out))
    rest = g1[:, 896:1184].reshape(64, 4, 1152)
    rest_s, rest_t = rest[:, :2].reshape(128, 1152), rest[:, 2:].reshape(128, 1152)
    sp_qkv = jnp.concatenate([g1[:, :864], rest_s[:, :864]])
    tm_qkv = jnp.concatenate([g3[:, :864], rest_t[:, :864]])
    sp_out = jnp.concatenate([g2[:, :288], rest_s[:, 864:]])
    tm_out = jnp.concatenate([g4[:, :288], rest_t[:, 864:]])
    outs = lax.all_gather(jnp.stack([sp_out, tm_out]), "space", axis=2, tiled=True)
    sp_out, tm_out = outs[0], outs[1]
    whole = lax.all_gather(
        jnp.concatenate([latents, fresh_noise[0]]), "space", axis=1, tiled=True
    )
    lat, noise = whole[:2], whole[2:]
    frame_query = jnp.arange(2, dtype=jnp.int32)[:, None]
    frame_key = jnp.arange(4, dtype=jnp.int32)[None, :]
    global_key = position * frames + frame_key - 1
    inside = (
        (jnp.abs(frame_key - 1 - frame_query) <= 1)
        & (global_key >= 0)
        & (global_key < frames * queue_count)
    )
    table = permuted(time_table)
    embed_in, embed_out = permuted(embed_in), permuted(embed_out.T).T
    ring = [(i, (i + 1) % queue_count) for i in range(queue_count)]
    back = [(j, i) for i, j in ring]
    for step in range(STEPS):
        level = level_index[0, step]
        shift_vec, scale_vec = table[level, 0], table[level, 1]
        size_now = step_sizes[level]
        hidden = jnp.dot(lat.reshape(256, 16), embed_in, precision=lax.Precision.HIGHEST)
        normed = (rms_scale(hidden) * (1.0 + scale_vec) + shift_vec).astype(BF)
        qkv = jnp.dot(normed, sp_qkv, preferred_element_type=F32).astype(BF).reshape(2, 128, 3, 288)
        mixed = spatial_attend(qkv[:, :, 0], qkv[:, :, 1], qkv[:, :, 2], head_dim)
        mixed = lax.all_gather(mixed.reshape(256, 288), "space", axis=1, tiled=True)
        hidden = hidden + jnp.dot(mixed, sp_out.T, preferred_element_type=F32)
        normed = (rms_scale(hidden) * (1.0 + scale_vec) + shift_vec).astype(BF)
        qkv = jnp.dot(normed, tm_qkv, preferred_element_type=F32).astype(BF).reshape(2, 128, 3, 288)
        kv = qkv[:, :, 1:]
        before = lax.ppermute(kv[1:], "queue", ring)
        after = lax.ppermute(kv[:1], "queue", back)
        kv = jnp.concatenate([before, kv, after])
        mixed = temporal_attend(qkv[:, :, 0], kv[:, :, 0], kv[:, :, 1], inside, head_dim)
        mixed = lax.all_gather(mixed.reshape(256, 288), "space", axis=1, tiled=True)
        hidden = hidden + jnp.dot(mixed, tm_out.T, preferred_element_type=F32)
        velocity = jnp.dot(rms_scale(hidden), embed_out, precision=lax.Precision.HIGHEST)
        lat = lat - size_now * velocity.reshape(2, 2048)
        if step == 0:
            moved = lax.ppermute(lat, "queue", ring)
            lat = jnp.where(position == 0, noise, moved)
    lat = lax.dynamic_slice_in_dim(lat, share * 512, 512, axis=1)
    moved = lax.ppermute(lat, "queue", ring)
    return jnp.where(position == 0, fresh_noise[1], moved)


def solution(mesh):
    placed = (
        P("queue", "space"),
        P(None, None, "space"),
        P("queue", None),
        P(),
        P(),
        P(),
        P("queue", None, "space"),
        P("space", "queue"),
        P("queue", None, "space"),
        P("space", "queue"),
        P(),
    )
    return jax.shard_map(
        per_device, mesh=mesh, in_specs=placed, out_specs=P("queue", "space"), check_vma=False
    )
```

```python
import functools

import jax
import jax.numpy as jnp
from jax import lax
from jax.experimental import pallas as pl
from jax.experimental.pallas import tpu as pltpu
from jax.sharding import PartitionSpec as P

STEPS = 2
BF = jnp.bfloat16
F32 = jnp.float32


MESH = pl.DeviceIdType.MESH
MAIN, REST = 1024, 128
WIDTH = MAIN + REST
HEAD_COLUMNS = 288
HEAD_DIM = 72
INVERSE = 1.0 / HEAD_DIM**0.5
LANES = 384
COPIES = 160


class Place:
    def __init__(self):
        q, s = lax.axis_index("queue"), lax.axis_index("space")
        self.q, self.s = q, s
        self.x, self.zh, self.y = q // 16, (q // 4) % 4, q % 4
        self.zl, self.c = s // 2, s % 2
        self.v = (1 - self.c) * self.y + self.c * self.x
        self.w = (1 - self.c) * self.x + self.c * self.y
        self.zpeer = (q, (1 - self.zl) * 2 + self.c)
        self.cpeer = (q, self.zl * 2 + 1 - self.c)
        self.zcpeer = (q, (1 - self.zl) * 2 + 1 - self.c)
        self.next = ((q + 1) % 64, s)
        self.previous = ((q + 63) % 64, s)

    def cell(self, v, w):
        x = self.c * v + (1 - self.c) * w
        y = (1 - self.c) * v + self.c * w
        return x * 4 + y

    def ring(self, v, w):
        x = self.c * v + (1 - self.c) * w
        y = (1 - self.c) * v + self.c * w
        return ((x * 4 + self.zh) * 4 + y, self.s)

    def up(self, dz):
        return ((self.x * 4 + (self.zh + dz) % 4) * 4 + self.y, self.s)

    def beside(self, dz):
        z = (self.zh * 2 + self.zl + dz) % 8
        return ((self.x * 4 + z // 2) * 4 + self.y, (z % 2) * 2 + self.c)


class Copies:
    def __init__(self, send, recv):
        self.send, self.recv, self.started = send, recv, []

    def start(self, src, dst, target):
        i = len(self.started)
        assert i < COPIES
        op = pltpu.make_async_remote_copy(
            src_ref=src,
            dst_ref=dst,
            send_sem=self.send.at[i],
            recv_sem=self.recv.at[i],
            device_id=target,
            device_id_type=MESH,
        )
        op.start()
        self.started.append(op)
        return op

    def drain(self):
        for op in self.started:
            op.wait_send()


def greet(partners):
    barrier = pltpu.get_barrier_semaphore()
    for partner in partners:
        pl.semaphore_signal(barrier, inc=1, device_id=partner, device_id_type=MESH)
    pl.semaphore_wait(barrier, len(partners))


class Stream:
    def __init__(self, place, copies, buf, columns):
        self.p, self.copies, self.buf, self.columns = place, copies, buf, columns
        self.ops = {}

    def copy(self, key, rows, count, target):
        part = self.buf.at[pl.ds(pl.multiple_of(rows, 16), count), pl.ds(*self.columns)]
        self.ops[key] = self.copies.start(part, part, target)

    def z(self, piece):
        p = self.p
        row = pl.multiple_of((p.cell(p.v, p.w) * 4 + p.zh) * 16, 16)
        self.buf[pl.ds(row, 16), pl.ds(*self.columns)] = piece[...]
        for d in (1, 3, 2):
            self.copy(("z", d), row, 16, p.up(d))

    def both(self, key, v, w, right, left):
        rows = self.p.cell(v, w) * 64
        self.copy((key, "R"), rows, 64, right)
        self.copy((key, "L"), rows, 64, left)

    def w_sends(self, k):
        p = self.p
        v = (p.v + (0, 3, 1, 2)[k]) % 4
        self.both(("w", k), v, p.w, p.ring(p.v, (p.w + 1) % 4), p.ring(p.v, (p.w + 3) % 4))

    def v1(self):
        p = self.p
        for d in (1, 3, 2):
            self.ops["z", d].wait_recv()
        self.both("v", p.v, p.w, p.ring((p.v + 1) % 4, p.w), p.ring((p.v + 3) % 4, p.w))
        self.w_sends(0)

    def v2(self):
        p = self.p
        self.ops["v", "R"].wait_recv()
        self.copy("vfR", p.cell((p.v + 3) % 4, p.w) * 64, 32, p.ring((p.v + 1) % 4, p.w))
        self.w_sends(1)
        self.ops["v", "L"].wait_recv()
        self.copy("vfL", p.cell((p.v + 1) % 4, p.w) * 64 + 32, 32, p.ring((p.v + 3) % 4, p.w))
        self.w_sends(2)

    def w_forward(self, *blocks):
        p = self.p
        for k in blocks:
            v = (p.v + (0, 3, 1, 2)[k]) % 4
            self.ops[("w", k), "R"].wait_recv()
            self.copy(("wfR", k), p.cell(v, (p.w + 3) % 4) * 64, 32, p.ring(p.v, (p.w + 1) % 4))
            self.ops[("w", k), "L"].wait_recv()
            self.copy(("wfL", k), p.cell(v, (p.w + 1) % 4) * 64 + 32, 32, p.ring(p.v, (p.w + 3) % 4))

    def v3(self):
        self.ops["vfR"].wait_recv()
        self.ops["vfL"].wait_recv()
        self.w_sends(3)

    def end(self):
        for k in range(4):
            self.ops["wfR", k].wait_recv()
            self.ops["wfL", k].wait_recv()


class Spread:
    def __init__(self, place, copies, buf, first):
        self.p, self.copies, self.buf, self.first = place, copies, buf, first
        self.ops = []

    def part(self, slot, rows, count):
        return self.buf.at[pl.ds(pl.multiple_of(rows, 16), count), pl.ds(self.first + LANES * slot, LANES)]

    def block(self, dw, dz):
        p = self.p
        for v in range(4):
            rows = p.cell(v, (p.w + dw) % 4) * 64
            self.ops.append(
                self.copies.start(self.part(0, rows, 64), self.part(1, rows, 64), p.beside(dz))
            )

    def rest(self):
        self.ops.append(
            self.copies.start(self.part(0, MAIN, REST), self.part(1, MAIN, REST), self.p.zpeer)
        )

    def core(self, slot):
        return self.copies.start(
            self.part(slot, 0, WIDTH), self.part(slot + 2, 0, WIDTH), self.p.cpeer
        )

    def wait(self):
        for op in self.ops:
            op.wait_recv()


def nt_dot(a, b):
    return lax.dot_general(a, b, (((1,), (1,)), ((), ())), preferred_element_type=F32)


def dot(a, b):
    return jnp.dot(a, b, preferred_element_type=F32)


def halves(array):
    high = array.astype(BF)
    return high, (array - high.astype(F32)).astype(BF)


def head_masks(rows):
    lane = lax.broadcasted_iota(jnp.int32, (rows, HEAD_COLUMNS), 1)
    return [(lane >= HEAD_DIM * h) & (lane < HEAD_DIM * (h + 1)) for h in range(4)]


def kernel(
    g1_in,
    g2_in,
    g3_in,
    lat_in,
    noise_in,
    mods,
    sizes,
    embed_in,
    embed_out,
    out,
    first,
    out_s,
    second,
    lat_all,
    lat_next,
    lat_send,
    lat_last,
    last_send,
    hidden,
    normed,
    query,
    kv,
    before,
    after,
    mixes,
    mix_last,
    same_head,
    send,
    recv,
):
    p = Place()
    copies = Copies(send, recv)
    partners = [p.up(d) for d in (1, 2, 3)]
    partners += [p.ring((p.v + d) % 4, p.w) for d in (1, 3)]
    partners += [p.ring(p.v, (p.w + d) % 4) for d in (1, 3)]
    partners += [p.beside(1), p.beside(7), p.cpeer, p.zcpeer, p.next, p.previous]
    greet(partners)
    a = Stream(p, copies, first, (0, 1152))
    b = Stream(p, copies, out_s, (0, LANES))
    c = Stream(p, copies, second, (0, 1152))
    spread_s = Spread(p, copies, out_s, 0)
    spread_t = Spread(p, copies, second, 768)
    position = p.q

    a.z(g1_in)
    own_lat = lat_all.at[:, pl.ds(pl.multiple_of(p.s * 32, 32), 32)]
    lat_all[:, pl.ds(pl.multiple_of(p.s * 32, 32), 32), :] = lat_in[...]
    lat_ops = [copies.start(own_lat, own_lat, t) for t in (p.cpeer, p.zpeer, p.zcpeer)]

    row = lax.broadcasted_iota(jnp.int32, (HEAD_COLUMNS, HEAD_COLUMNS), 0)
    column = lax.broadcasted_iota(jnp.int32, (HEAD_COLUMNS, HEAD_COLUMNS), 1)
    same = jnp.zeros((HEAD_COLUMNS, HEAD_COLUMNS), F32)
    for h in range(4):
        low, high = HEAD_DIM * h, HEAD_DIM * (h + 1)
        inside = (row >= low) & (row < high) & (column >= low) & (column < high)
        same = jnp.where(inside, 1.0, same)
    same_head[...] = same.astype(BF)
    out_high, out_low = halves(embed_out[...])
    out_pair = jnp.concatenate([out_high.astype(F32), out_low.astype(F32)], axis=1).astype(BF)

    def embed(lat):
        hidden[...] = jnp.dot(lat, embed_in[...], precision=lax.Precision.HIGHEST)

    def normalise(step):
        shift, scale = mods[2 * step : 2 * step + 1, :], mods[2 * step + 1 : 2 * step + 2, :]

        def rows_of(i, carry):
            rows = pl.ds(pl.multiple_of(i * 32, 32), 32)
            h = hidden[rows, :]
            inverse = lax.rsqrt(jnp.mean(h * h, axis=-1, keepdims=True) + 1e-06)
            normed[rows, :] = (h * inverse * scale + shift).astype(BF)
            return carry

        lax.fori_loop(0, 8, rows_of, 0)

    def project_kv(weights, half):
        kv[half] = dot(normed[...], weights[:, 256:896]).astype(BF)

    def project_query(weights):
        query[...] = dot(normed[...], weights[:, :384])

    def attend_frame(half, frame, mix):
        rows = slice(128 * frame, 128 * frame + 128)
        masks = head_masks(128)
        q = query[rows, :HEAD_COLUMNS].astype(BF).astype(F32)
        both = kv[half, rows, :].astype(F32)
        k = both[:, 32 : 32 + HEAD_COLUMNS].astype(BF)
        v = both[:, 320 : 320 + HEAD_COLUMNS]
        q_heads = jnp.concatenate([jnp.where(m, q, 0.0).astype(BF) for m in masks], axis=0)
        v_heads = jnp.concatenate([jnp.where(m, v, 0.0).astype(BF) for m in masks], axis=0)
        scores = nt_dot(q_heads, k) * INVERSE
        scores = jnp.exp(scores - jnp.max(scores, axis=-1, keepdims=True))
        probs = (scores / jnp.sum(scores, axis=-1, keepdims=True)).astype(BF)
        probs = jnp.concatenate([probs[128 * h : 128 * h + 128] for h in range(4)], axis=1)
        mixed = dot(probs, v_heads)
        mixed = jnp.concatenate([mixed, jnp.zeros((128, LANES - HEAD_COLUMNS), F32)], axis=1)
        mix[rows, :LANES] = mixed.astype(BF)

    def start_mix(mix, frame):
        part = lambda slot: mix.at[pl.ds(128 * frame, 128), pl.ds(LANES * slot, LANES)]
        by_z = copies.start(part(0), part(1), p.zpeer)
        by_core = copies.start(part(0), part(2), p.cpeer)
        return by_z, by_core, part

    def finish_mix(started):
        last = []
        for by_z, _, part in started:
            by_z.wait_recv()
            last.append(copies.start(part(1), part(3), p.cpeer))
        for _, by_core, _ in started:
            by_core.wait_recv()
        for op in last:
            op.wait_recv()

    def temporal(half, prepare):
        halo = [
            copies.start(kv.at[half, pl.ds(128, 128)], before.at[half], p.next),
            copies.start(kv.at[half, pl.ds(0, 128)], after.at[half], p.previous),
        ]
        prepare()

        def keys_values(ref_value):
            both = ref_value.astype(F32)
            return both[:, 32 : 32 + HEAD_COLUMNS], both[:, 320 : 320 + HEAD_COLUMNS]

        def score(q, k):
            high, low = halves(q * k)
            same_now = same_head[...]
            return (dot(high, same_now) + dot(low, same_now)) * INVERSE

        q0 = query[:128, :HEAD_COLUMNS].astype(BF).astype(F32)
        q1 = query[128:, :HEAD_COLUMNS].astype(BF).astype(F32)
        k0, v0 = keys_values(kv[half, :128])
        k1, v1 = keys_values(kv[half, 128:])
        s00, s01, s10, s11 = score(q0, k0), score(q0, k1), score(q1, k0), score(q1, k1)

        def blend(sa, sb, sc, va, vb, vc):
            top = jnp.maximum(jnp.maximum(sa, sb), sc)
            ea, eb, ec = jnp.exp(sa - top), jnp.exp(sb - top), jnp.exp(sc - top)
            total = ea + eb + ec
            rounded = lambda e: (e / total).astype(BF).astype(F32)
            mixed = rounded(ea) * va + rounded(eb) * vb + rounded(ec) * vc
            return jnp.concatenate([jnp.zeros((128, LANES - HEAD_COLUMNS), F32), mixed], axis=1).astype(BF)

        halo[0].wait_recv()
        kb, vb = keys_values(before[half])
        sb = jnp.where(position == 0, -1e30, score(q0, kb))
        yield blend(sb, s00, s01, vb, v0, v1)
        halo[1].wait_recv()
        ka, va = keys_values(after[half])
        sa = jnp.where(position == 63, -1e30, score(q1, ka))
        yield blend(s10, s11, sa, v0, v1, va)

    def velocity(h):
        inverse = lax.rsqrt(jnp.mean(h * h, axis=-1, keepdims=True) + 1e-06)
        high, low = halves(h * inverse)
        a, b = dot(high, out_pair), dot(low, out_pair)
        return a[:, :16] + a[:, 16:32] + b[:, :16] + b[:, 16:32]

    def selected(j, t):
        target = lax.broadcasted_iota(jnp.int32, (REST, MAIN), 0)
        source = lax.broadcasted_iota(jnp.int32, (REST, MAIN), 1)
        choose = jnp.where(source == 8 * target - 4 * (target % 2) + 8 * t + j, 1.0, 0.0).astype(BF)
        return dot(choose, first[:MAIN, 768:1152])[:, 96:]

    a.v1()
    b.z(g2_in)
    a.v2()
    a.w_forward(0)
    a.v3()
    b.v1()
    for op in lat_ops:
        op.wait_recv()
    embed(lat_all[0:2].reshape(256, 16))
    normalise(0)
    a.w_forward(1, 2)
    b.v2()
    c.z(g3_in)
    a.w_forward(3)
    b.w_forward(0)
    b.v3()
    spread_s.block(0, 1)
    c.v1()
    a.end()

    blocks = [selected(j, 0) for j in range(4)]
    pad = jnp.zeros((REST, 96), F32)
    first[MAIN:, :896] = jnp.concatenate(blocks[:3] + [pad[:, :32]], axis=1).astype(BF)
    out_s[MAIN:, :LANES] = jnp.concatenate([blocks[3], pad], axis=1).astype(BF)
    spread_s.rest()
    b.w_forward(1, 2)
    c.v2()
    b.w_forward(3)
    spread_s.block(3, 1)
    spread_s.block(1, 7)
    project_kv(first, 0)
    project_query(first)
    c.w_forward(0)
    c.v3()
    spread_t.block(0, 1)
    b.end()
    spread_s.block(2, 7)
    cores_s = [spread_s.core(0)]
    mix = mixes.at[0]
    attend_frame(0, 0, mix)
    started = [start_mix(mix, 0)]
    c.w_forward(1, 2)
    attend_frame(0, 1, mix)
    started.append(start_mix(mix, 1))
    blocks = [selected(j, 1) for j in range(4)]
    second[MAIN:, :1152] = jnp.concatenate(blocks, axis=1).astype(BF)
    spread_t.rest()
    c.w_forward(3)
    spread_t.block(3, 1)
    spread_t.block(1, 7)
    spread_s.wait()
    cores_s.append(spread_s.core(1))
    finish_mix(started)
    for op in cores_s:
        op.wait_recv()
    hidden[...] += nt_dot(mix[...], out_s[...])
    normalise(0)
    c.end()
    spread_t.block(2, 7)
    cores_t = [spread_t.core(0)]
    project_kv(second, 1)
    mix = mixes.at[1]
    started = []
    for frame, mixed in enumerate(temporal(1, lambda: project_query(second))):
        mix[128 * frame : 128 * frame + 128, :LANES] = mixed
        started.append(start_mix(mix, frame))
    spread_t.wait()
    cores_t.append(spread_t.core(1))
    finish_mix(started)
    for op in cores_t:
        op.wait_recv()
    hidden[...] += nt_dot(mix[...], second[:, 768:])
    lat = lat_all[0:2].reshape(256, 16) - sizes[0:1, :16] * velocity(hidden[...])
    lat_send[...] = lat.reshape(2, 128, 16)
    shifted = copies.start(lat_send, lat_next, p.next)
    shifted.wait_recv()

    lat = jnp.where(position == 0, lat_all[2:4], lat_next[...])
    embed(lat.reshape(256, 16))
    normalise(1)
    project_kv(first, 2)
    project_query(first)
    mix = mixes.at[2]
    started = []
    for frame in range(2):
        attend_frame(2, frame, mix)
        started.append(start_mix(mix, frame))
    finish_mix(started)
    hidden[...] += nt_dot(mix[...], out_s[...])
    normalise(1)
    project_kv(second, 3)
    own = pl.multiple_of(p.s * 32, 32)
    mix = mixes.at[3]
    ops = []
    for frame, mixed in enumerate(temporal(3, lambda: project_query(second))):
        mix[128 * frame : 128 * frame + 128, :LANES] = mixed
        for slot, peer in ((1, p.zpeer), (2, p.cpeer), (3, p.zcpeer)):
            theirs = pl.multiple_of(128 * frame + peer[1] * 32, 32)
            ops.append(
                copies.start(
                    mix.at[pl.ds(theirs, 32), pl.ds(0, LANES)],
                    mix_last.at[pl.ds(32 * frame, 32), pl.ds(LANES * slot, LANES)],
                    peer,
                )
            )
        mix_last[32 * frame : 32 * frame + 32, :LANES] = mix[
            pl.ds(pl.multiple_of(128 * frame + own, 32), 32), :LANES
        ]
    for op in ops:
        op.wait_recv()
    h = jnp.concatenate([hidden[pl.ds(own, 32), :], hidden[pl.ds(own + 128, 32), :]], axis=0)
    h = h + nt_dot(mix_last[...], second[:, 768:])
    move = (sizes[1:2, :16] * velocity(h)).reshape(2, 32, 16)
    own_rows = pl.ds(own, 32)
    lat_own = jnp.where(position == 0, lat_all[2:4, own_rows, :], lat_next[:, own_rows, :])
    last_send[...] = lat_own - move
    shifted = copies.start(last_send, lat_last, p.next)
    shifted.wait_recv()
    out[...] = jnp.where(position == 0, noise_in[...], lat_last[...])
    copies.drain()


def run(*operands):
    vmem = pl.BlockSpec(memory_space=pltpu.VMEM)
    return pl.pallas_call(
        kernel,
        out_shape=jax.ShapeDtypeStruct((2, 32, 16), F32),
        in_specs=[vmem] * len(operands),
        out_specs=vmem,
        scratch_shapes=[
            pltpu.VMEM((WIDTH, 1152), BF),
            pltpu.VMEM((WIDTH, 4 * LANES), BF),
            pltpu.VMEM((WIDTH, 768 + 4 * LANES), BF),
            pltpu.VMEM((4, 128, 16), F32),
            pltpu.VMEM((2, 128, 16), F32),
            pltpu.VMEM((2, 128, 16), F32),
            pltpu.VMEM((2, 32, 16), F32),
            pltpu.VMEM((2, 32, 16), F32),
            pltpu.VMEM((256, WIDTH), F32),
            pltpu.VMEM((256, WIDTH), BF),
            pltpu.VMEM((256, LANES), F32),
            pltpu.VMEM((4, 256, 640), BF),
            pltpu.VMEM((4, 128, 640), BF),
            pltpu.VMEM((4, 128, 640), BF),
            pltpu.VMEM((4, 256, 4 * LANES), BF),
            pltpu.VMEM((64, 4 * LANES), BF),
            pltpu.VMEM((HEAD_COLUMNS, HEAD_COLUMNS), BF),
            pltpu.SemaphoreType.DMA((COPIES,)),
            pltpu.SemaphoreType.DMA((COPIES,)),
        ],
        compiler_params=pltpu.CompilerParams(
            collective_id=0, has_side_effects=True, vmem_limit_bytes=56 * 2**20
        ),
        name="denoise",
    )(*operands)


def permuted(array):
    lead = array.shape[:-1]
    split = array.reshape(*lead, 4, 4, 4, 18)
    split = jnp.swapaxes(split, -2, -3)
    main, rest = split[..., :16], split[..., 16:]
    return jnp.concatenate([main.reshape(*lead, MAIN), rest.reshape(*lead, REST)], axis=-1)


def pieces_of(spatial_qkv, spatial_out, temporal_qkv, temporal_out):
    s = jnp.concatenate([spatial_qkv.reshape(18, 864), spatial_out.T], axis=1)
    t = jnp.concatenate([temporal_qkv.reshape(18, 864), temporal_out.T], axis=1)
    rest = jnp.concatenate([s[16:], t[16:]]).reshape(16, HEAD_COLUMNS)
    g1 = jnp.concatenate([s[:16, :864], rest], axis=1)
    return g1, jnp.pad(s[:16, 864:], ((0, 0), (0, LANES - HEAD_COLUMNS))), t[:16]


def per_device(
    latents,
    fresh_noise,
    level_index,
    step_sizes,
    time_table,
    embed_in,
    spatial_qkv,
    spatial_out,
    temporal_qkv,
    temporal_out,
    embed_out,
):
    pieces = pieces_of(spatial_qkv, spatial_out, temporal_qkv, temporal_out)
    lat_in = jnp.concatenate([latents, fresh_noise[0]]).reshape(4, 32, 16)
    rows = [time_table[level_index[0, step]] for step in range(STEPS)]
    mods = jnp.concatenate([jnp.stack([r[0], 1.0 + r[1]]) for r in rows])
    sizes = jnp.stack([step_sizes[level_index[0, step]] for step in range(STEPS)])
    sizes = jnp.broadcast_to(sizes[:, None], (STEPS, 128))
    result = run(
        *pieces,
        lat_in,
        fresh_noise[1].reshape(2, 32, 16),
        permuted(mods),
        sizes,
        permuted(embed_in),
        permuted(embed_out.T).T,
    )
    return result.reshape(2, 512)


def solution(mesh):
    placed = (
        P("queue", "space"),
        P(None, None, "space"),
        P("queue", None),
        P(),
        P(),
        P(),
        P("queue", None, "space"),
        P("space", "queue"),
        P("queue", None, "space"),
        P("space", "queue"),
        P(),
    )
    return jax.shard_map(
        per_device, mesh=mesh, in_specs=placed, out_specs=P("queue", "space"), check_vma=False
    )
```

```python
import functools

import jax
import jax.numpy as jnp
from jax import lax
from jax.experimental import pallas as pl
from jax.experimental.pallas import tpu as pltpu
from jax.sharding import PartitionSpec as P

STEPS = 2
BF = jnp.bfloat16
F32 = jnp.float32


MESH = pl.DeviceIdType.MESH
MAIN, REST = 1024, 128
WIDTH = MAIN + REST
HEAD_COLUMNS = 288
HEAD_DIM = 72
INVERSE = 1.0 / HEAD_DIM**0.5
LANES = 384
COPIES = 160


class Place:
    def __init__(self):
        q, s = lax.axis_index("queue"), lax.axis_index("space")
        self.q, self.s = q, s
        self.x, self.zh, self.y = q // 16, (q // 4) % 4, q % 4
        self.zl, self.c = s // 2, s % 2
        self.v = (1 - self.c) * self.y + self.c * self.x
        self.w = (1 - self.c) * self.x + self.c * self.y
        self.zpeer = (q, (1 - self.zl) * 2 + self.c)
        self.cpeer = (q, self.zl * 2 + 1 - self.c)
        self.zcpeer = (q, (1 - self.zl) * 2 + 1 - self.c)
        self.next = ((q + 1) % 64, s)
        self.previous = ((q + 63) % 64, s)

    def cell(self, v, w):
        x = self.c * v + (1 - self.c) * w
        y = (1 - self.c) * v + self.c * w
        return x * 4 + y

    def ring(self, v, w):
        x = self.c * v + (1 - self.c) * w
        y = (1 - self.c) * v + self.c * w
        return ((x * 4 + self.zh) * 4 + y, self.s)

    def up(self, dz):
        return ((self.x * 4 + (self.zh + dz) % 4) * 4 + self.y, self.s)

    def beside(self, dz):
        z = (self.zh * 2 + self.zl + dz) % 8
        return ((self.x * 4 + z // 2) * 4 + self.y, (z % 2) * 2 + self.c)


class Copies:
    def __init__(self, send, recv):
        self.send, self.recv, self.started = send, recv, []

    def start(self, src, dst, target):
        i = len(self.started)
        assert i < COPIES
        op = pltpu.make_async_remote_copy(
            src_ref=src,
            dst_ref=dst,
            send_sem=self.send.at[i],
            recv_sem=self.recv.at[i],
            device_id=target,
            device_id_type=MESH,
        )
        op.start()
        self.started.append(op)
        return op

    def drain(self):
        for op in self.started:
            op.wait_send()


def greet(partners):
    barrier = pltpu.get_barrier_semaphore()
    for partner in partners:
        pl.semaphore_signal(barrier, inc=1, device_id=partner, device_id_type=MESH)
    pl.semaphore_wait(barrier, len(partners))


class Stream:
    def __init__(self, place, copies, buf, columns):
        self.p, self.copies, self.buf, self.columns = place, copies, buf, columns
        self.ops = {}

    def copy(self, key, rows, count, target):
        part = self.buf.at[pl.ds(pl.multiple_of(rows, 16), count), pl.ds(*self.columns)]
        self.ops[key] = self.copies.start(part, part, target)

    def place(self, piece):
        p = self.p
        self.row = pl.multiple_of((p.cell(p.v, p.w) * 4 + p.zh) * 16, 16)
        self.buf[pl.ds(self.row, 16), pl.ds(*self.columns)] = piece

    def z(self):
        for d in (1, 3, 2):
            self.copy(("z", d), self.row, 16, self.p.up(d))

    def both(self, key, v, w, right, left):
        rows = self.p.cell(v, w) * 64
        self.copy((key, "R"), rows, 64, right)
        self.copy((key, "L"), rows, 64, left)

    def w_sends(self, k):
        p = self.p
        v = (p.v + (0, 3, 1, 2)[k]) % 4
        self.both(("w", k), v, p.w, p.ring(p.v, (p.w + 1) % 4), p.ring(p.v, (p.w + 3) % 4))

    def v1(self):
        p = self.p
        for d in (1, 3, 2):
            self.ops["z", d].wait_recv()
        self.both("v", p.v, p.w, p.ring((p.v + 1) % 4, p.w), p.ring((p.v + 3) % 4, p.w))
        self.w_sends(0)

    def v2(self):
        p = self.p
        self.ops["v", "R"].wait_recv()
        self.copy("vfR", p.cell((p.v + 3) % 4, p.w) * 64, 32, p.ring((p.v + 1) % 4, p.w))
        self.w_sends(1)
        self.ops["v", "L"].wait_recv()
        self.copy("vfL", p.cell((p.v + 1) % 4, p.w) * 64 + 32, 32, p.ring((p.v + 3) % 4, p.w))
        self.w_sends(2)

    def w_forward(self, *blocks):
        p = self.p
        for k in blocks:
            v = (p.v + (0, 3, 1, 2)[k]) % 4
            self.ops[("w", k), "R"].wait_recv()
            self.copy(("wfR", k), p.cell(v, (p.w + 3) % 4) * 64, 32, p.ring(p.v, (p.w + 1) % 4))
            self.ops[("w", k), "L"].wait_recv()
            self.copy(("wfL", k), p.cell(v, (p.w + 1) % 4) * 64 + 32, 32, p.ring(p.v, (p.w + 3) % 4))

    def v3(self):
        self.ops["vfR"].wait_recv()
        self.ops["vfL"].wait_recv()
        self.w_sends(3)

    def end(self):
        for k in range(4):
            self.ops["wfR", k].wait_recv()
            self.ops["wfL", k].wait_recv()


class Spread:
    def __init__(self, place, copies, buf, first):
        self.p, self.copies, self.buf, self.first = place, copies, buf, first
        self.ops = []

    def part(self, slot, rows, count):
        return self.buf.at[pl.ds(pl.multiple_of(rows, 16), count), pl.ds(self.first + LANES * slot, LANES)]

    def block(self, dw, dz):
        p = self.p
        for v in range(4):
            rows = p.cell(v, (p.w + dw) % 4) * 64
            self.ops.append(
                self.copies.start(self.part(0, rows, 64), self.part(1, rows, 64), p.beside(dz))
            )

    def rest(self):
        self.ops.append(
            self.copies.start(self.part(0, MAIN, REST), self.part(1, MAIN, REST), self.p.zpeer)
        )

    def core(self, slot):
        return self.copies.start(
            self.part(slot, 0, WIDTH), self.part(slot + 2, 0, WIDTH), self.p.cpeer
        )

    def wait(self):
        for op in self.ops:
            op.wait_recv()


def nt_dot(a, b):
    return lax.dot_general(a, b, (((1,), (1,)), ((), ())), preferred_element_type=F32)


def dot(a, b):
    return jnp.dot(a, b, preferred_element_type=F32)


def halves(array):
    high = array.astype(BF)
    return high, (array - high.astype(F32)).astype(BF)


def thirds(array):
    high = array.astype(BF)
    rest = array - high.astype(F32)
    middle = rest.astype(BF)
    return high, middle, (rest - middle.astype(F32)).astype(BF)


def iotas(shape):
    return [lax.broadcasted_iota(jnp.int32, shape, axis) for axis in (0, 1)]


def head_masks(rows):
    lane = lax.broadcasted_iota(jnp.int32, (rows, HEAD_COLUMNS), 1)
    return [(lane >= HEAD_DIM * h) & (lane < HEAD_DIM * (h + 1)) for h in range(4)]


def kernel(
    latents,
    fresh_noise,
    level_index,
    step_sizes,
    time_table,
    embed_in,
    spatial_qkv,
    spatial_out,
    temporal_qkv,
    temporal_out,
    embed_out,
    out,
    in_latents,
    in_noise,
    in_table,
    in_embed,
    in_qkv,
    in_out,
    in_velocity,
    first,
    out_s,
    second,
    lat_pieces,
    lat_now,
    noise_now,
    lat_next,
    lat_send,
    lat_last,
    last_send,
    features,
    features_new,
    embed_six,
    out_three,
    hidden,
    normed,
    lower,
    query,
    kv,
    before,
    after,
    mixes,
    mix_last,
    same_head,
    local,
    send,
    recv,
):
    p = Place()
    copies = Copies(send, recv)
    fetches = [
        pltpu.make_async_copy(src, dst, local.at[i])
        for i, (src, dst) in enumerate(
            (
                (spatial_qkv, in_qkv.at[0]),
                (temporal_qkv, in_qkv.at[1]),
                (spatial_out, in_out.at[0]),
                (temporal_out, in_out.at[1]),
                (latents, in_latents),
                (fresh_noise, in_noise),
                (embed_in, in_embed),
                (embed_out, in_velocity),
                (time_table, in_table),
            )
        )
    ]
    for fetch in fetches:
        fetch.start()
    partners = [p.up(d) for d in (1, 2, 3)]
    partners += [p.ring((p.v + d) % 4, p.w) for d in (1, 3)]
    partners += [p.ring(p.v, (p.w + d) % 4) for d in (1, 3)]
    partners += [p.beside(1), p.beside(7), p.cpeer, p.zcpeer, p.next, p.previous]
    greet(partners)
    a = Stream(p, copies, first, (0, 1152))
    b = Stream(p, copies, out_s, (0, LANES))
    c = Stream(p, copies, second, (0, 1152))
    spread_s = Spread(p, copies, out_s, 0)
    spread_t = Spread(p, copies, second, 768)
    position = p.q

    for fetch in fetches[:4]:
        fetch.wait()
    to, source = iotas((16, 18))
    leading = jnp.where(to == source, 1.0, 0.0).astype(BF)
    rest = jnp.zeros((16, HEAD_COLUMNS), F32)
    blocks = []
    for t in range(2):
        for j in range(4):
            chosen = (source >= 16) & (to == 8 * t + 4 * (source - 16) + j)
            chosen = jnp.where(chosen, 1.0, 0.0).astype(BF)
            if j < 3:
                block = in_qkv[t, :, j, :]
                blocks.append(dot(leading, block))
                rest = rest + dot(chosen, block)
            else:
                block = in_out[t]
                blocks.append(nt_dot(leading, block))
                rest = rest + nt_dot(chosen, block)
    a.place(jnp.concatenate(blocks[:3] + [rest], axis=1).astype(BF))
    a.z()
    pad = jnp.zeros((16, LANES - HEAD_COLUMNS), F32)
    b.place(jnp.concatenate([blocks[3], pad], axis=1).astype(BF))
    c.place(jnp.concatenate(blocks[4:], axis=1).astype(BF))

    for fetch in fetches[4:]:
        fetch.wait()
    sub, lane = iotas((16, 512))
    diagonal = (lane & 15) == sub
    token, lane = iotas((32, 512))
    repeat = jnp.where((lane >> 4) == token, 1.0, 0.0).astype(BF)

    def unflatten(line):
        wide = jnp.where(diagonal, jnp.broadcast_to(line, (16, 512)), 0.0)
        high, middle, low = thirds(wide)
        return nt_dot(high, repeat) + nt_dot(middle, repeat) + nt_dot(low, repeat)

    lines = [in_latents[f : f + 1, :] for f in range(2)] + [in_noise[0, f : f + 1, :] for f in range(2)]
    lat_pieces[p.s] = jnp.concatenate([unflatten(line) for line in lines], axis=1)
    own_lat = lat_pieces.at[p.s]
    lat_ops = [copies.start(own_lat, own_lat, t) for t in (p.cpeer, p.zpeer, p.zcpeer)]
    last_noise = jnp.concatenate(
        [unflatten(in_noise[1, f : f + 1, :]) for f in range(2)] + [jnp.zeros((16, 64), F32)], axis=1
    )

    levels = [level_index[0, step] for step in range(STEPS)]
    small = jnp.concatenate(
        [in_embed[...], in_velocity[...].T, in_table[levels[0]], in_table[levels[1]], jnp.zeros((4, WIDTH), F32)],
        axis=0,
    )
    for i, part in enumerate(thirds(small)):
        features[48 * i : 48 * i + 40, :] = part
        features[48 * i + 40 : 48 * i + 48, :] = jnp.zeros((8, WIDTH), BF)
    new = lax.broadcasted_iota(jnp.int32, (1, WIDTH), 1)
    late = new - MAIN
    piece = jnp.where(new < MAIN, new >> 4, late >> 1)
    within = jnp.where(new < MAIN, new & 15, 16 + (late & 1))
    owner = (piece & 48) + ((piece & 3) << 2) + ((piece >> 2) & 3)
    old = owner * 18 + within
    features_new[...] = jnp.zeros((144, WIDTH), F32)

    def reorder(i, carry):
        row = lax.broadcasted_iota(jnp.int32, (128, WIDTH), 0) + i * 128
        move = jnp.where(row == old, 1.0, 0.0).astype(BF)
        features_new[...] += dot(features[:, pl.ds(pl.multiple_of(i * 128, 128), 128)], move)
        return carry

    lax.fori_loop(0, 9, reorder, 0)
    parts = [features_new[48 * i : 48 * i + 16, :] for i in range(3)]
    embed_six[...] = jnp.concatenate([parts[i] for i in (0, 1, 0, 1, 2, 0)], axis=0).astype(BF)
    out_three[...] = jnp.concatenate(
        [features_new[48 * i + 16 : 48 * i + 32, :] for i in range(3)], axis=0
    ).astype(BF)
    mods = features_new[32:36, :] + features_new[80:84, :] + features_new[128:132, :]

    row, column = iotas((HEAD_COLUMNS, HEAD_COLUMNS))
    same = jnp.zeros((HEAD_COLUMNS, HEAD_COLUMNS), F32)
    for h in range(4):
        low, high = HEAD_DIM * h, HEAD_DIM * (h + 1)
        inside = (row >= low) & (row < high) & (column >= low) & (column < high)
        same = jnp.where(inside, 1.0, same)
    same_head[...] = same.astype(BF)

    def embed(lat):
        high, middle, low = (part.astype(F32) for part in thirds(lat))
        stack = jnp.concatenate([high, high, middle, middle, high, low], axis=0)
        hidden[...] = dot(stack.T.astype(BF), embed_six[...])

    def normalise(step):
        shift, scale = mods[2 * step : 2 * step + 1, :], 1.0 + mods[2 * step + 1 : 2 * step + 2, :]

        def rows_of(i, carry):
            rows = pl.ds(pl.multiple_of(i * 32, 32), 32)
            h = hidden[rows, :]
            inverse = lax.rsqrt(jnp.mean(h * h, axis=-1, keepdims=True) + 1e-06)
            normed[rows, :] = (h * inverse * scale + shift).astype(BF)
            return carry

        lax.fori_loop(0, 8, rows_of, 0)

    def project_kv(weights, half):
        kv[half] = dot(normed[...], weights[:, 256:896]).astype(BF)

    def project_query(weights):
        query[...] = dot(normed[...], weights[:, :384])

    def attend_frame(half, frame, mix):
        rows = slice(128 * frame, 128 * frame + 128)
        masks = head_masks(128)
        q = query[rows, :HEAD_COLUMNS].astype(BF).astype(F32)
        both = kv[half, rows, :].astype(F32)
        k = both[:, 32 : 32 + HEAD_COLUMNS].astype(BF)
        v = both[:, 320 : 320 + HEAD_COLUMNS]
        q_heads = jnp.concatenate([jnp.where(m, q, 0.0).astype(BF) for m in masks], axis=0)
        v_heads = jnp.concatenate([jnp.where(m, v, 0.0).astype(BF) for m in masks], axis=0)
        scores = nt_dot(q_heads, k) * INVERSE
        scores = jnp.exp(scores - jnp.max(scores, axis=-1, keepdims=True))
        probs = (scores / jnp.sum(scores, axis=-1, keepdims=True)).astype(BF)
        probs = jnp.concatenate([probs[128 * h : 128 * h + 128] for h in range(4)], axis=1)
        mixed = dot(probs, v_heads)
        mixed = jnp.concatenate([mixed, jnp.zeros((128, LANES - HEAD_COLUMNS), F32)], axis=1)
        mix[rows, :LANES] = mixed.astype(BF)

    def start_mix(mix, frame):
        part = lambda slot: mix.at[pl.ds(128 * frame, 128), pl.ds(LANES * slot, LANES)]
        by_z = copies.start(part(0), part(1), p.zpeer)
        by_core = copies.start(part(0), part(2), p.cpeer)
        return by_z, by_core, part

    def finish_mix(started):
        last = []
        for by_z, _, part in started:
            by_z.wait_recv()
            last.append(copies.start(part(1), part(3), p.cpeer))
        for _, by_core, _ in started:
            by_core.wait_recv()
        for op in last:
            op.wait_recv()

    def temporal(half, prepare):
        halo = [
            copies.start(kv.at[half, pl.ds(128, 128)], before.at[half], p.next),
            copies.start(kv.at[half, pl.ds(0, 128)], after.at[half], p.previous),
        ]
        prepare()

        def keys_values(ref_value):
            both = ref_value.astype(F32)
            return both[:, 32 : 32 + HEAD_COLUMNS], both[:, 320 : 320 + HEAD_COLUMNS]

        def score(q, k):
            high, low = halves(q * k)
            same_now = same_head[...]
            return (dot(high, same_now) + dot(low, same_now)) * INVERSE

        q0 = query[:128, :HEAD_COLUMNS].astype(BF).astype(F32)
        q1 = query[128:, :HEAD_COLUMNS].astype(BF).astype(F32)
        k0, v0 = keys_values(kv[half, :128])
        k1, v1 = keys_values(kv[half, 128:])
        s00, s01, s10, s11 = score(q0, k0), score(q0, k1), score(q1, k0), score(q1, k1)

        def blend(sa, sb, sc, va, vb, vc):
            top = jnp.maximum(jnp.maximum(sa, sb), sc)
            ea, eb, ec = jnp.exp(sa - top), jnp.exp(sb - top), jnp.exp(sc - top)
            total = ea + eb + ec
            rounded = lambda e: (e / total).astype(BF).astype(F32)
            mixed = rounded(ea) * va + rounded(eb) * vb + rounded(ec) * vc
            return jnp.concatenate([jnp.zeros((128, LANES - HEAD_COLUMNS), F32), mixed], axis=1).astype(BF)

        halo[0].wait_recv()
        kb, vb = keys_values(before[half])
        sb = jnp.where(position == 0, -1e30, score(q0, kb))
        yield blend(sb, s00, s01, vb, v0, v1)
        halo[1].wait_recv()
        ka, va = keys_values(after[half])
        sa = jnp.where(position == 63, -1e30, score(q1, ka))
        yield blend(s10, s11, sa, v0, v1, va)

    def velocity(ref, rows):
        def rows_of(i, carry):
            part = pl.ds(pl.multiple_of(i * 32, 32), 32)
            h = ref[part, :]
            h = h * lax.rsqrt(jnp.mean(h * h, axis=-1, keepdims=True) + 1e-06)
            normed[part, :], lower[part, :] = halves(h)
            return carry

        lax.fori_loop(0, rows // 32, rows_of, 0)
        both = nt_dot(out_three[...], normed[:rows, :]) + nt_dot(out_three[...], lower[:rows, :])
        return both[:16] + both[16:32] + both[32:48]

    def selected(j, t):
        target = lax.broadcasted_iota(jnp.int32, (REST, MAIN), 0)
        source = lax.broadcasted_iota(jnp.int32, (REST, MAIN), 1)
        choose = jnp.where(source == 8 * target - 4 * (target % 2) + 8 * t + j, 1.0, 0.0).astype(BF)
        return dot(choose, first[:MAIN, 768:1152])[:, 96:]

    a.v1()
    b.z()
    for op in lat_ops:
        op.wait_recv()
    by_frame = [
        jnp.concatenate([lat_pieces[s, :, 32 * f : 32 * f + 32] for s in range(4)], axis=1)
        for f in range(4)
    ]
    lat_now[...] = jnp.concatenate(by_frame[:2], axis=1)
    noise_now[...] = jnp.concatenate(by_frame[2:], axis=1)
    embed(lat_now[...])
    a.v2()
    a.w_forward(0)
    c.z()
    normalise(0)
    a.v3()
    b.v1()
    a.w_forward(1, 2)
    b.v2()
    a.w_forward(3)
    b.w_forward(0)
    b.v3()
    spread_s.block(0, 1)
    c.v1()
    a.end()

    blocks = [selected(j, 0) for j in range(4)]
    pad = jnp.zeros((REST, 96), F32)
    first[MAIN:, :896] = jnp.concatenate(blocks[:3] + [pad[:, :32]], axis=1).astype(BF)
    out_s[MAIN:, :LANES] = jnp.concatenate([blocks[3], pad], axis=1).astype(BF)
    spread_s.rest()
    b.w_forward(1, 2)
    c.v2()
    b.w_forward(3)
    spread_s.block(3, 1)
    spread_s.block(1, 7)
    project_kv(first, 0)
    project_query(first)
    c.w_forward(0)
    c.v3()
    spread_t.block(0, 1)
    b.end()
    spread_s.block(2, 7)
    cores_s = [spread_s.core(0)]
    mix = mixes.at[0]
    attend_frame(0, 0, mix)
    started = [start_mix(mix, 0)]
    c.w_forward(1, 2)
    attend_frame(0, 1, mix)
    started.append(start_mix(mix, 1))
    blocks = [selected(j, 1) for j in range(4)]
    second[MAIN:, :1152] = jnp.concatenate(blocks, axis=1).astype(BF)
    spread_t.rest()
    c.w_forward(3)
    spread_t.block(3, 1)
    spread_t.block(1, 7)
    spread_s.wait()
    cores_s.append(spread_s.core(1))
    finish_mix(started)
    for op in cores_s:
        op.wait_recv()
    hidden[...] += nt_dot(mix[...], out_s[...])
    normalise(0)
    c.end()
    spread_t.block(2, 7)
    cores_t = [spread_t.core(0)]
    project_kv(second, 1)
    mix = mixes.at[1]
    started = []
    for frame, mixed in enumerate(temporal(1, lambda: project_query(second))):
        mix[128 * frame : 128 * frame + 128, :LANES] = mixed
        started.append(start_mix(mix, frame))
    spread_t.wait()
    cores_t.append(spread_t.core(1))
    finish_mix(started)
    for op in cores_t:
        op.wait_recv()
    hidden[...] += nt_dot(mix[...], second[:, 768:])
    lat_send[...] = lat_now[...] - step_sizes[levels[0]] * velocity(hidden, 256)
    shifted = copies.start(lat_send, lat_next, p.next)
    shifted.wait_recv()

    lat_now[...] = jnp.where(position == 0, noise_now[...], lat_next[...])
    embed(lat_now[...])
    normalise(1)
    project_kv(first, 2)
    project_query(first)
    mix = mixes.at[2]
    started = []
    for frame in range(2):
        attend_frame(2, frame, mix)
        started.append(start_mix(mix, frame))
    finish_mix(started)
    hidden[...] += nt_dot(mix[...], out_s[...])
    normalise(1)
    project_kv(second, 3)
    own = pl.multiple_of(p.s * 32, 32)
    mix = mixes.at[3]
    ops = []
    for frame, mixed in enumerate(temporal(3, lambda: project_query(second))):
        mix[128 * frame : 128 * frame + 128, :LANES] = mixed
        for slot, peer in ((1, p.zpeer), (2, p.cpeer), (3, p.zcpeer)):
            theirs = pl.multiple_of(128 * frame + peer[1] * 32, 32)
            ops.append(
                copies.start(
                    mix.at[pl.ds(theirs, 32), pl.ds(0, LANES)],
                    mix_last.at[pl.ds(32 * frame, 32), pl.ds(LANES * slot, LANES)],
                    peer,
                )
            )
        mix_last[32 * frame : 32 * frame + 32, :LANES] = mix[
            pl.ds(pl.multiple_of(128 * frame + own, 32), 32), :LANES
        ]
    for op in ops:
        op.wait_recv()
    h = jnp.concatenate([hidden[pl.ds(own, 32), :], hidden[pl.ds(own + 128, 32), :]], axis=0)
    hidden[:64, :] = h + nt_dot(mix_last[...], second[:, 768:])
    move = step_sizes[levels[1]] * velocity(hidden, 64)
    lat = lat_now[...]
    lat_own = jnp.zeros((16, 64), F32)
    for k in range(4):
        theirs = [lat[:, 128 * f + 32 * k : 128 * f + 32 * k + 32] for f in range(2)]
        lat_own = jnp.where(p.s == k, jnp.concatenate(theirs, axis=1), lat_own)
    last_send[...] = jnp.concatenate([lat_own - move, jnp.zeros((16, 64), F32)], axis=1)
    shifted = copies.start(last_send, lat_last, p.next)
    shifted.wait_recv()
    final = jnp.where(position == 0, last_noise, lat_last[...])
    for f in range(2):
        high, middle, low = thirds(final[:, 32 * f : 32 * f + 32])
        wide = dot(high, repeat) + dot(middle, repeat) + dot(low, repeat)
        out[f : f + 1, :] = jnp.sum(jnp.where(diagonal, wide, 0.0), axis=0, keepdims=True)
    copies.drain()


def per_device(*operands):
    smem, whole = pl.BlockSpec(memory_space=pltpu.SMEM), pl.BlockSpec(memory_space=pl.ANY)
    specs = [smem if i in (2, 3) else whole for i in range(len(operands))]
    return pl.pallas_call(
        kernel,
        out_shape=jax.ShapeDtypeStruct((2, 512), F32),
        in_specs=specs,
        out_specs=pl.BlockSpec(memory_space=pltpu.VMEM),
        scratch_shapes=[
            pltpu.VMEM((2, 512), F32),
            pltpu.VMEM((2, 2, 512), F32),
            pltpu.VMEM((30, 2, WIDTH), F32),
            pltpu.VMEM((16, WIDTH), F32),
            pltpu.VMEM((2, 18, 3, HEAD_COLUMNS), BF),
            pltpu.VMEM((2, HEAD_COLUMNS, 18), BF),
            pltpu.VMEM((WIDTH, 16), F32),
            pltpu.VMEM((WIDTH, 1152), BF),
            pltpu.VMEM((WIDTH, 4 * LANES), BF),
            pltpu.VMEM((WIDTH, 768 + 4 * LANES), BF),
            pltpu.VMEM((4, 16, 128), F32),
            pltpu.VMEM((16, 256), F32),
            pltpu.VMEM((16, 256), F32),
            pltpu.VMEM((16, 256), F32),
            pltpu.VMEM((16, 256), F32),
            pltpu.VMEM((16, 128), F32),
            pltpu.VMEM((16, 128), F32),
            pltpu.VMEM((144, WIDTH), BF),
            pltpu.VMEM((144, WIDTH), F32),
            pltpu.VMEM((96, WIDTH), BF),
            pltpu.VMEM((48, WIDTH), BF),
            pltpu.VMEM((256, WIDTH), F32),
            pltpu.VMEM((256, WIDTH), BF),
            pltpu.VMEM((256, WIDTH), BF),
            pltpu.VMEM((256, LANES), F32),
            pltpu.VMEM((4, 256, 640), BF),
            pltpu.VMEM((4, 128, 640), BF),
            pltpu.VMEM((4, 128, 640), BF),
            pltpu.VMEM((4, 256, 4 * LANES), BF),
            pltpu.VMEM((64, 4 * LANES), BF),
            pltpu.VMEM((HEAD_COLUMNS, HEAD_COLUMNS), BF),
            pltpu.SemaphoreType.DMA((9,)),
            pltpu.SemaphoreType.DMA((COPIES,)),
            pltpu.SemaphoreType.DMA((COPIES,)),
        ],
        compiler_params=pltpu.CompilerParams(
            collective_id=0, has_side_effects=True, vmem_limit_bytes=56 * 2**20
        ),
        name="denoise",
    )(*operands)


def solution(mesh):
    placed = (
        P("queue", "space"),
        P(None, None, "space"),
        P("queue", None),
        P(),
        P(),
        P(),
        P("queue", None, "space"),
        P("space", "queue"),
        P("queue", None, "space"),
        P("space", "queue"),
        P(),
    )
    return jax.shard_map(
        per_device, mesh=mesh, in_specs=placed, out_specs=P("queue", "space"), check_vma=False
    )
```

```python
import functools

import jax
import jax.numpy as jnp
from jax import lax
from jax.experimental import pallas as pl
from jax.experimental.pallas import tpu as pltpu
from jax.sharding import PartitionSpec as P

STEPS = 2
BF = jnp.bfloat16
F32 = jnp.float32


MESH = pl.DeviceIdType.MESH
MAIN, REST = 1024, 128
WIDTH = MAIN + REST
HEAD_COLUMNS = 288
HEAD_DIM = 72
INVERSE = 1.0 / HEAD_DIM**0.5
LANES = 384
COPIES = 160


class Place:
    def __init__(self):
        q, s = lax.axis_index("queue"), lax.axis_index("space")
        self.q, self.s = q, s
        self.x, self.zh, self.y = q // 16, (q // 4) % 4, q % 4
        self.zl, self.c = s // 2, s % 2
        self.v = (1 - self.c) * self.y + self.c * self.x
        self.w = (1 - self.c) * self.x + self.c * self.y
        self.zpeer = (q, (1 - self.zl) * 2 + self.c)
        self.cpeer = (q, self.zl * 2 + 1 - self.c)
        self.zcpeer = (q, (1 - self.zl) * 2 + 1 - self.c)
        self.next = ((q + 1) % 64, s)
        self.previous = ((q + 63) % 64, s)
        self.second = ((q + 2) % 64, s)
        self.second_previous = ((q + 62) % 64, s)

    def cell(self, v, w):
        x = self.c * v + (1 - self.c) * w
        y = (1 - self.c) * v + self.c * w
        return x * 4 + y

    def ring(self, v, w):
        x = self.c * v + (1 - self.c) * w
        y = (1 - self.c) * v + self.c * w
        return ((x * 4 + self.zh) * 4 + y, self.s)

    def up(self, dz):
        return ((self.x * 4 + (self.zh + dz) % 4) * 4 + self.y, self.s)

    def beside(self, dz):
        z = (self.zh * 2 + self.zl + dz) % 8
        return ((self.x * 4 + z // 2) * 4 + self.y, (z % 2) * 2 + self.c)


class Copies:
    def __init__(self, send, recv):
        self.send, self.recv, self.started = send, recv, []

    def start(self, src, dst, target):
        i = len(self.started)
        assert i < COPIES
        op = pltpu.make_async_remote_copy(
            src_ref=src,
            dst_ref=dst,
            send_sem=self.send.at[i],
            recv_sem=self.recv.at[i],
            device_id=target,
            device_id_type=MESH,
        )
        op.start()
        self.started.append(op)
        return op

    def drain(self):
        for op in self.started:
            op.wait_send()


def greet(partners):
    barrier = pltpu.get_barrier_semaphore()
    for partner in partners:
        pl.semaphore_signal(barrier, inc=1, device_id=partner, device_id_type=MESH)
    pl.semaphore_wait(barrier, len(partners))


class Stream:
    def __init__(self, place, copies, buf, columns):
        self.p, self.copies, self.buf, self.columns = place, copies, buf, columns
        self.ops = {}

    def copy(self, key, rows, count, target):
        part = self.buf.at[pl.ds(pl.multiple_of(rows, 16), count), pl.ds(*self.columns)]
        self.ops[key] = self.copies.start(part, part, target)

    def place(self, piece):
        p = self.p
        self.row = pl.multiple_of((p.cell(p.v, p.w) * 4 + p.zh) * 16, 16)
        self.buf[pl.ds(self.row, 16), pl.ds(*self.columns)] = piece

    def z(self):
        for d in (1, 3, 2):
            self.copy(("z", d), self.row, 16, self.p.up(d))

    def both(self, key, v, w, right, left):
        rows = self.p.cell(v, w) * 64
        self.copy((key, "R"), rows, 64, right)
        self.copy((key, "L"), rows, 64, left)

    def w_sends(self, k):
        p = self.p
        v = (p.v + (0, 3, 1, 2)[k]) % 4
        self.both(("w", k), v, p.w, p.ring(p.v, (p.w + 1) % 4), p.ring(p.v, (p.w + 3) % 4))

    def v1(self):
        p = self.p
        for d in (1, 3, 2):
            self.ops["z", d].wait_recv()
        self.both("v", p.v, p.w, p.ring((p.v + 1) % 4, p.w), p.ring((p.v + 3) % 4, p.w))
        self.w_sends(0)

    def v2(self):
        p = self.p
        self.ops["v", "R"].wait_recv()
        self.copy("vfR", p.cell((p.v + 3) % 4, p.w) * 64, 32, p.ring((p.v + 1) % 4, p.w))
        self.w_sends(1)
        self.ops["v", "L"].wait_recv()
        self.copy("vfL", p.cell((p.v + 1) % 4, p.w) * 64 + 32, 32, p.ring((p.v + 3) % 4, p.w))
        self.w_sends(2)

    def w_forward(self, *blocks):
        p = self.p
        for k in blocks:
            v = (p.v + (0, 3, 1, 2)[k]) % 4
            self.ops[("w", k), "R"].wait_recv()
            self.copy(("wfR", k), p.cell(v, (p.w + 3) % 4) * 64, 32, p.ring(p.v, (p.w + 1) % 4))
            self.ops[("w", k), "L"].wait_recv()
            self.copy(("wfL", k), p.cell(v, (p.w + 1) % 4) * 64 + 32, 32, p.ring(p.v, (p.w + 3) % 4))

    def v3(self):
        self.ops["vfR"].wait_recv()
        self.ops["vfL"].wait_recv()
        self.w_sends(3)

    def end(self):
        for k in range(4):
            self.ops["wfR", k].wait_recv()
            self.ops["wfL", k].wait_recv()


class Spread:
    def __init__(self, place, copies, buf, first):
        self.p, self.copies, self.buf, self.first = place, copies, buf, first
        self.ops = []

    def part(self, slot, rows, count):
        return self.buf.at[pl.ds(pl.multiple_of(rows, 16), count), pl.ds(self.first + LANES * slot, LANES)]

    def block(self, dw):
        p = self.p
        for v in range(4):
            rows = p.cell(v, (p.w + dw) % 4) * 64
            to = p.beside(1 if v < 2 else 7)
            self.ops.append(self.copies.start(self.part(0, rows, 64), self.part(1, rows, 64), to))

    def rest(self):
        self.ops.append(
            self.copies.start(self.part(0, MAIN, REST), self.part(1, MAIN, REST), self.p.zpeer)
        )

    def core(self, slot):
        return self.copies.start(
            self.part(slot, 0, WIDTH), self.part(slot + 2, 0, WIDTH), self.p.cpeer
        )

    def wait(self):
        for op in self.ops:
            op.wait_recv()


def nt_dot(a, b):
    return lax.dot_general(a, b, (((1,), (1,)), ((), ())), preferred_element_type=F32)


def dot(a, b):
    return jnp.dot(a, b, preferred_element_type=F32)


def halves(array):
    high = array.astype(BF)
    return high, (array - high.astype(F32)).astype(BF)


def thirds(array):
    high = array.astype(BF)
    rest = array - high.astype(F32)
    middle = rest.astype(BF)
    return high, middle, (rest - middle.astype(F32)).astype(BF)


def iotas(shape):
    return [lax.broadcasted_iota(jnp.int32, shape, axis) for axis in (0, 1)]


def head_masks(rows):
    lane = lax.broadcasted_iota(jnp.int32, (rows, HEAD_COLUMNS), 1)
    return [(lane >= HEAD_DIM * h) & (lane < HEAD_DIM * (h + 1)) for h in range(4)]


def kernel(
    latents,
    fresh_noise,
    level_index,
    step_sizes,
    time_table,
    embed_in,
    spatial_qkv,
    spatial_out,
    temporal_qkv,
    temporal_out,
    embed_out,
    out,
    in_latents,
    in_noise,
    in_table,
    in_embed,
    in_qkv,
    in_out,
    in_velocity,
    first,
    out_s,
    second,
    lat_pieces,
    lat_second,
    lat_last,
    last_send,
    mods_own,
    mods_next,
    features,
    features_new,
    embed_six,
    out_three,
    hidden,
    normed,
    lower,
    query,
    kv,
    before,
    after,
    mixes,
    mix_last,
    same_head,
    local,
    send,
    recv,
):
    p = Place()
    copies = Copies(send, recv)
    fetches = [
        pltpu.make_async_copy(src, dst, local.at[i])
        for i, (src, dst) in enumerate(
            (
                (spatial_qkv, in_qkv.at[0]),
                (temporal_qkv, in_qkv.at[1]),
                (spatial_out, in_out.at[0]),
                (temporal_out, in_out.at[1]),
                (latents, in_latents),
                (fresh_noise, in_noise),
                (embed_in, in_embed),
                (embed_out, in_velocity),
                (time_table, in_table),
            )
        )
    ]
    for fetch in fetches:
        fetch.start()
    partners = [p.up(d) for d in (1, 2, 3)]
    partners += [p.ring((p.v + d) % 4, p.w) for d in (1, 3)]
    partners += [p.ring(p.v, (p.w + d) % 4) for d in (1, 3)]
    partners += [p.beside(1), p.beside(7), p.cpeer, p.zcpeer]
    partners += [p.next, p.previous, p.second, p.second_previous]
    greet(partners)
    a = Stream(p, copies, first, (0, 1152))
    b = Stream(p, copies, out_s, (0, LANES))
    c = Stream(p, copies, second, (0, 1152))
    spread_s = Spread(p, copies, out_s, 0)
    spread_t = Spread(p, copies, second, 768)
    position = p.q

    for fetch in fetches[:4]:
        fetch.wait()
    to, source = iotas((16, 18))
    leading = jnp.where(to == source, 1.0, 0.0).astype(BF)
    rest = jnp.zeros((16, HEAD_COLUMNS), F32)
    blocks = []
    for t in range(2):
        for j in range(4):
            chosen = (source >= 16) & (to == 8 * t + 4 * (source - 16) + j)
            chosen = jnp.where(chosen, 1.0, 0.0).astype(BF)
            block = in_qkv[t, :, j, :] if j < 3 else in_out[t]
            blocks.append(dot(leading, block))
            rest = rest + dot(chosen, block)
    a.place(jnp.concatenate(blocks[:3] + [rest], axis=1).astype(BF))
    a.z()
    pad = jnp.zeros((16, LANES - HEAD_COLUMNS), F32)
    b.place(jnp.concatenate([blocks[3], pad], axis=1).astype(BF))
    c.place(jnp.concatenate(blocks[4:], axis=1).astype(BF))

    for fetch in fetches[4:]:
        fetch.wait()
    sub, lane = iotas((16, 512))
    diagonal = (lane & 15) == sub
    token, lane = iotas((32, 512))
    repeat = jnp.where((lane >> 4) == token, 1.0, 0.0).astype(BF)

    def unflatten(line):
        wide = jnp.where(diagonal, jnp.broadcast_to(line, (16, 512)), 0.0)
        high, middle, low = thirds(wide)
        return nt_dot(high, repeat) + nt_dot(middle, repeat) + nt_dot(low, repeat)

    lines = [in_latents[f : f + 1, :] for f in range(2)] + [in_noise[0, f : f + 1, :] for f in range(2)]
    lat_pieces[p.s] = jnp.concatenate([unflatten(line) for line in lines], axis=1)

    def share(pieces):
        own = pieces.at[p.s]
        return [copies.start(own, own, t) for t in (p.cpeer, p.zpeer, p.zcpeer)]

    def whole(pieces):
        parts = [pieces[s, :, 32 * f : 32 * f + 32] for f in range(2) for s in range(4)]
        return jnp.concatenate(parts, axis=1)

    lat_ops = share(lat_pieces)
    last_noise = jnp.concatenate(
        [unflatten(in_noise[1, f : f + 1, :]) for f in range(2)] + [jnp.zeros((16, 64), F32)], axis=1
    )

    levels = [level_index[0, step] for step in range(STEPS)]
    small = jnp.concatenate(
        [in_embed[...], in_velocity[...], in_table[levels[0]], in_table[levels[1]], jnp.zeros((4, WIDTH), F32)],
        axis=0,
    )
    for i, part in enumerate(thirds(small)):
        features[48 * i : 48 * i + 40, :] = part
        features[48 * i + 40 : 48 * i + 48, :] = jnp.zeros((8, WIDTH), BF)
    new = lax.broadcasted_iota(jnp.int32, (1, WIDTH), 1)
    late = new - MAIN
    piece = jnp.where(new < MAIN, new >> 4, late >> 1)
    within = jnp.where(new < MAIN, new & 15, 16 + (late & 1))
    owner = (piece & 48) + ((piece & 3) << 2) + ((piece >> 2) & 3)
    old = owner * 18 + within
    features_new[...] = jnp.zeros((144, WIDTH), F32)

    def reorder(i, carry):
        row = lax.broadcasted_iota(jnp.int32, (128, WIDTH), 0) + i * 128
        move = jnp.where(row == old, 1.0, 0.0).astype(BF)
        features_new[...] += dot(features[:, pl.ds(pl.multiple_of(i * 128, 128), 128)], move)
        return carry

    lax.fori_loop(0, 9, reorder, 0)
    parts = [features_new[48 * i : 48 * i + 16, :] for i in range(3)]
    embed_six[...] = jnp.concatenate([parts[i] for i in (0, 1, 0, 1, 2, 0)], axis=0).astype(BF)
    out_three[...] = jnp.concatenate(
        [features_new[48 * i + 16 : 48 * i + 32, :] for i in range(3)], axis=0
    ).astype(BF)
    mods = features_new[32:36, :] + features_new[80:84, :] + features_new[128:132, :]
    size_line = jnp.full((1, WIDTH), step_sizes[levels[1]], F32)
    mods_own[...] = jnp.concatenate([mods[2:], size_line, jnp.zeros((5, WIDTH), F32)], axis=0)
    mods_op = copies.start(mods_own, mods_next, p.previous)

    row, column = iotas((HEAD_COLUMNS, HEAD_COLUMNS))
    same = jnp.zeros((HEAD_COLUMNS, HEAD_COLUMNS), F32)
    for h in range(4):
        low, high = HEAD_DIM * h, HEAD_DIM * (h + 1)
        inside = (row >= low) & (row < high) & (column >= low) & (column < high)
        same = jnp.where(inside, 1.0, same)
    same_head[...] = same.astype(BF)

    def embed(lat):
        high, middle, low = (part.astype(F32) for part in thirds(lat))
        stack = jnp.concatenate([high, high, middle, middle, high, low], axis=0)
        hidden[...] = dot(stack.T.astype(BF), embed_six[...])

    def normalise(shift, scale):
        scale = 1.0 + scale

        def rows_of(i, carry):
            rows = pl.ds(pl.multiple_of(i * 32, 32), 32)
            h = hidden[rows, :]
            inverse = lax.rsqrt(jnp.mean(h * h, axis=-1, keepdims=True) + 1e-06)
            normed[rows, :] = (h * inverse * scale + shift).astype(BF)
            return carry

        lax.fori_loop(0, 8, rows_of, 0)

    def project_kv(weights, half):
        kv[half] = dot(normed[...], weights[:, 256:896]).astype(BF)

    def project_query(weights):
        query[...] = dot(normed[...], weights[:, :384])

    def attend_frame(half, frame, mix):
        rows = slice(128 * frame, 128 * frame + 128)
        masks = head_masks(128)
        q = query[rows, :HEAD_COLUMNS].astype(BF).astype(F32)
        both = kv[half, rows, :].astype(F32)
        k = both[:, 32 : 32 + HEAD_COLUMNS].astype(BF)
        v = both[:, 320 : 320 + HEAD_COLUMNS]
        q_heads = jnp.concatenate([jnp.where(m, q, 0.0).astype(BF) for m in masks], axis=0)
        v_heads = jnp.concatenate([jnp.where(m, v, 0.0).astype(BF) for m in masks], axis=0)
        scores = nt_dot(q_heads, k) * INVERSE
        scores = jnp.exp(scores - jnp.max(scores, axis=-1, keepdims=True))
        probs = (scores / jnp.sum(scores, axis=-1, keepdims=True)).astype(BF)
        probs = jnp.concatenate([probs[128 * h : 128 * h + 128] for h in range(4)], axis=1)
        mixed = dot(probs, v_heads)
        mixed = jnp.concatenate([mixed, jnp.zeros((128, LANES - HEAD_COLUMNS), F32)], axis=1)
        mix[rows, :LANES] = mixed.astype(BF)

    def start_mix(mix, frame):
        part = lambda slot: mix.at[pl.ds(128 * frame, 128), pl.ds(LANES * slot, LANES)]
        by_z = copies.start(part(0), part(1), p.zpeer)
        by_core = copies.start(part(0), part(2), p.cpeer)
        return by_z, by_core, part

    def finish_mix(started):
        last = []
        for by_z, _, part in started:
            by_z.wait_recv()
            last.append(copies.start(part(1), part(3), p.cpeer))
        for _, by_core, _ in started:
            by_core.wait_recv()
        for op in last:
            op.wait_recv()

    def temporal(half, first_place, last_place, prepare):
        halo = [
            copies.start(kv.at[half, pl.ds(128, 128)], before.at[half], p.next),
            copies.start(kv.at[half, pl.ds(0, 128)], after.at[half], p.previous),
        ]
        prepare()

        def keys_values(ref_value):
            both = ref_value.astype(F32)
            return both[:, 32 : 32 + HEAD_COLUMNS], both[:, 320 : 320 + HEAD_COLUMNS]

        def score(q, k):
            high, low = halves(q * k)
            same_now = same_head[...]
            return (dot(high, same_now) + dot(low, same_now)) * INVERSE

        q0 = query[:128, :HEAD_COLUMNS].astype(BF).astype(F32)
        q1 = query[128:, :HEAD_COLUMNS].astype(BF).astype(F32)
        k0, v0 = keys_values(kv[half, :128])
        k1, v1 = keys_values(kv[half, 128:])
        s00, s01, s10, s11 = score(q0, k0), score(q0, k1), score(q1, k0), score(q1, k1)

        def blend(sa, sb, sc, va, vb, vc):
            top = jnp.maximum(jnp.maximum(sa, sb), sc)
            ea, eb, ec = jnp.exp(sa - top), jnp.exp(sb - top), jnp.exp(sc - top)
            total = ea + eb + ec
            rounded = lambda e: (e / total).astype(BF).astype(F32)
            mixed = rounded(ea) * va + rounded(eb) * vb + rounded(ec) * vc
            return jnp.concatenate([jnp.zeros((128, LANES - HEAD_COLUMNS), F32), mixed], axis=1).astype(BF)

        halo[0].wait_recv()
        kb, vb = keys_values(before[half])
        sb = jnp.where(position == first_place, -1e30, score(q0, kb))
        yield blend(sb, s00, s01, vb, v0, v1)
        halo[1].wait_recv()
        ka, va = keys_values(after[half])
        sa = jnp.where(position == last_place, -1e30, score(q1, ka))
        yield blend(s10, s11, sa, v0, v1, va)

    def velocity(ref, rows):
        def rows_of(i, carry):
            part = pl.ds(pl.multiple_of(i * 32, 32), 32)
            h = ref[part, :]
            h = h * lax.rsqrt(jnp.mean(h * h, axis=-1, keepdims=True) + 1e-06)
            normed[part, :], lower[part, :] = halves(h)
            return carry

        lax.fori_loop(0, rows // 32, rows_of, 0)
        both = nt_dot(out_three[...], normed[:rows, :]) + nt_dot(out_three[...], lower[:rows, :])
        return both[:16] + both[16:32] + both[32:48]

    def selected(j, t):
        target = lax.broadcasted_iota(jnp.int32, (REST, MAIN), 0)
        source = lax.broadcasted_iota(jnp.int32, (REST, MAIN), 1)
        choose = jnp.where(source == 8 * target - 4 * (target % 2) + 8 * t + j, 1.0, 0.0).astype(BF)
        return dot(choose, first[:MAIN, 768:1152])[:, 96:]

    own = pl.multiple_of(p.s * 32, 32)

    def exchange_tokens(mix, last, mixed_frames):
        ops = []
        for frame, mixed in enumerate(mixed_frames):
            mix[128 * frame : 128 * frame + 128, :LANES] = mixed
            for slot, peer in ((1, p.zpeer), (3, p.zcpeer), (2, p.cpeer)):
                theirs = pl.multiple_of(128 * frame + peer[1] * 32, 32)
                ops.append(
                    copies.start(
                        mix.at[pl.ds(theirs, 32), pl.ds(0, LANES)],
                        last.at[pl.ds(32 * frame, 32), pl.ds(LANES * slot, LANES)],
                        peer,
                    )
                )
            mine = pl.ds(pl.multiple_of(128 * frame + own, 32), 32)
            last[32 * frame : 32 * frame + 32, :LANES] = mix[mine, :LANES]
        return ops

    def move_tokens(last):
        h = jnp.concatenate([hidden[pl.ds(own, 32), :], hidden[pl.ds(own + 128, 32), :]], axis=0)
        hidden[:64, :] = h + nt_dot(last[...], second[:, 768:])
        return velocity(hidden, 64)

    a.v1()
    b.z()
    c.z()
    for op in lat_ops:
        op.wait_recv()
    embed(whole(lat_pieces))
    a.v2()
    a.w_forward(0)
    b.v1()
    normalise(mods[0:1], mods[1:2])
    a.v3()
    b.v2()
    a.w_forward(1, 2)
    b.w_forward(0)
    c.v1()
    b.v3()
    a.w_forward(3)
    b.w_forward(1, 2)
    c.v2()
    c.w_forward(0)
    spread_s.block(0)
    a.end()

    blocks = [selected(j, 0) for j in range(4)]
    pad = jnp.zeros((REST, 96), F32)
    first[MAIN:, :896] = jnp.concatenate(blocks[:3] + [pad[:, :32]], axis=1).astype(BF)
    out_s[MAIN:, :LANES] = jnp.concatenate([blocks[3], pad], axis=1).astype(BF)
    b.w_forward(3)
    c.v3()
    spread_s.rest()
    spread_s.block(3)
    spread_s.block(1)
    project_kv(first, 0)
    project_query(first)
    b.end()
    spread_s.block(2)
    cores_s = [spread_s.core(0)]
    c.w_forward(1, 2)
    mix = mixes.at[0]
    attend_frame(0, 0, mix)
    started = [start_mix(mix, 0)]
    c.w_forward(3)
    spread_t.block(0)
    attend_frame(0, 1, mix)
    started.append(start_mix(mix, 1))
    blocks = [selected(j, 1) for j in range(4)]
    second[MAIN:, :1152] = jnp.concatenate(blocks, axis=1).astype(BF)
    spread_s.wait()
    cores_s.append(spread_s.core(1))
    finish_mix(started)
    spread_t.rest()
    spread_t.block(3)
    spread_t.block(1)
    for op in cores_s:
        op.wait_recv()
    hidden[...] += nt_dot(mix[...], out_s[...])
    normalise(mods[0:1], mods[1:2])
    c.end()
    project_kv(second, 1)
    cores_t = []

    def meanwhile():
        spread_t.block(2)
        cores_t.append(spread_t.core(0))
        project_query(second)

    ops = exchange_tokens(mixes.at[1], mix_last.at[0], temporal(1, 0, 63, meanwhile))
    spread_t.wait()
    cores_t.append(spread_t.core(1))
    for op in ops + cores_t:
        op.wait_recv()
    moved = lat_pieces[p.s, :, :64] - step_sizes[levels[0]] * move_tokens(mix_last.at[0])
    moved = jnp.where(position == 63, lat_pieces[p.s, :, 64:], moved)
    lat_second[p.s] = jnp.concatenate([moved, jnp.zeros((16, 64), F32)], axis=1)
    for op in share(lat_second):
        op.wait_recv()

    embed(whole(lat_second))
    mods_op.wait_recv()
    normalise(mods_next[0:1], mods_next[1:2])
    project_kv(first, 2)
    project_query(first)
    mix = mixes.at[2]
    started = []
    for frame in range(2):
        attend_frame(2, frame, mix)
        started.append(start_mix(mix, frame))
    finish_mix(started)
    hidden[...] += nt_dot(mix[...], out_s[...])
    normalise(mods_next[0:1], mods_next[1:2])
    project_kv(second, 3)
    ops = exchange_tokens(
        mixes.at[3], mix_last.at[1], temporal(3, 63, 62, lambda: project_query(second))
    )
    for op in ops:
        op.wait_recv()
    moved = lat_second[p.s, :, :64] - mods_next[2:3, :64] * move_tokens(mix_last.at[1])
    last_send[...] = jnp.concatenate([moved, jnp.zeros((16, 64), F32)], axis=1)
    shifted = copies.start(last_send, lat_last, p.second)
    shifted.wait_recv()
    final = jnp.where(position == 0, last_noise, lat_last[...])
    for f in range(2):
        high, middle, low = thirds(final[:, 32 * f : 32 * f + 32])
        wide = dot(high, repeat) + dot(middle, repeat) + dot(low, repeat)
        out[f : f + 1, :] = jnp.sum(jnp.where(diagonal, wide, 0.0), axis=0, keepdims=True)
    copies.drain()


def per_device(*operands):
    operands = [operand.T if i in (7, 9, 10) else operand for i, operand in enumerate(operands)]
    smem, whole = pl.BlockSpec(memory_space=pltpu.SMEM), pl.BlockSpec(memory_space=pl.ANY)
    specs = [smem if i in (2, 3) else whole for i in range(len(operands))]
    return pl.pallas_call(
        kernel,
        out_shape=jax.ShapeDtypeStruct((2, 512), F32),
        in_specs=specs,
        out_specs=pl.BlockSpec(memory_space=pltpu.VMEM),
        scratch_shapes=[
            pltpu.VMEM((2, 512), F32),
            pltpu.VMEM((2, 2, 512), F32),
            pltpu.VMEM((30, 2, WIDTH), F32),
            pltpu.VMEM((16, WIDTH), F32),
            pltpu.VMEM((2, 18, 3, HEAD_COLUMNS), BF),
            pltpu.VMEM((2, 18, HEAD_COLUMNS), BF),
            pltpu.VMEM((16, WIDTH), F32),
            pltpu.VMEM((WIDTH, 1152), BF),
            pltpu.VMEM((WIDTH, 4 * LANES), BF),
            pltpu.VMEM((WIDTH, 768 + 4 * LANES), BF),
            pltpu.VMEM((4, 16, 128), F32),
            pltpu.VMEM((4, 16, 128), F32),
            pltpu.VMEM((16, 128), F32),
            pltpu.VMEM((16, 128), F32),
            pltpu.VMEM((8, WIDTH), F32),
            pltpu.VMEM((8, WIDTH), F32),
            pltpu.VMEM((144, WIDTH), BF),
            pltpu.VMEM((144, WIDTH), F32),
            pltpu.VMEM((96, WIDTH), BF),
            pltpu.VMEM((48, WIDTH), BF),
            pltpu.VMEM((256, WIDTH), F32),
            pltpu.VMEM((256, WIDTH), BF),
            pltpu.VMEM((256, WIDTH), BF),
            pltpu.VMEM((256, LANES), F32),
            pltpu.VMEM((4, 256, 640), BF),
            pltpu.VMEM((4, 128, 640), BF),
            pltpu.VMEM((4, 128, 640), BF),
            pltpu.VMEM((4, 256, 4 * LANES), BF),
            pltpu.VMEM((2, 64, 4 * LANES), BF),
            pltpu.VMEM((HEAD_COLUMNS, HEAD_COLUMNS), BF),
            pltpu.SemaphoreType.DMA((9,)),
            pltpu.SemaphoreType.DMA((COPIES,)),
            pltpu.SemaphoreType.DMA((COPIES,)),
        ],
        compiler_params=pltpu.CompilerParams(
            collective_id=0, has_side_effects=True, vmem_limit_bytes=56 * 2**20
        ),
        name="denoise",
    )(*operands)


def solution(mesh):
    placed = (
        P("queue", "space"),
        P(None, None, "space"),
        P("queue", None),
        P(),
        P(),
        P(),
        P("queue", None, "space"),
        P("space", "queue"),
        P("queue", None, "space"),
        P("space", "queue"),
        P(),
    )
    return jax.shard_map(
        per_device, mesh=mesh, in_specs=placed, out_specs=P("queue", "space"), check_vma=False
    )
```

```python
import functools

import jax
import jax.numpy as jnp
from jax import lax
from jax.experimental import pallas as pl
from jax.experimental.pallas import tpu as pltpu
from jax.sharding import PartitionSpec as P

STEPS = 2
BF = jnp.bfloat16
F32 = jnp.float32


MESH = pl.DeviceIdType.MESH
MAIN, REST = 1024, 128
WIDTH = MAIN + REST
HEAD_COLUMNS = 288
HEAD_DIM = 72
INVERSE = 1.0 / HEAD_DIM**0.5
LANES = 384
COPIES = 160


def device_of(n):
    r, j = (n % 64) // 4, n % 4
    x, i = r // 4, r % 4
    zh = i + (x % 2) * (3 - 2 * i)
    y = j + (r % 2) * (3 - 2 * j)
    return (x * 4 + zh) * 4 + y


def span_of(x, zh, y):
    r = x * 4 + zh + (x % 2) * (3 - 2 * zh)
    return r * 4 + y + (r % 2) * (3 - 2 * y)


class Place:
    def __init__(self):
        q, s = lax.axis_index("queue"), lax.axis_index("space")
        self.q, self.s = q, s
        self.x, self.zh, self.y = q // 16, (q // 4) % 4, q % 4
        self.zl, self.c = s // 2, s % 2
        self.v = (1 - self.c) * self.y + self.c * self.x
        self.w = (1 - self.c) * self.x + self.c * self.y
        self.zpeer = (q, (1 - self.zl) * 2 + self.c)
        self.cpeer = (q, self.zl * 2 + 1 - self.c)
        self.zcpeer = (q, (1 - self.zl) * 2 + 1 - self.c)
        self.n = span_of(self.x, self.zh, self.y)
        self.next = (device_of(self.n + 1), s)
        self.previous = (device_of(self.n + 63), s)
        self.worker, self.holder = device_of(q), self.n
        self.worker_before, self.holder_after = device_of(q + 63), (self.n + 1) % 64
        self.final, self.final_source = (self.n + 2) % 64, device_of(q + 62)

    def cell(self, v, w):
        x = self.c * v + (1 - self.c) * w
        y = (1 - self.c) * v + self.c * w
        return x * 4 + y

    def ring(self, v, w):
        x = self.c * v + (1 - self.c) * w
        y = (1 - self.c) * v + self.c * w
        return ((x * 4 + self.zh) * 4 + y, self.s)

    def up(self, dz):
        return ((self.x * 4 + (self.zh + dz) % 4) * 4 + self.y, self.s)

    def beside(self, dz):
        z = (self.zh * 2 + self.zl + dz) % 8
        return ((self.x * 4 + z // 2) * 4 + self.y, (z % 2) * 2 + self.c)


class Copies:
    def __init__(self, send, recv):
        self.send, self.recv, self.started = send, recv, []

    def start(self, src, dst, target):
        i = len(self.started)
        assert i < COPIES
        op = pltpu.make_async_remote_copy(
            src_ref=src,
            dst_ref=dst,
            send_sem=self.send.at[i],
            recv_sem=self.recv.at[i],
            device_id=target,
            device_id_type=MESH,
        )
        op.start()
        self.started.append(op)
        return op

    def route(self, src, dst, target, me):
        same = (target[0] == me[0]) & (target[1] == me[1])
        op = Routed(src, dst, same)
        i = len(self.started)
        op.remote = pltpu.make_async_remote_copy(
            src_ref=src,
            dst_ref=dst,
            send_sem=self.send.at[i],
            recv_sem=self.recv.at[i],
            device_id=target,
            device_id_type=MESH,
        )
        pl.when(jnp.logical_not(same))(op.remote.start)
        pl.when(same)(op.keep)
        self.started.append(op)
        return op

    def drain(self):
        for op in self.started:
            op.wait_send()


class Routed:
    def __init__(self, src, dst, same):
        self.src, self.dst, self.same = src, dst, same

    def keep(self):
        self.dst[...] = self.src[...]

    def wait_recv(self):
        pl.when(jnp.logical_not(self.same))(self.remote.wait_recv)

    def wait_send(self):
        pl.when(jnp.logical_not(self.same))(self.remote.wait_send)


def greet(partners, perhaps, me):
    barrier = pltpu.get_barrier_semaphore()
    count = len(partners)
    for partner in partners:
        pl.semaphore_signal(barrier, inc=1, device_id=partner, device_id_type=MESH)
    for partner in perhaps:
        other = (partner[0] != me[0]) | (partner[1] != me[1])

        @pl.when(other)
        def _():
            pl.semaphore_signal(barrier, inc=1, device_id=partner, device_id_type=MESH)

        count = count + jnp.where(other, 1, 0)
    pl.semaphore_wait(barrier, count)


class Stream:
    def __init__(self, place, copies, buf, columns):
        self.p, self.copies, self.buf, self.columns = place, copies, buf, columns
        self.ops = {}

    def copy(self, key, rows, count, target):
        part = self.buf.at[pl.ds(pl.multiple_of(rows, 16), count), pl.ds(*self.columns)]
        self.ops[key] = self.copies.start(part, part, target)

    def place(self, piece):
        p = self.p
        self.row = pl.multiple_of((p.cell(p.v, p.w) * 4 + p.zh) * 16, 16)
        self.buf[pl.ds(self.row, 16), pl.ds(*self.columns)] = piece

    def z(self):
        for d in (1, 3, 2):
            self.copy(("z", d), self.row, 16, self.p.up(d))

    def both(self, key, v, w, right, left):
        rows = self.p.cell(v, w) * 64
        self.copy((key, "R"), rows, 64, right)
        self.copy((key, "L"), rows, 64, left)

    def w_sends(self, k):
        p = self.p
        v = (p.v + (0, 3, 1, 2)[k]) % 4
        self.both(("w", k), v, p.w, p.ring(p.v, (p.w + 1) % 4), p.ring(p.v, (p.w + 3) % 4))

    def v1(self):
        p = self.p
        for d in (1, 3, 2):
            self.ops["z", d].wait_recv()
        self.both("v", p.v, p.w, p.ring((p.v + 1) % 4, p.w), p.ring((p.v + 3) % 4, p.w))
        self.w_sends(0)

    def v2(self):
        p = self.p
        self.ops["v", "R"].wait_recv()
        self.copy("vfR", p.cell((p.v + 3) % 4, p.w) * 64, 32, p.ring((p.v + 1) % 4, p.w))
        self.w_sends(1)
        self.ops["v", "L"].wait_recv()
        self.copy("vfL", p.cell((p.v + 1) % 4, p.w) * 64 + 32, 32, p.ring((p.v + 3) % 4, p.w))
        self.w_sends(2)

    def w_forward(self, *blocks):
        p = self.p
        for k in blocks:
            v = (p.v + (0, 3, 1, 2)[k]) % 4
            self.ops[("w", k), "R"].wait_recv()
            self.copy(("wfR", k), p.cell(v, (p.w + 3) % 4) * 64, 32, p.ring(p.v, (p.w + 1) % 4))
            self.ops[("w", k), "L"].wait_recv()
            self.copy(("wfL", k), p.cell(v, (p.w + 1) % 4) * 64 + 32, 32, p.ring(p.v, (p.w + 3) % 4))

    def v3(self):
        self.ops["vfR"].wait_recv()
        self.ops["vfL"].wait_recv()
        self.w_sends(3)

    def end(self):
        for k in range(4):
            self.ops["wfR", k].wait_recv()
            self.ops["wfL", k].wait_recv()


class Spread:
    def __init__(self, place, copies, buf, first):
        self.p, self.copies, self.buf, self.first = place, copies, buf, first
        self.ops = []

    def part(self, slot, rows, count):
        return self.buf.at[pl.ds(pl.multiple_of(rows, 16), count), pl.ds(self.first + LANES * slot, LANES)]

    def block(self, dw):
        p = self.p
        for v in range(4):
            rows = p.cell(v, (p.w + dw) % 4) * 64
            to = p.beside(1 if v < 2 else 7)
            self.ops.append(self.copies.start(self.part(0, rows, 64), self.part(1, rows, 64), to))

    def rest(self):
        self.ops.append(
            self.copies.start(self.part(0, MAIN, REST), self.part(1, MAIN, REST), self.p.zpeer)
        )

    def core(self, slot):
        return self.copies.start(
            self.part(slot, 0, WIDTH), self.part(slot + 2, 0, WIDTH), self.p.cpeer
        )

    def wait(self):
        for op in self.ops:
            op.wait_recv()


def nt_dot(a, b):
    return lax.dot_general(a, b, (((1,), (1,)), ((), ())), preferred_element_type=F32)


def dot(a, b):
    return jnp.dot(a, b, preferred_element_type=F32)


def halves(array):
    high = array.astype(BF)
    return high, (array - high.astype(F32)).astype(BF)


def thirds(array):
    high = array.astype(BF)
    rest = array - high.astype(F32)
    middle = rest.astype(BF)
    return high, middle, (rest - middle.astype(F32)).astype(BF)


def iotas(shape):
    return [lax.broadcasted_iota(jnp.int32, shape, axis) for axis in (0, 1)]


def head_masks(rows):
    lane = lax.broadcasted_iota(jnp.int32, (rows, HEAD_COLUMNS), 1)
    return [(lane >= HEAD_DIM * h) & (lane < HEAD_DIM * (h + 1)) for h in range(4)]


def kernel(
    latents,
    fresh_noise,
    level_index,
    step_sizes,
    time_table,
    embed_in,
    spatial_qkv,
    spatial_out,
    temporal_qkv,
    temporal_out,
    embed_out,
    out,
    in_latents,
    in_noise,
    in_table,
    in_embed,
    in_qkv,
    in_out,
    in_velocity,
    first,
    out_s,
    second,
    lat_own,
    lat_pieces,
    lat_second,
    lat_last,
    last_send,
    mods_own,
    mods_here,
    features,
    features_new,
    embed_six,
    out_three,
    hidden,
    normed,
    lower,
    query,
    kv,
    before,
    after,
    mixes,
    mix_last,
    same_head,
    local,
    send,
    recv,
):
    p = Place()
    copies = Copies(send, recv)
    fetches = [
        pltpu.make_async_copy(src, dst, local.at[i])
        for i, (src, dst) in enumerate(
            (
                (spatial_qkv, in_qkv.at[0]),
                (temporal_qkv, in_qkv.at[1]),
                (spatial_out, in_out.at[0]),
                (temporal_out, in_out.at[1]),
                (latents, in_latents),
                (fresh_noise, in_noise),
                (embed_in, in_embed),
                (embed_out, in_velocity),
                (time_table, in_table),
            )
        )
    ]
    for fetch in fetches:
        fetch.start()
    partners = [p.up(d) for d in (1, 2, 3)]
    partners += [p.ring((p.v + d) % 4, p.w) for d in (1, 3)]
    partners += [p.ring(p.v, (p.w + d) % 4) for d in (1, 3)]
    partners += [p.beside(1), p.beside(7), p.cpeer, p.zcpeer]
    partners += [p.next, p.previous]
    me = (p.q, p.s)
    perhaps = [(q, s) for q in (p.worker, p.holder) for s in range(4)]
    perhaps += [(q, p.s) for q in (p.worker_before, p.holder_after, p.final, p.final_source)]
    greet(partners, perhaps, me)
    a = Stream(p, copies, first, (0, 1152))
    b = Stream(p, copies, out_s, (0, LANES))
    c = Stream(p, copies, second, (0, 1152))
    spread_s = Spread(p, copies, out_s, 0)
    spread_t = Spread(p, copies, second, 768)
    position = p.n

    for fetch in fetches[:4]:
        fetch.wait()
    to, source = iotas((16, 18))
    leading = jnp.where(to == source, 1.0, 0.0).astype(BF)
    rest = jnp.zeros((16, HEAD_COLUMNS), F32)
    blocks = []
    for t in range(2):
        for j in range(4):
            chosen = (source >= 16) & (to == 8 * t + 4 * (source - 16) + j)
            chosen = jnp.where(chosen, 1.0, 0.0).astype(BF)
            block = in_qkv[t, :, j, :] if j < 3 else in_out[t]
            blocks.append(dot(leading, block))
            rest = rest + dot(chosen, block)
    a.place(jnp.concatenate(blocks[:3] + [rest], axis=1).astype(BF))
    a.z()
    pad = jnp.zeros((16, LANES - HEAD_COLUMNS), F32)
    b.place(jnp.concatenate([blocks[3], pad], axis=1).astype(BF))
    b.z()
    c.place(jnp.concatenate(blocks[4:], axis=1).astype(BF))

    for fetch in fetches[4:]:
        fetch.wait()
    sub, lane = iotas((16, 512))
    diagonal = (lane & 15) == sub
    token, lane = iotas((32, 512))
    repeat = jnp.where((lane >> 4) == token, 1.0, 0.0).astype(BF)

    def unflatten(line):
        wide = jnp.where(diagonal, jnp.broadcast_to(line, (16, 512)), 0.0)
        high, middle, low = thirds(wide)
        return nt_dot(high, repeat) + nt_dot(middle, repeat) + nt_dot(low, repeat)

    lines = [in_latents[f : f + 1, :] for f in range(2)] + [in_noise[0, f : f + 1, :] for f in range(2)]
    lat_own[...] = jnp.concatenate([unflatten(line) for line in lines], axis=1)

    def share(pieces):
        own = pieces.at[p.s]
        return [copies.start(own, own, t) for t in (p.cpeer, p.zpeer, p.zcpeer)]

    def whole(pieces):
        parts = [pieces[s, :, 32 * f : 32 * f + 32] for f in range(2) for s in range(4)]
        return jnp.concatenate(parts, axis=1)

    lat_ops = [
        copies.route(lat_own, lat_pieces.at[p.s], (p.worker, s), me)
        for s in (p.s, p.cpeer[1], p.zpeer[1], p.zcpeer[1])
    ]
    last_noise = jnp.concatenate(
        [unflatten(in_noise[1, f : f + 1, :]) for f in range(2)] + [jnp.zeros((16, 64), F32)], axis=1
    )

    levels = [level_index[0, step] for step in range(STEPS)]
    small = jnp.concatenate(
        [in_embed[...], in_velocity[...], in_table[levels[0]], in_table[levels[1]], jnp.zeros((4, WIDTH), F32)],
        axis=0,
    )
    for i, part in enumerate(thirds(small)):
        features[48 * i : 48 * i + 40, :] = part
        features[48 * i + 40 : 48 * i + 48, :] = jnp.zeros((8, WIDTH), BF)
    new = lax.broadcasted_iota(jnp.int32, (1, WIDTH), 1)
    late = new - MAIN
    piece = jnp.where(new < MAIN, new >> 4, late >> 1)
    within = jnp.where(new < MAIN, new & 15, 16 + (late & 1))
    owner = (piece & 48) + ((piece & 3) << 2) + ((piece >> 2) & 3)
    old = owner * 18 + within
    features_new[...] = jnp.zeros((144, WIDTH), F32)

    def reorder(i, carry):
        row = lax.broadcasted_iota(jnp.int32, (128, WIDTH), 0) + i * 128
        move = jnp.where(row == old, 1.0, 0.0).astype(BF)
        features_new[...] += dot(features[:, pl.ds(pl.multiple_of(i * 128, 128), 128)], move)
        return carry

    lax.fori_loop(0, 9, reorder, 0)
    parts = [features_new[48 * i : 48 * i + 16, :] for i in range(3)]
    embed_six[...] = jnp.concatenate([parts[i] for i in (0, 1, 0, 1, 2, 0)], axis=0).astype(BF)
    out_three[...] = jnp.concatenate(
        [features_new[48 * i + 16 : 48 * i + 32, :] for i in range(3)], axis=0
    ).astype(BF)
    mods = features_new[32:36, :] + features_new[80:84, :] + features_new[128:132, :]
    for step in range(STEPS):
        size_line = jnp.full((1, WIDTH), step_sizes[levels[step]], F32)
        lines = [mods[2 * step : 2 * step + 2], size_line, jnp.zeros((5, WIDTH), F32)]
        mods_own[step] = jnp.concatenate(lines, axis=0)
    mods_ops = [
        copies.route(mods_own.at[step], mods_here.at[step], (target, p.s), me)
        for step, target in enumerate((p.worker, p.worker_before))
    ]

    row, column = iotas((HEAD_COLUMNS, HEAD_COLUMNS))
    same = jnp.zeros((HEAD_COLUMNS, HEAD_COLUMNS), F32)
    for h in range(4):
        low, high = HEAD_DIM * h, HEAD_DIM * (h + 1)
        inside = (row >= low) & (row < high) & (column >= low) & (column < high)
        same = jnp.where(inside, 1.0, same)
    same_head[...] = same.astype(BF)

    def embed(lat):
        high, middle, low = (part.astype(F32) for part in thirds(lat))
        stack = jnp.concatenate([high, high, middle, middle, high, low], axis=0)
        hidden[...] = dot(stack.T.astype(BF), embed_six[...])

    def normalise(step, frames=(0, 1)):
        shift, scale = mods_here[step, 0:1, :], 1.0 + mods_here[step, 1:2, :]

        def rows_of(i, carry):
            rows = pl.ds(pl.multiple_of(i * 32, 32), 32)
            h = hidden[rows, :]
            inverse = lax.rsqrt(jnp.mean(h * h, axis=-1, keepdims=True) + 1e-06)
            normed[rows, :] = (h * inverse * scale + shift).astype(BF)
            return carry

        lax.fori_loop(4 * frames[0], 4 * frames[-1] + 4, rows_of, 0)

    def project_kv(weights, half, rows=slice(0, 256)):
        kv[half, rows, :] = dot(normed[rows, :], weights[:, 256:896]).astype(BF)

    def project_query(weights):
        query[...] = dot(normed[...], weights[:, :384])

    def attend_frame(half, frame, mix):
        rows = slice(128 * frame, 128 * frame + 128)
        masks = head_masks(128)
        q = query[rows, :HEAD_COLUMNS].astype(BF).astype(F32)
        both = kv[half, rows, :].astype(F32)
        k = both[:, 32 : 32 + HEAD_COLUMNS].astype(BF)
        v = both[:, 320 : 320 + HEAD_COLUMNS]
        q_heads = jnp.concatenate([jnp.where(m, q, 0.0).astype(BF) for m in masks], axis=0)
        v_heads = jnp.concatenate([jnp.where(m, v, 0.0).astype(BF) for m in masks], axis=0)
        scores = nt_dot(q_heads, k) * INVERSE
        scores = jnp.exp(scores - jnp.max(scores, axis=-1, keepdims=True))
        probs = (scores / jnp.sum(scores, axis=-1, keepdims=True)).astype(BF)
        probs = jnp.concatenate([probs[128 * h : 128 * h + 128] for h in range(4)], axis=1)
        mixed = dot(probs, v_heads)
        mixed = jnp.concatenate([mixed, jnp.zeros((128, LANES - HEAD_COLUMNS), F32)], axis=1)
        mix[rows, :LANES] = mixed.astype(BF)

    def start_mix(mix, frame):
        part = lambda slot: mix.at[pl.ds(128 * frame, 128), pl.ds(LANES * slot, LANES)]
        by_z = copies.start(part(0), part(1), p.zpeer)
        by_core = copies.start(part(0), part(2), p.cpeer)
        return by_z, by_core, part

    def finish_mix(started):
        last = []
        for by_z, _, part in started:
            by_z.wait_recv()
            last.append(copies.start(part(1), part(3), p.cpeer))

        def wait(frame):
            started[frame][1].wait_recv()
            last[frame].wait_recv()

        return wait

    def spatial_out(mix, frame):
        rows = slice(128 * frame, 128 * frame + 128)
        hidden[rows, :] += nt_dot(mix[rows, :], out_s[...])

    def start_halo(half, frame):
        rows = kv.at[half, pl.ds(128 * frame, 128)]
        if frame == 1:
            return copies.start(rows, before.at[half], p.next)
        return copies.start(rows, after.at[half], p.previous)

    def temporal(half, halo, first_place, last_place, prepare):
        prepare()

        def keys_values(ref_value):
            both = ref_value.astype(F32)
            return both[:, 32 : 32 + HEAD_COLUMNS], both[:, 320 : 320 + HEAD_COLUMNS]

        def score(q, k):
            high, low = halves(q * k)
            same_now = same_head[...]
            return (dot(high, same_now) + dot(low, same_now)) * INVERSE

        q0 = query[:128, :HEAD_COLUMNS].astype(BF).astype(F32)
        q1 = query[128:, :HEAD_COLUMNS].astype(BF).astype(F32)
        k0, v0 = keys_values(kv[half, :128])
        k1, v1 = keys_values(kv[half, 128:])
        s00, s01, s10, s11 = score(q0, k0), score(q0, k1), score(q1, k0), score(q1, k1)

        def blend(sa, sb, sc, va, vb, vc):
            top = jnp.maximum(jnp.maximum(sa, sb), sc)
            ea, eb, ec = jnp.exp(sa - top), jnp.exp(sb - top), jnp.exp(sc - top)
            total = ea + eb + ec
            rounded = lambda e: (e / total).astype(BF).astype(F32)
            mixed = rounded(ea) * va + rounded(eb) * vb + rounded(ec) * vc
            return jnp.concatenate([jnp.zeros((128, LANES - HEAD_COLUMNS), F32), mixed], axis=1).astype(BF)

        halo[0].wait_recv()
        ka, va = keys_values(after[half])
        sa = jnp.where(position == last_place, -1e30, score(q1, ka))
        yield 1, blend(s10, s11, sa, v0, v1, va)
        halo[1].wait_recv()
        kb, vb = keys_values(before[half])
        sb = jnp.where(position == first_place, -1e30, score(q0, kb))
        yield 0, blend(sb, s00, s01, vb, v0, v1)

    def velocity(ref, rows):
        def rows_of(i, carry):
            part = pl.ds(pl.multiple_of(i * 32, 32), 32)
            h = ref[part, :]
            h = h * lax.rsqrt(jnp.mean(h * h, axis=-1, keepdims=True) + 1e-06)
            normed[part, :], lower[part, :] = halves(h)
            return carry

        lax.fori_loop(0, rows // 32, rows_of, 0)
        both = nt_dot(out_three[...], normed[:rows, :]) + nt_dot(out_three[...], lower[:rows, :])
        return both[:16] + both[16:32] + both[32:48]

    def selected(j, t):
        target = lax.broadcasted_iota(jnp.int32, (REST, MAIN), 0)
        source = lax.broadcasted_iota(jnp.int32, (REST, MAIN), 1)
        choose = jnp.where(source == 8 * target - 4 * (target % 2) + 8 * t + j, 1.0, 0.0).astype(BF)
        return dot(choose, first[:MAIN, 768:1152])[:, 96:]

    own = pl.multiple_of(p.s * 32, 32)

    def exchange_tokens(mix, last, mixed_frames):
        ops = []
        for frame, mixed in mixed_frames:
            mix[128 * frame : 128 * frame + 128, :LANES] = mixed
            for slot, peer in ((1, p.zpeer), (3, p.zcpeer), (2, p.cpeer)):
                theirs = pl.multiple_of(128 * frame + peer[1] * 32, 32)
                ops.append(
                    copies.start(
                        mix.at[pl.ds(theirs, 32), pl.ds(0, LANES)],
                        last.at[pl.ds(32 * frame, 32), pl.ds(LANES * slot, LANES)],
                        peer,
                    )
                )
            mine = pl.ds(pl.multiple_of(128 * frame + own, 32), 32)
            last[32 * frame : 32 * frame + 32, :LANES] = mix[mine, :LANES]
        return ops

    def move_tokens(last):
        h = jnp.concatenate([hidden[pl.ds(own, 32), :], hidden[pl.ds(own + 128, 32), :]], axis=0)
        hidden[:64, :] = h + nt_dot(last[...], second[:, 768:])
        return velocity(hidden, 64)

    c.z()
    a.v1()
    for op in lat_ops:
        op.wait_recv()
    embed(whole(lat_pieces))
    b.v1()
    a.v2()
    a.w_forward(0)
    for op in mods_ops:
        op.wait_recv()
    normalise(0)
    b.v2()
    a.v3()
    b.w_forward(0)
    a.w_forward(1, 2)
    b.v3()
    c.v1()
    a.w_forward(3)
    b.w_forward(1, 2)
    b.w_forward(3)
    c.v2()
    c.w_forward(0)
    spread_s.block(0)
    spread_s.block(3)
    spread_s.block(1)
    a.end()

    blocks = [selected(j, 0) for j in range(4)]
    pad = jnp.zeros((REST, 96), F32)
    first[MAIN:, :896] = jnp.concatenate(blocks[:3] + [pad[:, :32]], axis=1).astype(BF)
    out_s[MAIN:, :LANES] = jnp.concatenate([blocks[3], pad], axis=1).astype(BF)
    b.end()
    c.v3()
    spread_s.rest()
    spread_s.block(2)
    cores_s = [spread_s.core(0)]
    project_kv(first, 0)
    project_query(first)
    c.w_forward(1, 2)
    mix = mixes.at[0]
    attend_frame(0, 0, mix)
    started = [start_mix(mix, 0)]
    c.w_forward(3)
    spread_t.block(0)
    attend_frame(0, 1, mix)
    started.append(start_mix(mix, 1))
    spread_t.block(3)
    spread_t.block(1)
    spread_s.wait()
    cores_s.append(spread_s.core(1))
    wait_mix = finish_mix(started)
    blocks = [selected(j, 1) for j in range(4)]
    second[MAIN:, :1152] = jnp.concatenate(blocks, axis=1).astype(BF)
    for op in cores_s:
        op.wait_recv()
    for frame in range(2):
        wait_mix(frame)
        spatial_out(mix, frame)
    normalise(0)
    c.end()
    project_kv(second, 1)
    halo = [start_halo(1, 0), start_halo(1, 1)]
    cores_t = []

    def meanwhile():
        spread_t.rest()
        spread_t.block(2)
        cores_t.append(spread_t.core(0))
        project_query(second)

    ops = exchange_tokens(mixes.at[1], mix_last.at[0], temporal(1, halo, 0, 63, meanwhile))
    spread_t.wait()
    cores_t.append(spread_t.core(1))
    for op in ops + cores_t:
        op.wait_recv()
    moved = lat_pieces[p.s, :, :64] - mods_here[0, 2:3, :64] * move_tokens(mix_last.at[0])
    moved = jnp.where(position == 63, lat_pieces[p.s, :, 64:], moved)
    lat_second[p.s] = jnp.concatenate([moved, jnp.zeros((16, 64), F32)], axis=1)
    for op in share(lat_second):
        op.wait_recv()

    embed(whole(lat_second))
    normalise(1)
    project_kv(first, 2)
    project_query(first)
    mix = mixes.at[2]
    started = []
    for frame in range(2):
        attend_frame(2, frame, mix)
        started.append(start_mix(mix, frame))
    wait_mix = finish_mix(started)
    halo = []
    for frame in range(2):
        wait_mix(frame)
        spatial_out(mix, frame)
        normalise(1, (frame,))
        project_kv(second, 3, slice(128 * frame, 128 * frame + 128))
        halo.append(start_halo(3, frame))
    ops = exchange_tokens(
        mixes.at[3], mix_last.at[1], temporal(3, halo, 63, 62, lambda: project_query(second))
    )
    for op in ops:
        op.wait_recv()
    moved = lat_second[p.s, :, :64] - mods_here[1, 2:3, :64] * move_tokens(mix_last.at[1])
    last_send[...] = jnp.concatenate([moved, jnp.zeros((16, 64), F32)], axis=1)
    shifted = copies.route(last_send, lat_last, (p.final, p.s), me)
    shifted.wait_recv()
    final = jnp.where(p.q == 0, last_noise, lat_last[...])
    for f in range(2):
        high, middle, low = thirds(final[:, 32 * f : 32 * f + 32])
        wide = dot(high, repeat) + dot(middle, repeat) + dot(low, repeat)
        out[f : f + 1, :] = jnp.sum(jnp.where(diagonal, wide, 0.0), axis=0, keepdims=True)
    copies.drain()


def per_device(*operands):
    operands = [operand.T if i in (7, 9, 10) else operand for i, operand in enumerate(operands)]
    smem, whole = pl.BlockSpec(memory_space=pltpu.SMEM), pl.BlockSpec(memory_space=pl.ANY)
    specs = [smem if i in (2, 3) else whole for i in range(len(operands))]
    return pl.pallas_call(
        kernel,
        out_shape=jax.ShapeDtypeStruct((2, 512), F32),
        in_specs=specs,
        out_specs=pl.BlockSpec(memory_space=pltpu.VMEM),
        scratch_shapes=[
            pltpu.VMEM((2, 512), F32),
            pltpu.VMEM((2, 2, 512), F32),
            pltpu.VMEM((30, 2, WIDTH), F32),
            pltpu.VMEM((16, WIDTH), F32),
            pltpu.VMEM((2, 18, 3, HEAD_COLUMNS), BF),
            pltpu.VMEM((2, 18, HEAD_COLUMNS), BF),
            pltpu.VMEM((16, WIDTH), F32),
            pltpu.VMEM((WIDTH, 1152), BF),
            pltpu.VMEM((WIDTH, 4 * LANES), BF),
            pltpu.VMEM((WIDTH, 768 + 4 * LANES), BF),
            pltpu.VMEM((16, 128), F32),
            pltpu.VMEM((4, 16, 128), F32),
            pltpu.VMEM((4, 16, 128), F32),
            pltpu.VMEM((16, 128), F32),
            pltpu.VMEM((16, 128), F32),
            pltpu.VMEM((2, 8, WIDTH), F32),
            pltpu.VMEM((2, 8, WIDTH), F32),
            pltpu.VMEM((144, WIDTH), BF),
            pltpu.VMEM((144, WIDTH), F32),
            pltpu.VMEM((96, WIDTH), BF),
            pltpu.VMEM((48, WIDTH), BF),
            pltpu.VMEM((256, WIDTH), F32),
            pltpu.VMEM((256, WIDTH), BF),
            pltpu.VMEM((256, WIDTH), BF),
            pltpu.VMEM((256, LANES), F32),
            pltpu.VMEM((4, 256, 640), BF),
            pltpu.VMEM((4, 128, 640), BF),
            pltpu.VMEM((4, 128, 640), BF),
            pltpu.VMEM((4, 256, 4 * LANES), BF),
            pltpu.VMEM((2, 64, 4 * LANES), BF),
            pltpu.VMEM((HEAD_COLUMNS, HEAD_COLUMNS), BF),
            pltpu.SemaphoreType.DMA((9,)),
            pltpu.SemaphoreType.DMA((COPIES,)),
            pltpu.SemaphoreType.DMA((COPIES,)),
        ],
        compiler_params=pltpu.CompilerParams(
            collective_id=0, has_side_effects=True, vmem_limit_bytes=56 * 2**20
        ),
        name="denoise",
    )(*operands)


def solution(mesh):
    placed = (
        P("queue", "space"),
        P(None, None, "space"),
        P("queue", None),
        P(),
        P(),
        P(),
        P("queue", None, "space"),
        P("space", "queue"),
        P("queue", None, "space"),
        P("space", "queue"),
        P(),
    )
    return jax.shard_map(
        per_device, mesh=mesh, in_specs=placed, out_specs=P("queue", "space"), check_vma=False
    )
```

```python
import functools

import jax
import jax.numpy as jnp
from jax import lax
from jax.experimental import pallas as pl
from jax.experimental.pallas import tpu as pltpu
from jax.sharding import PartitionSpec as P

STEPS = 2
BF = jnp.bfloat16
F32 = jnp.float32


MESH = pl.DeviceIdType.MESH
MAIN, REST = 1024, 128
WIDTH = MAIN + REST
HEAD_COLUMNS = 288
HEAD_DIM = 72
INVERSE = 1.0 / HEAD_DIM**0.5
LANES = 384
COPIES = 160


def device_of(n):
    r, j = (n % 64) // 4, n % 4
    x, i = r // 4, r % 4
    zh = i + (x % 2) * (3 - 2 * i)
    y = j + (r % 2) * (3 - 2 * j)
    return (x * 4 + zh) * 4 + y


def span_of(x, zh, y):
    r = x * 4 + zh + (x % 2) * (3 - 2 * zh)
    return r * 4 + y + (r % 2) * (3 - 2 * y)


class Place:
    def __init__(self):
        q, s = lax.axis_index("queue"), lax.axis_index("space")
        self.q, self.s = q, s
        self.x, self.zh, self.y = q // 16, (q // 4) % 4, q % 4
        self.zl, self.c = s // 2, s % 2
        self.v = (1 - self.c) * self.y + self.c * self.x
        self.w = (1 - self.c) * self.x + self.c * self.y
        self.zpeer = (q, (1 - self.zl) * 2 + self.c)
        self.cpeer = (q, self.zl * 2 + 1 - self.c)
        self.zcpeer = (q, (1 - self.zl) * 2 + 1 - self.c)
        self.n = span_of(self.x, self.zh, self.y)
        self.next = (device_of(self.n + 1), s)
        self.previous = (device_of(self.n + 63), s)
        self.worker, self.holder = device_of(q), self.n
        self.worker_before, self.holder_after = device_of(q + 63), (self.n + 1) % 64
        self.final, self.final_source = (self.n + 2) % 64, device_of(q + 62)

    def cell(self, v, w):
        x = self.c * v + (1 - self.c) * w
        y = (1 - self.c) * v + self.c * w
        return x * 4 + y

    def ring(self, v, w):
        x = self.c * v + (1 - self.c) * w
        y = (1 - self.c) * v + self.c * w
        return ((x * 4 + self.zh) * 4 + y, self.s)

    def up(self, dz):
        return ((self.x * 4 + (self.zh + dz) % 4) * 4 + self.y, self.s)

    def beside(self, dz):
        z = (self.zh * 2 + self.zl + dz) % 8
        return ((self.x * 4 + z // 2) * 4 + self.y, (z % 2) * 2 + self.c)


class Copies:
    def __init__(self, send, recv):
        self.send, self.recv, self.started = send, recv, []

    def start(self, src, dst, target):
        i = len(self.started)
        assert i < COPIES
        op = pltpu.make_async_remote_copy(
            src_ref=src,
            dst_ref=dst,
            send_sem=self.send.at[i],
            recv_sem=self.recv.at[i],
            device_id=target,
            device_id_type=MESH,
        )
        op.start()
        self.started.append(op)
        return op

    def route(self, src, dst, target, me):
        same = (target[0] == me[0]) & (target[1] == me[1])
        op = Routed(src, dst, same)
        i = len(self.started)
        op.remote = pltpu.make_async_remote_copy(
            src_ref=src,
            dst_ref=dst,
            send_sem=self.send.at[i],
            recv_sem=self.recv.at[i],
            device_id=target,
            device_id_type=MESH,
        )
        pl.when(jnp.logical_not(same))(op.remote.start)
        pl.when(same)(op.keep)
        self.started.append(op)
        return op

    def drain(self):
        for op in self.started:
            op.wait_send()


class Routed:
    def __init__(self, src, dst, same):
        self.src, self.dst, self.same = src, dst, same

    def keep(self):
        self.dst[...] = self.src[...]

    def wait_recv(self):
        pl.when(jnp.logical_not(self.same))(self.remote.wait_recv)

    def wait_send(self):
        pl.when(jnp.logical_not(self.same))(self.remote.wait_send)


def greet(partners, perhaps, me):
    barrier = pltpu.get_barrier_semaphore()
    count = len(partners)
    for partner in partners:
        pl.semaphore_signal(barrier, inc=1, device_id=partner, device_id_type=MESH)
    for partner in perhaps:
        other = (partner[0] != me[0]) | (partner[1] != me[1])

        @pl.when(other)
        def _():
            pl.semaphore_signal(barrier, inc=1, device_id=partner, device_id_type=MESH)

        count = count + jnp.where(other, 1, 0)
    pl.semaphore_wait(barrier, count)


class Stream:
    def __init__(self, place, copies, buf, columns):
        self.p, self.copies, self.buf, self.columns = place, copies, buf, columns
        self.ops = {}

    def copy(self, key, rows, count, target):
        part = self.buf.at[pl.ds(pl.multiple_of(rows, 16), count), pl.ds(*self.columns)]
        self.ops[key] = self.copies.start(part, part, target)

    def place(self, piece):
        p = self.p
        self.row = pl.multiple_of((p.cell(p.v, p.w) * 4 + p.zh) * 16, 16)
        self.buf[pl.ds(self.row, 16), pl.ds(*self.columns)] = piece

    def z(self):
        for d in (1, 3, 2):
            self.copy(("z", d), self.row, 16, self.p.up(d))

    def both(self, key, v, w, right, left):
        rows = self.p.cell(v, w) * 64
        self.copy((key, "R"), rows, 64, right)
        self.copy((key, "L"), rows, 64, left)

    def w_sends(self, k):
        p = self.p
        v = (p.v + (0, 3, 1, 2)[k]) % 4
        self.both(("w", k), v, p.w, p.ring(p.v, (p.w + 1) % 4), p.ring(p.v, (p.w + 3) % 4))

    def v1(self):
        p = self.p
        for d in (1, 3, 2):
            self.ops["z", d].wait_recv()
        self.both("v", p.v, p.w, p.ring((p.v + 1) % 4, p.w), p.ring((p.v + 3) % 4, p.w))
        self.w_sends(0)

    def v2(self):
        p = self.p
        self.ops["v", "R"].wait_recv()
        self.copy("vfR", p.cell((p.v + 3) % 4, p.w) * 64, 32, p.ring((p.v + 1) % 4, p.w))
        self.w_sends(1)
        self.ops["v", "L"].wait_recv()
        self.copy("vfL", p.cell((p.v + 1) % 4, p.w) * 64 + 32, 32, p.ring((p.v + 3) % 4, p.w))
        self.w_sends(2)

    def w_forward(self, *blocks):
        p = self.p
        for k in blocks:
            v = (p.v + (0, 3, 1, 2)[k]) % 4
            self.ops[("w", k), "R"].wait_recv()
            self.copy(("wfR", k), p.cell(v, (p.w + 3) % 4) * 64, 32, p.ring(p.v, (p.w + 1) % 4))
            self.ops[("w", k), "L"].wait_recv()
            self.copy(("wfL", k), p.cell(v, (p.w + 1) % 4) * 64 + 32, 32, p.ring(p.v, (p.w + 3) % 4))

    def v3(self):
        self.ops["vfR"].wait_recv()
        self.ops["vfL"].wait_recv()
        self.w_sends(3)

    def end(self):
        for k in range(4):
            self.ops["wfR", k].wait_recv()
            self.ops["wfL", k].wait_recv()


class Spread:
    def __init__(self, place, copies, buf, first):
        self.p, self.copies, self.buf, self.first = place, copies, buf, first
        self.ops = []

    def part(self, slot, rows, count):
        return self.buf.at[pl.ds(pl.multiple_of(rows, 16), count), pl.ds(self.first + LANES * slot, LANES)]

    def block(self, dw):
        p = self.p
        for v in range(4):
            rows = p.cell(v, (p.w + dw) % 4) * 64
            to = p.beside(1 if v < 2 else 7)
            self.ops.append(self.copies.start(self.part(0, rows, 64), self.part(1, rows, 64), to))

    def rest(self):
        self.ops.append(
            self.copies.start(self.part(0, MAIN, REST), self.part(1, MAIN, REST), self.p.zpeer)
        )

    def core(self, slot):
        return self.copies.start(
            self.part(slot, 0, WIDTH), self.part(slot + 2, 0, WIDTH), self.p.cpeer
        )

    def wait(self):
        for op in self.ops:
            op.wait_recv()


def nt_dot(a, b):
    return lax.dot_general(a, b, (((1,), (1,)), ((), ())), preferred_element_type=F32)


def dot(a, b):
    return jnp.dot(a, b, preferred_element_type=F32)


def halves(array):
    high = array.astype(BF)
    return high, (array - high.astype(F32)).astype(BF)


def thirds(array):
    high = array.astype(BF)
    rest = array - high.astype(F32)
    middle = rest.astype(BF)
    return high, middle, (rest - middle.astype(F32)).astype(BF)


def iotas(shape):
    return [lax.broadcasted_iota(jnp.int32, shape, axis) for axis in (0, 1)]


def head_masks(rows):
    lane = lax.broadcasted_iota(jnp.int32, (rows, HEAD_COLUMNS), 1)
    return [(lane >= HEAD_DIM * h) & (lane < HEAD_DIM * (h + 1)) for h in range(4)]


def kernel(
    latents,
    fresh_noise,
    level_index,
    step_sizes,
    time_table,
    embed_in,
    spatial_qkv,
    spatial_out,
    temporal_qkv,
    temporal_out,
    embed_out,
    out,
    in_latents,
    in_noise,
    in_table,
    in_embed,
    in_qkv,
    in_out,
    in_velocity,
    first,
    out_s,
    second,
    lat_own,
    lat_pieces,
    lat_second,
    lat_last,
    last_send,
    mods_own,
    mods_here,
    features,
    features_new,
    embed_six,
    out_three,
    hidden,
    normed,
    lower,
    query,
    kv,
    before,
    after,
    mixes,
    mix_last,
    same_head,
    local,
    send,
    recv,
):
    p = Place()
    copies = Copies(send, recv)
    fetches = [
        pltpu.make_async_copy(src, dst, local.at[i])
        for i, (src, dst) in enumerate(
            (
                (spatial_qkv, in_qkv.at[0]),
                (temporal_qkv, in_qkv.at[1]),
                (spatial_out, in_out.at[0]),
                (temporal_out, in_out.at[1]),
                (latents, in_latents),
                (fresh_noise, in_noise),
                (embed_in, in_embed),
                (embed_out, in_velocity),
                (time_table, in_table),
            )
        )
    ]
    for fetch in fetches:
        fetch.start()
    partners = [p.up(d) for d in (1, 2, 3)]
    partners += [p.ring((p.v + d) % 4, p.w) for d in (1, 3)]
    partners += [p.ring(p.v, (p.w + d) % 4) for d in (1, 3)]
    partners += [p.beside(1), p.beside(7), p.cpeer, p.zcpeer]
    partners += [p.next, p.previous]
    me = (p.q, p.s)
    perhaps = [(q, s) for q in (p.worker, p.holder) for s in range(4)]
    perhaps += [(q, p.s) for q in (p.worker_before, p.holder_after, p.final, p.final_source)]
    greet(partners, perhaps, me)
    a = Stream(p, copies, first, (0, 1152))
    b = Stream(p, copies, out_s, (0, LANES))
    c = Stream(p, copies, second, (0, 1152))
    spread_s = Spread(p, copies, out_s, 0)
    spread_t = Spread(p, copies, second, 768)
    position = p.n

    for fetch in fetches[:4]:
        fetch.wait()
    to, source = iotas((16, 18))
    leading = jnp.where(to == source, 1.0, 0.0).astype(BF)
    rest = jnp.zeros((16, HEAD_COLUMNS), F32)
    blocks = []
    for t in range(2):
        for j in range(4):
            chosen = (source >= 16) & (to == 8 * t + 4 * (source - 16) + j)
            chosen = jnp.where(chosen, 1.0, 0.0).astype(BF)
            block = in_qkv[t, :, j, :] if j < 3 else in_out[t]
            blocks.append(dot(leading, block))
            rest = rest + dot(chosen, block)
    a.place(jnp.concatenate(blocks[:3] + [rest], axis=1).astype(BF))
    a.z()
    pad = jnp.zeros((16, LANES - HEAD_COLUMNS), F32)
    b.place(jnp.concatenate([blocks[3], pad], axis=1).astype(BF))
    b.z()
    c.place(jnp.concatenate(blocks[4:], axis=1).astype(BF))

    for fetch in fetches[4:]:
        fetch.wait()
    sub, lane = iotas((16, 512))
    diagonal = (lane & 15) == sub
    token, lane = iotas((32, 512))
    repeat = jnp.where((lane >> 4) == token, 1.0, 0.0).astype(BF)

    def unflatten(line):
        wide = jnp.where(diagonal, jnp.broadcast_to(line, (16, 512)), 0.0)
        high, middle, low = thirds(wide)
        return nt_dot(high, repeat) + nt_dot(middle, repeat) + nt_dot(low, repeat)

    lines = [in_latents[f : f + 1, :] for f in range(2)] + [in_noise[0, f : f + 1, :] for f in range(2)]
    lat_own[...] = jnp.concatenate([unflatten(line) for line in lines], axis=1)

    def share(pieces):
        own = pieces.at[p.s]
        return [copies.start(own, own, t) for t in (p.cpeer, p.zpeer, p.zcpeer)]

    def whole(pieces):
        parts = [pieces[s, :, 32 * f : 32 * f + 32] for f in range(2) for s in range(4)]
        return jnp.concatenate(parts, axis=1)

    lat_ops = [
        copies.route(lat_own, lat_pieces.at[p.s], (p.worker, s), me)
        for s in (p.s, p.cpeer[1], p.zpeer[1], p.zcpeer[1])
    ]
    last_noise = jnp.concatenate(
        [unflatten(in_noise[1, f : f + 1, :]) for f in range(2)] + [jnp.zeros((16, 64), F32)], axis=1
    )

    levels = [level_index[0, step] for step in range(STEPS)]
    small = jnp.concatenate(
        [in_embed[...], in_velocity[...], in_table[levels[0]], in_table[levels[1]], jnp.zeros((4, WIDTH), F32)],
        axis=0,
    )
    for i, part in enumerate(thirds(small)):
        features[48 * i : 48 * i + 40, :] = part
        features[48 * i + 40 : 48 * i + 48, :] = jnp.zeros((8, WIDTH), BF)
    new = lax.broadcasted_iota(jnp.int32, (1, WIDTH), 1)
    late = new - MAIN
    piece = jnp.where(new < MAIN, new >> 4, late >> 1)
    within = jnp.where(new < MAIN, new & 15, 16 + (late & 1))
    owner = (piece & 48) + ((piece & 3) << 2) + ((piece >> 2) & 3)
    old = owner * 18 + within
    features_new[...] = jnp.zeros((144, WIDTH), F32)

    def reorder(i, carry):
        row = lax.broadcasted_iota(jnp.int32, (128, WIDTH), 0) + i * 128
        move = jnp.where(row == old, 1.0, 0.0).astype(BF)
        features_new[...] += dot(features[:, pl.ds(pl.multiple_of(i * 128, 128), 128)], move)
        return carry

    lax.fori_loop(0, 9, reorder, 0)
    parts = [features_new[48 * i : 48 * i + 16, :] for i in range(3)]
    embed_six[...] = jnp.concatenate([parts[i] for i in (0, 1, 0, 1, 2, 0)], axis=0).astype(BF)
    out_three[...] = jnp.concatenate(
        [features_new[48 * i + 16 : 48 * i + 32, :] for i in range(3)], axis=0
    ).astype(BF)
    mods = features_new[32:36, :] + features_new[80:84, :] + features_new[128:132, :]
    for step in range(STEPS):
        size_line = jnp.full((1, WIDTH), step_sizes[levels[step]], F32)
        lines = [mods[2 * step : 2 * step + 2], size_line, jnp.zeros((5, WIDTH), F32)]
        mods_own[step] = jnp.concatenate(lines, axis=0)
    mods_ops = [
        copies.route(mods_own.at[step], mods_here.at[step], (target, p.s), me)
        for step, target in enumerate((p.worker, p.worker_before))
    ]

    row, column = iotas((HEAD_COLUMNS, HEAD_COLUMNS))
    same = jnp.zeros((HEAD_COLUMNS, HEAD_COLUMNS), F32)
    for h in range(4):
        low, high = HEAD_DIM * h, HEAD_DIM * (h + 1)
        inside = (row >= low) & (row < high) & (column >= low) & (column < high)
        same = jnp.where(inside, 1.0, same)
    same_head[...] = same.astype(BF)

    def embed(lat):
        high, middle, low = (part.astype(F32) for part in thirds(lat))
        stack = jnp.concatenate([high, high, middle, middle, high, low], axis=0)
        hidden[...] = dot(stack.T.astype(BF), embed_six[...])

    def normalise(step, frames=(0, 1)):
        shift, scale = mods_here[step, 0:1, :], 1.0 + mods_here[step, 1:2, :]

        def rows_of(i, carry):
            rows = pl.ds(pl.multiple_of(i * 32, 32), 32)
            h = hidden[rows, :]
            inverse = lax.rsqrt(jnp.mean(h * h, axis=-1, keepdims=True) + 1e-06)
            normed[rows, :] = (h * inverse * scale + shift).astype(BF)
            return carry

        lax.fori_loop(4 * frames[0], 4 * frames[-1] + 4, rows_of, 0)

    def project_kv(weights, half, rows=slice(0, 256)):
        kv[half, rows, :] = dot(normed[rows, :], weights[:, 256:896]).astype(BF)

    def project_query(weights):
        query[...] = dot(normed[...], weights[:, :384])

    def attend_frame(half, frame, mix):
        rows = slice(128 * frame, 128 * frame + 128)
        masks = head_masks(128)
        q = query[rows, :HEAD_COLUMNS].astype(BF).astype(F32)
        both = kv[half, rows, :].astype(F32)
        k = both[:, 32 : 32 + HEAD_COLUMNS].astype(BF)
        v = both[:, 320 : 320 + HEAD_COLUMNS]
        q_heads = jnp.concatenate([jnp.where(m, q, 0.0).astype(BF) for m in masks], axis=0)
        v_heads = jnp.concatenate([jnp.where(m, v, 0.0).astype(BF) for m in masks], axis=0)
        scores = nt_dot(q_heads, k) * INVERSE
        scores = jnp.exp(scores - jnp.max(scores, axis=-1, keepdims=True))
        probs = (scores / jnp.sum(scores, axis=-1, keepdims=True)).astype(BF)
        probs = jnp.concatenate([probs[128 * h : 128 * h + 128] for h in range(4)], axis=1)
        mixed = dot(probs, v_heads)
        mixed = jnp.concatenate([mixed, jnp.zeros((128, LANES - HEAD_COLUMNS), F32)], axis=1)
        mix[rows, :LANES] = mixed.astype(BF)

    def start_mix(mix, frame):
        part = lambda slot: mix.at[pl.ds(128 * frame, 128), pl.ds(LANES * slot, LANES)]
        by_z = copies.start(part(0), part(1), p.zpeer)
        by_core = copies.start(part(0), part(2), p.cpeer)
        return by_z, by_core, part

    def finish_mix(started):
        last = []
        for by_z, _, part in started:
            by_z.wait_recv()
            last.append(copies.start(part(1), part(3), p.cpeer))

        def wait(frame):
            started[frame][1].wait_recv()
            last[frame].wait_recv()

        return wait

    def spatial_out(mix, frame):
        rows = slice(128 * frame, 128 * frame + 128)
        hidden[rows, :] += nt_dot(mix[rows, :], out_s[...])

    def start_halo(half, frame):
        rows = kv.at[half, pl.ds(128 * frame, 128)]
        if frame == 1:
            return copies.start(rows, before.at[half], p.next)
        return copies.start(rows, after.at[half], p.previous)

    def temporal(half, halo, first_place, last_place, prepare):
        prepare()

        def keys_values(ref_value):
            both = ref_value.astype(F32)
            return both[:, 32 : 32 + HEAD_COLUMNS], both[:, 320 : 320 + HEAD_COLUMNS]

        def score(q, k):
            high, low = halves(q * k)
            same_now = same_head[...]
            return (dot(high, same_now) + dot(low, same_now)) * INVERSE

        q0 = query[:128, :HEAD_COLUMNS].astype(BF).astype(F32)
        q1 = query[128:, :HEAD_COLUMNS].astype(BF).astype(F32)
        k0, v0 = keys_values(kv[half, :128])
        k1, v1 = keys_values(kv[half, 128:])
        s00, s01, s10, s11 = score(q0, k0), score(q0, k1), score(q1, k0), score(q1, k1)

        def blend(sa, sb, sc, va, vb, vc):
            top = jnp.maximum(jnp.maximum(sa, sb), sc)
            ea, eb, ec = jnp.exp(sa - top), jnp.exp(sb - top), jnp.exp(sc - top)
            total = ea + eb + ec
            rounded = lambda e: (e / total).astype(BF).astype(F32)
            mixed = rounded(ea) * va + rounded(eb) * vb + rounded(ec) * vc
            return jnp.concatenate([jnp.zeros((128, LANES - HEAD_COLUMNS), F32), mixed], axis=1).astype(BF)

        halo[0].wait_recv()
        ka, va = keys_values(after[half])
        sa = jnp.where(position == last_place, -1e30, score(q1, ka))
        yield 1, blend(s10, s11, sa, v0, v1, va)
        halo[1].wait_recv()
        kb, vb = keys_values(before[half])
        sb = jnp.where(position == first_place, -1e30, score(q0, kb))
        yield 0, blend(sb, s00, s01, vb, v0, v1)

    def velocity(ref, rows):
        def rows_of(i, carry):
            part = pl.ds(pl.multiple_of(i * 32, 32), 32)
            h = ref[part, :]
            h = h * lax.rsqrt(jnp.mean(h * h, axis=-1, keepdims=True) + 1e-06)
            normed[part, :], lower[part, :] = halves(h)
            return carry

        lax.fori_loop(0, rows // 32, rows_of, 0)
        both = nt_dot(out_three[...], normed[:rows, :]) + nt_dot(out_three[...], lower[:rows, :])
        return both[:16] + both[16:32] + both[32:48]

    def selected(j, t):
        target = lax.broadcasted_iota(jnp.int32, (REST, MAIN), 0)
        source = lax.broadcasted_iota(jnp.int32, (REST, MAIN), 1)
        choose = jnp.where(source == 8 * target - 4 * (target % 2) + 8 * t + j, 1.0, 0.0).astype(BF)
        return dot(choose, first[:MAIN, 768:1152])[:, 96:]

    own = pl.multiple_of(p.s * 32, 32)

    def exchange_tokens(mix, last, mixed_frames):
        ops = []
        for frame, mixed in mixed_frames:
            mix[128 * frame : 128 * frame + 128, :LANES] = mixed
            for slot, peer in ((1, p.zpeer), (3, p.zcpeer), (2, p.cpeer)):
                theirs = pl.multiple_of(128 * frame + peer[1] * 32, 32)
                ops.append(
                    copies.start(
                        mix.at[pl.ds(theirs, 32), pl.ds(0, LANES)],
                        last.at[pl.ds(32 * frame, 32), pl.ds(LANES * slot, LANES)],
                        peer,
                    )
                )
            mine = pl.ds(pl.multiple_of(128 * frame + own, 32), 32)
            last[32 * frame : 32 * frame + 32, :LANES] = mix[mine, :LANES]
        return ops

    def move_tokens(last):
        h = jnp.concatenate([hidden[pl.ds(own, 32), :], hidden[pl.ds(own + 128, 32), :]], axis=0)
        hidden[:64, :] = h + nt_dot(last[...], second[:, 768:])
        return velocity(hidden, 64)

    a.v1()
    c.z()
    for op in lat_ops:
        op.wait_recv()
    embed(whole(lat_pieces))
    a.v2()
    a.w_forward(0)
    b.v1()
    for op in mods_ops:
        op.wait_recv()
    normalise(0)
    a.v3()
    b.v2()
    a.w_forward(1, 2)
    b.w_forward(0)
    b.v3()
    a.w_forward(3)
    b.w_forward(1, 2)
    c.v1()
    spread_s.block(0)
    a.end()

    blocks = [selected(j, 0) for j in range(4)]
    pad = jnp.zeros((REST, 96), F32)
    first[MAIN:, :896] = jnp.concatenate(blocks[:3] + [pad[:, :32]], axis=1).astype(BF)
    out_s[MAIN:, :LANES] = jnp.concatenate([blocks[3], pad], axis=1).astype(BF)
    b.w_forward(3)
    spread_s.block(3)
    spread_s.block(1)
    spread_s.rest()
    c.v2()
    c.w_forward(0)
    project_kv(first, 0)
    project_query(first)
    b.end()
    spread_s.block(2)
    c.v3()
    cores_s = [spread_s.core(0)]
    mix = mixes.at[0]
    attend_frame(0, 0, mix)
    started = [start_mix(mix, 0)]
    c.w_forward(1, 2)
    attend_frame(0, 1, mix)
    started.append(start_mix(mix, 1))
    c.w_forward(3)
    spread_s.wait()
    cores_s.append(spread_s.core(1))
    wait_mix = finish_mix(started)
    blocks = [selected(j, 1) for j in range(4)]
    second[MAIN:, :1152] = jnp.concatenate(blocks, axis=1).astype(BF)
    spread_t.block(0)
    for op in cores_s:
        op.wait_recv()
    for frame in range(2):
        wait_mix(frame)
        spatial_out(mix, frame)
    normalise(0)
    c.end()
    project_kv(second, 1)
    halo = [start_halo(1, 0), start_halo(1, 1)]
    spread_t.block(3)
    spread_t.block(1)
    cores_t = []

    def meanwhile():
        spread_t.rest()
        spread_t.block(2)
        cores_t.append(spread_t.core(0))
        project_query(second)

    ops = exchange_tokens(mixes.at[1], mix_last.at[0], temporal(1, halo, 0, 63, meanwhile))
    spread_t.wait()
    cores_t.append(spread_t.core(1))
    for op in ops + cores_t:
        op.wait_recv()
    moved = lat_pieces[p.s, :, :64] - mods_here[0, 2:3, :64] * move_tokens(mix_last.at[0])
    moved = jnp.where(position == 63, lat_pieces[p.s, :, 64:], moved)
    lat_second[p.s] = jnp.concatenate([moved, jnp.zeros((16, 64), F32)], axis=1)
    for op in share(lat_second):
        op.wait_recv()

    embed(whole(lat_second))
    normalise(1)
    project_kv(first, 2)
    project_query(first)
    mix = mixes.at[2]
    started = []
    for frame in range(2):
        attend_frame(2, frame, mix)
        started.append(start_mix(mix, frame))
    wait_mix = finish_mix(started)
    halo = []
    for frame in range(2):
        wait_mix(frame)
        spatial_out(mix, frame)
        normalise(1, (frame,))
        project_kv(second, 3, slice(128 * frame, 128 * frame + 128))
        halo.append(start_halo(3, frame))
    ops = exchange_tokens(
        mixes.at[3], mix_last.at[1], temporal(3, halo, 63, 62, lambda: project_query(second))
    )
    for op in ops:
        op.wait_recv()
    moved = lat_second[p.s, :, :64] - mods_here[1, 2:3, :64] * move_tokens(mix_last.at[1])
    last_send[...] = jnp.concatenate([moved, jnp.zeros((16, 64), F32)], axis=1)
    shifted = copies.route(last_send, lat_last, (p.final, p.s), me)
    shifted.wait_recv()
    final = jnp.where(p.q == 0, last_noise, lat_last[...])
    for f in range(2):
        high, middle, low = thirds(final[:, 32 * f : 32 * f + 32])
        wide = dot(high, repeat) + dot(middle, repeat) + dot(low, repeat)
        out[f : f + 1, :] = jnp.sum(jnp.where(diagonal, wide, 0.0), axis=0, keepdims=True)
    copies.drain()


def per_device(*operands):
    operands = [operand.T if i in (7, 9, 10) else operand for i, operand in enumerate(operands)]
    smem, whole = pl.BlockSpec(memory_space=pltpu.SMEM), pl.BlockSpec(memory_space=pl.ANY)
    specs = [smem if i in (2, 3) else whole for i in range(len(operands))]
    return pl.pallas_call(
        kernel,
        out_shape=jax.ShapeDtypeStruct((2, 512), F32),
        in_specs=specs,
        out_specs=pl.BlockSpec(memory_space=pltpu.VMEM),
        scratch_shapes=[
            pltpu.VMEM((2, 512), F32),
            pltpu.VMEM((2, 2, 512), F32),
            pltpu.VMEM((30, 2, WIDTH), F32),
            pltpu.VMEM((16, WIDTH), F32),
            pltpu.VMEM((2, 18, 3, HEAD_COLUMNS), BF),
            pltpu.VMEM((2, 18, HEAD_COLUMNS), BF),
            pltpu.VMEM((16, WIDTH), F32),
            pltpu.VMEM((WIDTH, 1152), BF),
            pltpu.VMEM((WIDTH, 4 * LANES), BF),
            pltpu.VMEM((WIDTH, 768 + 4 * LANES), BF),
            pltpu.VMEM((16, 128), F32),
            pltpu.VMEM((4, 16, 128), F32),
            pltpu.VMEM((4, 16, 128), F32),
            pltpu.VMEM((16, 128), F32),
            pltpu.VMEM((16, 128), F32),
            pltpu.VMEM((2, 8, WIDTH), F32),
            pltpu.VMEM((2, 8, WIDTH), F32),
            pltpu.VMEM((144, WIDTH), BF),
            pltpu.VMEM((144, WIDTH), F32),
            pltpu.VMEM((96, WIDTH), BF),
            pltpu.VMEM((48, WIDTH), BF),
            pltpu.VMEM((256, WIDTH), F32),
            pltpu.VMEM((256, WIDTH), BF),
            pltpu.VMEM((256, WIDTH), BF),
            pltpu.VMEM((256, LANES), F32),
            pltpu.VMEM((4, 256, 640), BF),
            pltpu.VMEM((4, 128, 640), BF),
            pltpu.VMEM((4, 128, 640), BF),
            pltpu.VMEM((4, 256, 4 * LANES), BF),
            pltpu.VMEM((2, 64, 4 * LANES), BF),
            pltpu.VMEM((HEAD_COLUMNS, HEAD_COLUMNS), BF),
            pltpu.SemaphoreType.DMA((9,)),
            pltpu.SemaphoreType.DMA((COPIES,)),
            pltpu.SemaphoreType.DMA((COPIES,)),
        ],
        compiler_params=pltpu.CompilerParams(
            collective_id=0, has_side_effects=True, vmem_limit_bytes=56 * 2**20
        ),
        name="denoise",
    )(*operands)


def solution(mesh):
    placed = (
        P("queue", "space"),
        P(None, None, "space"),
        P("queue", None),
        P(),
        P(),
        P(),
        P("queue", None, "space"),
        P("space", "queue"),
        P("queue", None, "space"),
        P("space", "queue"),
        P(),
    )
    return jax.shard_map(
        per_device, mesh=mesh, in_specs=placed, out_specs=P("queue", "space"), check_vma=False
    )
```

```python
import functools

import jax
import jax.numpy as jnp
from jax import lax
from jax.experimental import pallas as pl
from jax.experimental.pallas import tpu as pltpu
from jax.sharding import PartitionSpec as P

STEPS = 2
BF = jnp.bfloat16
F32 = jnp.float32


MESH = pl.DeviceIdType.MESH
MAIN, REST = 1024, 128
WIDTH = MAIN + REST
HEAD_COLUMNS = 288
HEAD_DIM = 72
INVERSE = 1.0 / HEAD_DIM**0.5
LANES = 384
COPIES = 160


def device_of(n):
    n = (n + 2) % 64
    r, j = n // 4, n % 4
    x, i = r // 4, r % 4
    zh = i + (x % 2) * (3 - 2 * i)
    y = j + (r % 2) * (3 - 2 * j)
    return (x * 4 + zh) * 4 + y


def span_of(x, zh, y):
    r = x * 4 + zh + (x % 2) * (3 - 2 * zh)
    return (r * 4 + y + (r % 2) * (3 - 2 * y) + 62) % 64


class Place:
    def __init__(self):
        q, s = lax.axis_index("queue"), lax.axis_index("space")
        self.q, self.s = q, s
        self.x, self.zh, self.y = q // 16, (q // 4) % 4, q % 4
        self.zl, self.c = s // 2, s % 2
        self.v = (1 - self.c) * self.y + self.c * self.x
        self.w = (1 - self.c) * self.x + self.c * self.y
        self.zpeer = (q, (1 - self.zl) * 2 + self.c)
        self.cpeer = (q, self.zl * 2 + 1 - self.c)
        self.zcpeer = (q, (1 - self.zl) * 2 + 1 - self.c)
        self.n = span_of(self.x, self.zh, self.y)
        self.next = (device_of(self.n + 1), s)
        self.previous = (device_of(self.n + 63), s)
        self.worker, self.holder = device_of(q), self.n
        self.worker_before, self.holder_after = device_of(q + 63), (self.n + 1) % 64
        self.final, self.final_source = (self.n + 2) % 64, device_of(q + 62)

    def cell(self, v, w):
        x = self.c * v + (1 - self.c) * w
        y = (1 - self.c) * v + self.c * w
        return x * 4 + y

    def ring(self, v, w):
        x = self.c * v + (1 - self.c) * w
        y = (1 - self.c) * v + self.c * w
        return ((x * 4 + self.zh) * 4 + y, self.s)

    def up(self, dz):
        return ((self.x * 4 + (self.zh + dz) % 4) * 4 + self.y, self.s)

    def beside(self, dz):
        z = (self.zh * 2 + self.zl + dz) % 8
        return ((self.x * 4 + z // 2) * 4 + self.y, (z % 2) * 2 + self.c)


class Copies:
    def __init__(self, send, recv):
        self.send, self.recv, self.started = send, recv, []

    def start(self, src, dst, target):
        i = len(self.started)
        assert i < COPIES
        op = pltpu.make_async_remote_copy(
            src_ref=src,
            dst_ref=dst,
            send_sem=self.send.at[i],
            recv_sem=self.recv.at[i],
            device_id=target,
            device_id_type=MESH,
        )
        op.start()
        self.started.append(op)
        return op

    def route(self, src, dst, target, me):
        same = (target[0] == me[0]) & (target[1] == me[1])
        op = Routed(src, dst, same)
        i = len(self.started)
        op.remote = pltpu.make_async_remote_copy(
            src_ref=src,
            dst_ref=dst,
            send_sem=self.send.at[i],
            recv_sem=self.recv.at[i],
            device_id=target,
            device_id_type=MESH,
        )
        pl.when(jnp.logical_not(same))(op.remote.start)
        pl.when(same)(op.keep)
        self.started.append(op)
        return op

    def drain(self):
        for op in self.started:
            op.wait_send()


class Routed:
    def __init__(self, src, dst, same):
        self.src, self.dst, self.same = src, dst, same

    def keep(self):
        self.dst[...] = self.src[...]

    def wait_recv(self):
        pl.when(jnp.logical_not(self.same))(self.remote.wait_recv)

    def wait_send(self):
        pl.when(jnp.logical_not(self.same))(self.remote.wait_send)


def greet(partners, perhaps, me):
    barrier = pltpu.get_barrier_semaphore()
    count = len(partners)
    for partner in partners:
        pl.semaphore_signal(barrier, inc=1, device_id=partner, device_id_type=MESH)
    for partner in perhaps:
        other = (partner[0] != me[0]) | (partner[1] != me[1])

        @pl.when(other)
        def _():
            pl.semaphore_signal(barrier, inc=1, device_id=partner, device_id_type=MESH)

        count = count + jnp.where(other, 1, 0)
    pl.semaphore_wait(barrier, count)


class Stream:
    def __init__(self, place, copies, buf, columns):
        self.p, self.copies, self.buf, self.columns = place, copies, buf, columns
        self.ops = {}

    def copy(self, key, rows, count, target):
        part = self.buf.at[pl.ds(pl.multiple_of(rows, 16), count), pl.ds(*self.columns)]
        self.ops[key] = self.copies.start(part, part, target)

    def place(self, piece):
        p = self.p
        self.row = pl.multiple_of((p.cell(p.v, p.w) * 4 + p.zh) * 16, 16)
        self.buf[pl.ds(self.row, 16), pl.ds(*self.columns)] = piece

    def z(self):
        for d in (1, 3, 2):
            self.copy(("z", d), self.row, 16, self.p.up(d))

    def both(self, key, v, w, right, left):
        rows = self.p.cell(v, w) * 64
        self.copy((key, "R"), rows, 64, right)
        self.copy((key, "L"), rows, 64, left)

    def w_sends(self, k):
        p = self.p
        v = (p.v + (0, 3, 1, 2)[k]) % 4
        self.both(("w", k), v, p.w, p.ring(p.v, (p.w + 1) % 4), p.ring(p.v, (p.w + 3) % 4))

    def v1(self):
        p = self.p
        for d in (1, 3, 2):
            self.ops["z", d].wait_recv()
        self.both("v", p.v, p.w, p.ring((p.v + 1) % 4, p.w), p.ring((p.v + 3) % 4, p.w))
        self.w_sends(0)

    def v2(self):
        p = self.p
        self.ops["v", "R"].wait_recv()
        self.copy("vfR", p.cell((p.v + 3) % 4, p.w) * 64, 32, p.ring((p.v + 1) % 4, p.w))
        self.w_sends(1)
        self.ops["v", "L"].wait_recv()
        self.copy("vfL", p.cell((p.v + 1) % 4, p.w) * 64 + 32, 32, p.ring((p.v + 3) % 4, p.w))
        self.w_sends(2)

    def w_forward(self, *blocks):
        p = self.p
        for k in blocks:
            v = (p.v + (0, 3, 1, 2)[k]) % 4
            self.ops[("w", k), "R"].wait_recv()
            self.copy(("wfR", k), p.cell(v, (p.w + 3) % 4) * 64, 32, p.ring(p.v, (p.w + 1) % 4))
            self.ops[("w", k), "L"].wait_recv()
            self.copy(("wfL", k), p.cell(v, (p.w + 1) % 4) * 64 + 32, 32, p.ring(p.v, (p.w + 3) % 4))

    def v3(self):
        self.ops["vfR"].wait_recv()
        self.ops["vfL"].wait_recv()
        self.w_sends(3)

    def end(self):
        for k in range(4):
            self.ops["wfR", k].wait_recv()
            self.ops["wfL", k].wait_recv()


class Spread:
    def __init__(self, place, copies, buf, first):
        self.p, self.copies, self.buf, self.first = place, copies, buf, first
        self.ops = []

    def part(self, slot, rows, count):
        return self.buf.at[pl.ds(pl.multiple_of(rows, 16), count), pl.ds(self.first + LANES * slot, LANES)]

    def block(self, dw):
        p = self.p
        for v in range(4):
            rows = p.cell(v, (p.w + dw) % 4) * 64
            to = p.beside(1 if v < 2 else 7)
            self.ops.append(self.copies.start(self.part(0, rows, 64), self.part(1, rows, 64), to))

    def rest(self):
        self.ops.append(
            self.copies.start(self.part(0, MAIN, REST), self.part(1, MAIN, REST), self.p.zpeer)
        )

    def core(self, slot):
        return self.copies.start(
            self.part(slot, 0, WIDTH), self.part(slot + 2, 0, WIDTH), self.p.cpeer
        )

    def wait(self):
        for op in self.ops:
            op.wait_recv()


def nt_dot(a, b):
    return lax.dot_general(a, b, (((1,), (1,)), ((), ())), preferred_element_type=F32)


def dot(a, b):
    return jnp.dot(a, b, preferred_element_type=F32)


def halves(array):
    high = array.astype(BF)
    return high, (array - high.astype(F32)).astype(BF)


def thirds(array):
    high = array.astype(BF)
    rest = array - high.astype(F32)
    middle = rest.astype(BF)
    return high, middle, (rest - middle.astype(F32)).astype(BF)


def iotas(shape):
    return [lax.broadcasted_iota(jnp.int32, shape, axis) for axis in (0, 1)]


def head_masks(rows):
    lane = lax.broadcasted_iota(jnp.int32, (rows, HEAD_COLUMNS), 1)
    return [(lane >= HEAD_DIM * h) & (lane < HEAD_DIM * (h + 1)) for h in range(4)]


def kernel(
    latents,
    fresh_noise,
    level_index,
    step_sizes,
    time_table,
    embed_in,
    spatial_qkv,
    spatial_out,
    temporal_qkv,
    temporal_out,
    embed_out,
    out,
    in_latents,
    in_noise,
    in_table,
    in_embed,
    in_qkv,
    in_out,
    in_velocity,
    first,
    out_s,
    second,
    lat_own,
    lat_pieces,
    lat_second,
    lat_last,
    last_send,
    mods_own,
    mods_here,
    features,
    features_new,
    embed_six,
    out_three,
    hidden,
    normed,
    lower,
    query,
    kv,
    before,
    after,
    mixes,
    mix_last,
    same_head,
    local,
    send,
    recv,
):
    p = Place()
    copies = Copies(send, recv)
    fetches = [
        pltpu.make_async_copy(src, dst, local.at[i])
        for i, (src, dst) in enumerate(
            (
                (spatial_qkv, in_qkv.at[0]),
                (temporal_qkv, in_qkv.at[1]),
                (spatial_out, in_out.at[0]),
                (temporal_out, in_out.at[1]),
                (latents, in_latents),
                (fresh_noise, in_noise),
                (embed_in, in_embed),
                (embed_out, in_velocity),
                (time_table, in_table),
            )
        )
    ]
    for fetch in fetches:
        fetch.start()
    partners = [p.up(d) for d in (1, 2, 3)]
    partners += [p.ring((p.v + d) % 4, p.w) for d in (1, 3)]
    partners += [p.ring(p.v, (p.w + d) % 4) for d in (1, 3)]
    partners += [p.beside(1), p.beside(7), p.cpeer, p.zcpeer]
    partners += [p.next, p.previous]
    me = (p.q, p.s)
    perhaps = [(q, s) for q in (p.worker, p.holder) for s in range(4)]
    perhaps += [(q, p.s) for q in (p.worker_before, p.holder_after, p.final, p.final_source)]
    greet(partners, perhaps, me)
    a = Stream(p, copies, first, (0, 1152))
    b = Stream(p, copies, out_s, (0, LANES))
    c = Stream(p, copies, second, (0, 1152))
    spread_s = Spread(p, copies, out_s, 0)
    spread_t = Spread(p, copies, second, 768)
    position = p.n

    for fetch in fetches[:4]:
        fetch.wait()
    to, source = iotas((16, 18))
    leading = jnp.where(to == source, 1.0, 0.0).astype(BF)
    rest = jnp.zeros((16, HEAD_COLUMNS), F32)
    blocks = []
    for t in range(2):
        for j in range(4):
            chosen = (source >= 16) & (to == 8 * t + 4 * (source - 16) + j)
            chosen = jnp.where(chosen, 1.0, 0.0).astype(BF)
            block = in_qkv[t, :, j, :] if j < 3 else in_out[t]
            blocks.append(dot(leading, block))
            rest = rest + dot(chosen, block)
    a.place(jnp.concatenate(blocks[:3] + [rest], axis=1).astype(BF))
    a.z()
    pad = jnp.zeros((16, LANES - HEAD_COLUMNS), F32)
    b.place(jnp.concatenate([blocks[3], pad], axis=1).astype(BF))
    b.z()
    c.place(jnp.concatenate(blocks[4:], axis=1).astype(BF))

    for fetch in fetches[4:]:
        fetch.wait()
    sub, lane = iotas((16, 512))
    diagonal = (lane & 15) == sub
    token, lane = iotas((32, 512))
    repeat = jnp.where((lane >> 4) == token, 1.0, 0.0).astype(BF)

    def unflatten(line):
        wide = jnp.where(diagonal, jnp.broadcast_to(line, (16, 512)), 0.0)
        high, middle, low = thirds(wide)
        return nt_dot(high, repeat) + nt_dot(middle, repeat) + nt_dot(low, repeat)

    lines = [in_latents[f : f + 1, :] for f in range(2)] + [in_noise[0, f : f + 1, :] for f in range(2)]
    lat_own[...] = jnp.concatenate([unflatten(line) for line in lines], axis=1)

    def share(pieces):
        own = pieces.at[p.s]
        return [copies.start(own, own, t) for t in (p.cpeer, p.zpeer, p.zcpeer)]

    def whole(pieces):
        parts = [pieces[s, :, 32 * f : 32 * f + 32] for f in range(2) for s in range(4)]
        return jnp.concatenate(parts, axis=1)

    lat_ops = [
        copies.route(lat_own, lat_pieces.at[p.s], (p.worker, s), me)
        for s in (p.s, p.cpeer[1], p.zpeer[1], p.zcpeer[1])
    ]
    last_noise = jnp.concatenate(
        [unflatten(in_noise[1, f : f + 1, :]) for f in range(2)] + [jnp.zeros((16, 64), F32)], axis=1
    )

    levels = [level_index[0, step] for step in range(STEPS)]
    small = jnp.concatenate(
        [in_embed[...], in_velocity[...], in_table[levels[0]], in_table[levels[1]], jnp.zeros((4, WIDTH), F32)],
        axis=0,
    )
    for i, part in enumerate(thirds(small)):
        features[48 * i : 48 * i + 40, :] = part
        features[48 * i + 40 : 48 * i + 48, :] = jnp.zeros((8, WIDTH), BF)
    new = lax.broadcasted_iota(jnp.int32, (1, WIDTH), 1)
    late = new - MAIN
    piece = jnp.where(new < MAIN, new >> 4, late >> 1)
    within = jnp.where(new < MAIN, new & 15, 16 + (late & 1))
    owner = (piece & 48) + ((piece & 3) << 2) + ((piece >> 2) & 3)
    old = owner * 18 + within
    features_new[...] = jnp.zeros((144, WIDTH), F32)

    def reorder(i, carry):
        row = lax.broadcasted_iota(jnp.int32, (128, WIDTH), 0) + i * 128
        move = jnp.where(row == old, 1.0, 0.0).astype(BF)
        features_new[...] += dot(features[:, pl.ds(pl.multiple_of(i * 128, 128), 128)], move)
        return carry

    lax.fori_loop(0, 9, reorder, 0)
    parts = [features_new[48 * i : 48 * i + 16, :] for i in range(3)]
    embed_six[...] = jnp.concatenate([parts[i] for i in (0, 1, 0, 1, 2, 0)], axis=0).astype(BF)
    out_three[...] = jnp.concatenate(
        [features_new[48 * i + 16 : 48 * i + 32, :] for i in range(3)], axis=0
    ).astype(BF)
    mods = features_new[32:36, :] + features_new[80:84, :] + features_new[128:132, :]
    for step in range(STEPS):
        size_line = jnp.full((1, WIDTH), step_sizes[levels[step]], F32)
        lines = [mods[2 * step : 2 * step + 2], size_line, jnp.zeros((5, WIDTH), F32)]
        mods_own[step] = jnp.concatenate(lines, axis=0)
    mods_ops = [
        copies.route(mods_own.at[step], mods_here.at[step], (target, p.s), me)
        for step, target in enumerate((p.worker, p.worker_before))
    ]

    row, column = iotas((HEAD_COLUMNS, HEAD_COLUMNS))
    same = jnp.zeros((HEAD_COLUMNS, HEAD_COLUMNS), F32)
    for h in range(4):
        low, high = HEAD_DIM * h, HEAD_DIM * (h + 1)
        inside = (row >= low) & (row < high) & (column >= low) & (column < high)
        same = jnp.where(inside, 1.0, same)
    same_head[...] = same.astype(BF)

    def embed(lat):
        high, middle, low = (part.astype(F32) for part in thirds(lat))
        stack = jnp.concatenate([high, high, middle, middle, high, low], axis=0)
        hidden[...] = dot(stack.T.astype(BF), embed_six[...])

    def normalise(step, frames=(0, 1)):
        shift, scale = mods_here[step, 0:1, :], 1.0 + mods_here[step, 1:2, :]

        def rows_of(i, carry):
            rows = pl.ds(pl.multiple_of(i * 32, 32), 32)
            h = hidden[rows, :]
            inverse = lax.rsqrt(jnp.mean(h * h, axis=-1, keepdims=True) + 1e-06)
            normed[rows, :] = (h * inverse * scale + shift).astype(BF)
            return carry

        lax.fori_loop(4 * frames[0], 4 * frames[-1] + 4, rows_of, 0)

    def project_kv(weights, half, rows=slice(0, 256)):
        kv[half, rows, :] = dot(normed[rows, :], weights[:, 256:896]).astype(BF)

    def project_query(weights):
        query[...] = dot(normed[...], weights[:, :384])

    def attend_frame(half, frame, mix):
        rows = slice(128 * frame, 128 * frame + 128)
        masks = head_masks(128)
        q = query[rows, :HEAD_COLUMNS].astype(BF).astype(F32)
        both = kv[half, rows, :].astype(F32)
        k = both[:, 32 : 32 + HEAD_COLUMNS].astype(BF)
        v = both[:, 320 : 320 + HEAD_COLUMNS]
        q_heads = jnp.concatenate([jnp.where(m, q, 0.0).astype(BF) for m in masks], axis=0)
        v_heads = jnp.concatenate([jnp.where(m, v, 0.0).astype(BF) for m in masks], axis=0)
        scores = nt_dot(q_heads, k) * INVERSE
        scores = jnp.exp(scores - jnp.max(scores, axis=-1, keepdims=True))
        probs = (scores / jnp.sum(scores, axis=-1, keepdims=True)).astype(BF)
        probs = jnp.concatenate([probs[128 * h : 128 * h + 128] for h in range(4)], axis=1)
        mixed = dot(probs, v_heads)
        mixed = jnp.concatenate([mixed, jnp.zeros((128, LANES - HEAD_COLUMNS), F32)], axis=1)
        mix[rows, :LANES] = mixed.astype(BF)

    def start_mix(mix, frame):
        part = lambda slot: mix.at[pl.ds(128 * frame, 128), pl.ds(LANES * slot, LANES)]
        by_z = copies.start(part(0), part(1), p.zpeer)
        by_core = copies.start(part(0), part(2), p.cpeer)
        return by_z, by_core, part

    def finish_mix(started):
        last = []
        for by_z, _, part in started:
            by_z.wait_recv()
            last.append(copies.start(part(1), part(3), p.cpeer))

        def wait(frame):
            started[frame][1].wait_recv()
            last[frame].wait_recv()

        return wait

    def spatial_out(mix, frame):
        rows = slice(128 * frame, 128 * frame + 128)
        hidden[rows, :] += nt_dot(mix[rows, :], out_s[...])

    def start_halo(half, frame):
        rows = kv.at[half, pl.ds(128 * frame, 128)]
        if frame == 1:
            return copies.start(rows, before.at[half], p.next)
        return copies.start(rows, after.at[half], p.previous)

    def temporal(half, halo, first_place, last_place, prepare):
        prepare()

        def keys_values(ref_value):
            both = ref_value.astype(F32)
            return both[:, 32 : 32 + HEAD_COLUMNS], both[:, 320 : 320 + HEAD_COLUMNS]

        def score(q, k):
            high, low = halves(q * k)
            same_now = same_head[...]
            return (dot(high, same_now) + dot(low, same_now)) * INVERSE

        q0 = query[:128, :HEAD_COLUMNS].astype(BF).astype(F32)
        q1 = query[128:, :HEAD_COLUMNS].astype(BF).astype(F32)
        k0, v0 = keys_values(kv[half, :128])
        k1, v1 = keys_values(kv[half, 128:])
        s00, s01, s10, s11 = score(q0, k0), score(q0, k1), score(q1, k0), score(q1, k1)

        def blend(sa, sb, sc, va, vb, vc):
            top = jnp.maximum(jnp.maximum(sa, sb), sc)
            ea, eb, ec = jnp.exp(sa - top), jnp.exp(sb - top), jnp.exp(sc - top)
            total = ea + eb + ec
            rounded = lambda e: (e / total).astype(BF).astype(F32)
            mixed = rounded(ea) * va + rounded(eb) * vb + rounded(ec) * vc
            return jnp.concatenate([jnp.zeros((128, LANES - HEAD_COLUMNS), F32), mixed], axis=1).astype(BF)

        halo[0].wait_recv()
        ka, va = keys_values(after[half])
        sa = jnp.where(position == last_place, -1e30, score(q1, ka))
        yield 1, blend(s10, s11, sa, v0, v1, va)
        halo[1].wait_recv()
        kb, vb = keys_values(before[half])
        sb = jnp.where(position == first_place, -1e30, score(q0, kb))
        yield 0, blend(sb, s00, s01, vb, v0, v1)

    def velocity(ref, rows):
        def rows_of(i, carry):
            part = pl.ds(pl.multiple_of(i * 32, 32), 32)
            h = ref[part, :]
            h = h * lax.rsqrt(jnp.mean(h * h, axis=-1, keepdims=True) + 1e-06)
            normed[part, :], lower[part, :] = halves(h)
            return carry

        lax.fori_loop(0, rows // 32, rows_of, 0)
        both = nt_dot(out_three[...], normed[:rows, :]) + nt_dot(out_three[...], lower[:rows, :])
        return both[:16] + both[16:32] + both[32:48]

    def selected(j, t):
        target = lax.broadcasted_iota(jnp.int32, (REST, MAIN), 0)
        source = lax.broadcasted_iota(jnp.int32, (REST, MAIN), 1)
        choose = jnp.where(source == 8 * target - 4 * (target % 2) + 8 * t + j, 1.0, 0.0).astype(BF)
        return dot(choose, first[:MAIN, 768:1152])[:, 96:]

    own = pl.multiple_of(p.s * 32, 32)

    def exchange_tokens(mix, last, mixed_frames):
        ops = []
        for frame, mixed in mixed_frames:
            mix[128 * frame : 128 * frame + 128, :LANES] = mixed
            for slot, peer in ((1, p.zpeer), (3, p.zcpeer), (2, p.cpeer)):
                theirs = pl.multiple_of(128 * frame + peer[1] * 32, 32)
                ops.append(
                    copies.start(
                        mix.at[pl.ds(theirs, 32), pl.ds(0, LANES)],
                        last.at[pl.ds(32 * frame, 32), pl.ds(LANES * slot, LANES)],
                        peer,
                    )
                )
            mine = pl.ds(pl.multiple_of(128 * frame + own, 32), 32)
            last[32 * frame : 32 * frame + 32, :LANES] = mix[mine, :LANES]
        return ops

    def move_tokens(last):
        h = jnp.concatenate([hidden[pl.ds(own, 32), :], hidden[pl.ds(own + 128, 32), :]], axis=0)
        hidden[:64, :] = h + nt_dot(last[...], second[:, 768:])
        return velocity(hidden, 64)

    a.v1()
    c.z()
    for op in lat_ops:
        op.wait_recv()
    embed(whole(lat_pieces))
    a.v2()
    a.w_forward(0)
    b.v1()
    for op in mods_ops:
        op.wait_recv()
    normalise(0)
    a.v3()
    b.v2()
    a.w_forward(1, 2)
    b.w_forward(0)
    b.v3()
    a.w_forward(3)
    b.w_forward(1, 2)
    c.v1()
    spread_s.block(0)
    a.end()

    blocks = [selected(j, 0) for j in range(4)]
    pad = jnp.zeros((REST, 96), F32)
    first[MAIN:, :896] = jnp.concatenate(blocks[:3] + [pad[:, :32]], axis=1).astype(BF)
    out_s[MAIN:, :LANES] = jnp.concatenate([blocks[3], pad], axis=1).astype(BF)
    b.w_forward(3)
    spread_s.block(3)
    spread_s.block(1)
    spread_s.rest()
    c.v2()
    c.w_forward(0)
    project_kv(first, 0)
    project_query(first)
    b.end()
    spread_s.block(2)
    c.v3()
    cores_s = [spread_s.core(0)]
    mix = mixes.at[0]
    attend_frame(0, 0, mix)
    started = [start_mix(mix, 0)]
    c.w_forward(1, 2)
    attend_frame(0, 1, mix)
    started.append(start_mix(mix, 1))
    c.w_forward(3)
    spread_t.block(0)
    spread_t.block(3)
    spread_t.block(1)
    spread_s.wait()
    cores_s.append(spread_s.core(1))
    wait_mix = finish_mix(started)
    blocks = [selected(j, 1) for j in range(4)]
    second[MAIN:, :1152] = jnp.concatenate(blocks, axis=1).astype(BF)
    for op in cores_s:
        op.wait_recv()
    halo = []
    for frame in range(2):
        wait_mix(frame)
        spatial_out(mix, frame)
        normalise(0, (frame,))
        if frame == 0:
            c.end()
        project_kv(second, 1, slice(128 * frame, 128 * frame + 128))
        halo.append(start_halo(1, frame))
    cores_t = []

    def meanwhile():
        spread_t.rest()
        spread_t.block(2)
        cores_t.append(spread_t.core(0))
        project_query(second)

    ops = exchange_tokens(mixes.at[1], mix_last.at[0], temporal(1, halo, 0, 63, meanwhile))
    spread_t.wait()
    cores_t.append(spread_t.core(1))
    for op in ops + cores_t:
        op.wait_recv()
    moved = lat_pieces[p.s, :, :64] - mods_here[0, 2:3, :64] * move_tokens(mix_last.at[0])
    moved = jnp.where(position == 63, lat_pieces[p.s, :, 64:], moved)
    lat_second[p.s] = jnp.concatenate([moved, jnp.zeros((16, 64), F32)], axis=1)
    for op in share(lat_second):
        op.wait_recv()

    embed(whole(lat_second))
    normalise(1)
    project_kv(first, 2)
    project_query(first)
    mix = mixes.at[2]
    started = []
    for frame in range(2):
        attend_frame(2, frame, mix)
        started.append(start_mix(mix, frame))
    wait_mix = finish_mix(started)
    halo = []
    for frame in range(2):
        wait_mix(frame)
        spatial_out(mix, frame)
        normalise(1, (frame,))
        project_kv(second, 3, slice(128 * frame, 128 * frame + 128))
        halo.append(start_halo(3, frame))
    ops = exchange_tokens(
        mixes.at[3], mix_last.at[1], temporal(3, halo, 63, 62, lambda: project_query(second))
    )
    for op in ops:
        op.wait_recv()
    moved = lat_second[p.s, :, :64] - mods_here[1, 2:3, :64] * move_tokens(mix_last.at[1])
    last_send[...] = jnp.concatenate([moved, jnp.zeros((16, 64), F32)], axis=1)
    shifted = copies.route(last_send, lat_last, (p.final, p.s), me)
    shifted.wait_recv()
    final = jnp.where(p.q == 0, last_noise, lat_last[...])
    for f in range(2):
        high, middle, low = thirds(final[:, 32 * f : 32 * f + 32])
        wide = dot(high, repeat) + dot(middle, repeat) + dot(low, repeat)
        out[f : f + 1, :] = jnp.sum(jnp.where(diagonal, wide, 0.0), axis=0, keepdims=True)
    copies.drain()


def per_device(*operands):
    operands = [operand.T if i in (7, 9, 10) else operand for i, operand in enumerate(operands)]
    smem, whole = pl.BlockSpec(memory_space=pltpu.SMEM), pl.BlockSpec(memory_space=pl.ANY)
    specs = [smem if i in (2, 3) else whole for i in range(len(operands))]
    return pl.pallas_call(
        kernel,
        out_shape=jax.ShapeDtypeStruct((2, 512), F32),
        in_specs=specs,
        out_specs=pl.BlockSpec(memory_space=pltpu.VMEM),
        scratch_shapes=[
            pltpu.VMEM((2, 512), F32),
            pltpu.VMEM((2, 2, 512), F32),
            pltpu.VMEM((30, 2, WIDTH), F32),
            pltpu.VMEM((16, WIDTH), F32),
            pltpu.VMEM((2, 18, 3, HEAD_COLUMNS), BF),
            pltpu.VMEM((2, 18, HEAD_COLUMNS), BF),
            pltpu.VMEM((16, WIDTH), F32),
            pltpu.VMEM((WIDTH, 1152), BF),
            pltpu.VMEM((WIDTH, 4 * LANES), BF),
            pltpu.VMEM((WIDTH, 768 + 4 * LANES), BF),
            pltpu.VMEM((16, 128), F32),
            pltpu.VMEM((4, 16, 128), F32),
            pltpu.VMEM((4, 16, 128), F32),
            pltpu.VMEM((16, 128), F32),
            pltpu.VMEM((16, 128), F32),
            pltpu.VMEM((2, 8, WIDTH), F32),
            pltpu.VMEM((2, 8, WIDTH), F32),
            pltpu.VMEM((144, WIDTH), BF),
            pltpu.VMEM((144, WIDTH), F32),
            pltpu.VMEM((96, WIDTH), BF),
            pltpu.VMEM((48, WIDTH), BF),
            pltpu.VMEM((256, WIDTH), F32),
            pltpu.VMEM((256, WIDTH), BF),
            pltpu.VMEM((256, WIDTH), BF),
            pltpu.VMEM((256, LANES), F32),
            pltpu.VMEM((4, 256, 640), BF),
            pltpu.VMEM((4, 128, 640), BF),
            pltpu.VMEM((4, 128, 640), BF),
            pltpu.VMEM((4, 256, 4 * LANES), BF),
            pltpu.VMEM((2, 64, 4 * LANES), BF),
            pltpu.VMEM((HEAD_COLUMNS, HEAD_COLUMNS), BF),
            pltpu.SemaphoreType.DMA((9,)),
            pltpu.SemaphoreType.DMA((COPIES,)),
            pltpu.SemaphoreType.DMA((COPIES,)),
        ],
        compiler_params=pltpu.CompilerParams(
            collective_id=0, has_side_effects=True, vmem_limit_bytes=56 * 2**20
        ),
        name="denoise",
    )(*operands)


def solution(mesh):
    placed = (
        P("queue", "space"),
        P(None, None, "space"),
        P("queue", None),
        P(),
        P(),
        P(),
        P("queue", None, "space"),
        P("space", "queue"),
        P("queue", None, "space"),
        P("space", "queue"),
        P(),
    )
    return jax.shard_map(
        per_device, mesh=mesh, in_specs=placed, out_specs=P("queue", "space"), check_vma=False
    )
```

```python
import functools

import jax
import jax.numpy as jnp
from jax import lax
from jax.experimental import pallas as pl
from jax.experimental.pallas import tpu as pltpu
from jax.sharding import PartitionSpec as P

STEPS = 2
BF = jnp.bfloat16
F32 = jnp.float32


MESH = pl.DeviceIdType.MESH
MAIN, REST = 1024, 128
WIDTH = MAIN + REST
HEAD_COLUMNS = 288
HEAD_DIM = 72
INVERSE = 1.0 / HEAD_DIM**0.5
LANES = 384
COPIES = 160


def device_of(n):
    n = (n + 2) % 64
    r, j = n // 4, n % 4
    x, i = r // 4, r % 4
    zh = i + (x % 2) * (3 - 2 * i)
    y = j + (r % 2) * (3 - 2 * j)
    return (x * 4 + zh) * 4 + y


def span_of(x, zh, y):
    r = x * 4 + zh + (x % 2) * (3 - 2 * zh)
    return (r * 4 + y + (r % 2) * (3 - 2 * y) + 62) % 64


class Place:
    def __init__(self):
        q, s = lax.axis_index("queue"), lax.axis_index("space")
        self.q, self.s = q, s
        self.x, self.zh, self.y = q // 16, (q // 4) % 4, q % 4
        self.zl, self.c = s // 2, s % 2
        self.v = (1 - self.c) * self.y + self.c * self.x
        self.w = (1 - self.c) * self.x + self.c * self.y
        self.zpeer = (q, (1 - self.zl) * 2 + self.c)
        self.cpeer = (q, self.zl * 2 + 1 - self.c)
        self.zcpeer = (q, (1 - self.zl) * 2 + 1 - self.c)
        self.n = span_of(self.x, self.zh, self.y)
        self.next = (device_of(self.n + 1), s)
        self.previous = (device_of(self.n + 63), s)
        self.worker, self.holder = device_of(q), self.n
        self.worker_before, self.holder_after = device_of(q + 63), (self.n + 1) % 64
        self.final, self.final_source = (self.n + 2) % 64, device_of(q + 62)

    def cell(self, v, w):
        x = self.c * v + (1 - self.c) * w
        y = (1 - self.c) * v + self.c * w
        return x * 4 + y

    def ring(self, v, w):
        x = self.c * v + (1 - self.c) * w
        y = (1 - self.c) * v + self.c * w
        return ((x * 4 + self.zh) * 4 + y, self.s)

    def up(self, dz):
        return ((self.x * 4 + (self.zh + dz) % 4) * 4 + self.y, self.s)

    def beside(self, dz):
        z = (self.zh * 2 + self.zl + dz) % 8
        return ((self.x * 4 + z // 2) * 4 + self.y, (z % 2) * 2 + self.c)


class Copies:
    def __init__(self, send, recv):
        self.send, self.recv, self.started = send, recv, []

    def start(self, src, dst, target):
        i = len(self.started)
        assert i < COPIES
        op = pltpu.make_async_remote_copy(
            src_ref=src,
            dst_ref=dst,
            send_sem=self.send.at[i],
            recv_sem=self.recv.at[i],
            device_id=target,
            device_id_type=MESH,
        )
        op.start()
        self.started.append(op)
        return op

    def route(self, src, dst, target, me):
        same = (target[0] == me[0]) & (target[1] == me[1])
        op = Routed(src, dst, same)
        i = len(self.started)
        op.remote = pltpu.make_async_remote_copy(
            src_ref=src,
            dst_ref=dst,
            send_sem=self.send.at[i],
            recv_sem=self.recv.at[i],
            device_id=target,
            device_id_type=MESH,
        )
        pl.when(jnp.logical_not(same))(op.remote.start)
        pl.when(same)(op.keep)
        self.started.append(op)
        return op

    def drain(self):
        for op in self.started:
            op.wait_send()


class Routed:
    def __init__(self, src, dst, same):
        self.src, self.dst, self.same = src, dst, same

    def keep(self):
        self.dst[...] = self.src[...]

    def wait_recv(self):
        pl.when(jnp.logical_not(self.same))(self.remote.wait_recv)

    def wait_send(self):
        pl.when(jnp.logical_not(self.same))(self.remote.wait_send)


def greet(partners, perhaps, me):
    barrier = pltpu.get_barrier_semaphore()
    count = len(partners)
    for partner in partners:
        pl.semaphore_signal(barrier, inc=1, device_id=partner, device_id_type=MESH)
    for partner in perhaps:
        other = (partner[0] != me[0]) | (partner[1] != me[1])

        @pl.when(other)
        def _():
            pl.semaphore_signal(barrier, inc=1, device_id=partner, device_id_type=MESH)

        count = count + jnp.where(other, 1, 0)
    pl.semaphore_wait(barrier, count)


class Stream:
    def __init__(self, place, copies, buf, columns):
        self.p, self.copies, self.buf, self.columns = place, copies, buf, columns
        self.ops = {}

    def copy(self, key, rows, count, target):
        part = self.buf.at[pl.ds(pl.multiple_of(rows, 16), count), pl.ds(*self.columns)]
        self.ops[key] = self.copies.start(part, part, target)

    def place(self, piece):
        p = self.p
        self.row = pl.multiple_of((p.cell(p.v, p.w) * 4 + p.zh) * 16, 16)
        self.buf[pl.ds(self.row, 16), pl.ds(*self.columns)] = piece

    def z(self):
        for d in (1, 3, 2):
            self.copy(("z", d), self.row, 16, self.p.up(d))

    def both(self, key, v, w, right, left):
        rows = self.p.cell(v, w) * 64
        self.copy((key, "R"), rows, 64, right)
        self.copy((key, "L"), rows, 64, left)

    def w_sends(self, k):
        p = self.p
        v = (p.v + (0, 3, 1, 2)[k]) % 4
        self.both(("w", k), v, p.w, p.ring(p.v, (p.w + 1) % 4), p.ring(p.v, (p.w + 3) % 4))

    def v1(self):
        p = self.p
        for d in (1, 3, 2):
            self.ops["z", d].wait_recv()
        self.both("v", p.v, p.w, p.ring((p.v + 1) % 4, p.w), p.ring((p.v + 3) % 4, p.w))
        self.w_sends(0)

    def v2(self):
        p = self.p
        self.ops["v", "R"].wait_recv()
        self.copy("vfR", p.cell((p.v + 3) % 4, p.w) * 64, 32, p.ring((p.v + 1) % 4, p.w))
        self.w_sends(1)
        self.ops["v", "L"].wait_recv()
        self.copy("vfL", p.cell((p.v + 1) % 4, p.w) * 64 + 32, 32, p.ring((p.v + 3) % 4, p.w))
        self.w_sends(2)

    def w_forward(self, *blocks):
        p = self.p
        for k in blocks:
            v = (p.v + (0, 3, 1, 2)[k]) % 4
            self.ops[("w", k), "R"].wait_recv()
            self.copy(("wfR", k), p.cell(v, (p.w + 3) % 4) * 64, 32, p.ring(p.v, (p.w + 1) % 4))
            self.ops[("w", k), "L"].wait_recv()
            self.copy(("wfL", k), p.cell(v, (p.w + 1) % 4) * 64 + 32, 32, p.ring(p.v, (p.w + 3) % 4))

    def v3(self):
        self.ops["vfR"].wait_recv()
        self.ops["vfL"].wait_recv()
        self.w_sends(3)

    def end(self):
        for k in range(4):
            self.ops["wfR", k].wait_recv()
            self.ops["wfL", k].wait_recv()


class Spread:
    def __init__(self, place, copies, buf, first):
        self.p, self.copies, self.buf, self.first = place, copies, buf, first
        self.ops = []

    def part(self, slot, rows, count):
        return self.buf.at[pl.ds(pl.multiple_of(rows, 16), count), pl.ds(self.first + LANES * slot, LANES)]

    def block(self, dw):
        p = self.p
        for v in range(4):
            rows = p.cell(v, (p.w + dw) % 4) * 64
            to = p.beside(1 if v < 2 else 7)
            self.ops.append(self.copies.start(self.part(0, rows, 64), self.part(1, rows, 64), to))

    def rest(self):
        self.ops.append(
            self.copies.start(self.part(0, MAIN, REST), self.part(1, MAIN, REST), self.p.zpeer)
        )

    def core(self, slot):
        return self.copies.start(
            self.part(slot, 0, WIDTH), self.part(slot + 2, 0, WIDTH), self.p.cpeer
        )

    def wait(self):
        for op in self.ops:
            op.wait_recv()


def nt_dot(a, b):
    return lax.dot_general(a, b, (((1,), (1,)), ((), ())), preferred_element_type=F32)


def dot(a, b):
    return jnp.dot(a, b, preferred_element_type=F32)


def halves(array):
    high = array.astype(BF)
    return high, (array - high.astype(F32)).astype(BF)


def thirds(array):
    high = array.astype(BF)
    rest = array - high.astype(F32)
    middle = rest.astype(BF)
    return high, middle, (rest - middle.astype(F32)).astype(BF)


def iotas(shape):
    return [lax.broadcasted_iota(jnp.int32, shape, axis) for axis in (0, 1)]


def head_masks(rows):
    lane = lax.broadcasted_iota(jnp.int32, (rows, HEAD_COLUMNS), 1)
    return [(lane >= HEAD_DIM * h) & (lane < HEAD_DIM * (h + 1)) for h in range(4)]


def kernel(
    latents,
    fresh_noise,
    level_index,
    step_sizes,
    time_table,
    embed_in,
    spatial_qkv,
    spatial_out,
    temporal_qkv,
    temporal_out,
    embed_out,
    out,
    in_latents,
    in_noise,
    in_table,
    in_embed,
    in_qkv,
    in_out,
    in_velocity,
    first,
    out_s,
    second,
    lat_own,
    lat_pieces,
    lat_second,
    lat_last,
    last_send,
    mods_own,
    mods_here,
    features,
    features_new,
    embed_six,
    out_three,
    hidden,
    normed,
    lower,
    query,
    kv,
    before,
    after,
    mixes,
    mix_last,
    same_head,
    out_turned,
    local,
    send,
    recv,
):
    p = Place()
    copies = Copies(send, recv)
    fetches = [
        pltpu.make_async_copy(src, dst, local.at[i])
        for i, (src, dst) in enumerate(
            (
                (spatial_qkv, in_qkv.at[0]),
                (temporal_qkv, in_qkv.at[1]),
                (spatial_out, in_out.at[0]),
                (temporal_out, in_out.at[1]),
                (latents, in_latents),
                (fresh_noise, in_noise),
                (embed_in, in_embed),
                (embed_out, in_velocity),
                (time_table, in_table),
            )
        )
    ]
    for fetch in fetches:
        fetch.start()
    partners = [p.up(d) for d in (1, 2, 3)]
    partners += [p.ring((p.v + d) % 4, p.w) for d in (1, 3)]
    partners += [p.ring(p.v, (p.w + d) % 4) for d in (1, 3)]
    partners += [p.beside(1), p.beside(7), p.cpeer, p.zcpeer]
    partners += [p.next, p.previous]
    me = (p.q, p.s)
    perhaps = [(q, s) for q in (p.worker, p.holder) for s in range(4)]
    perhaps += [(q, p.s) for q in (p.worker_before, p.holder_after, p.final, p.final_source)]
    greet(partners, perhaps, me)
    a = Stream(p, copies, first, (0, 1152))
    b = Stream(p, copies, out_s, (0, LANES))
    c = Stream(p, copies, second, (0, 1152))
    spread_s = Spread(p, copies, out_s, 0)
    spread_t = Spread(p, copies, second, 768)
    position = p.n

    for fetch in fetches[:4]:
        fetch.wait()
    to, source = iotas((16, 18))
    leading = jnp.where(to == source, 1.0, 0.0).astype(BF)
    rest = jnp.zeros((16, HEAD_COLUMNS), F32)
    blocks = []
    for t in range(2):
        for j in range(4):
            chosen = (source >= 16) & (to == 8 * t + 4 * (source - 16) + j)
            chosen = jnp.where(chosen, 1.0, 0.0).astype(BF)
            block = in_qkv[t, :, j, :] if j < 3 else in_out[t]
            blocks.append(dot(leading, block))
            rest = rest + dot(chosen, block)
    a.place(jnp.concatenate(blocks[:3] + [rest], axis=1).astype(BF))
    a.z()
    pad = jnp.zeros((16, LANES - HEAD_COLUMNS), F32)
    b.place(jnp.concatenate([blocks[3], pad], axis=1).astype(BF))
    b.z()
    c.place(jnp.concatenate(blocks[4:], axis=1).astype(BF))

    for fetch in fetches[4:]:
        fetch.wait()
    sub, lane = iotas((16, 512))
    diagonal = (lane & 15) == sub
    token, lane = iotas((32, 512))
    repeat = jnp.where((lane >> 4) == token, 1.0, 0.0).astype(BF)

    def unflatten(line):
        wide = jnp.where(diagonal, jnp.broadcast_to(line, (16, 512)), 0.0)
        high, middle, low = thirds(wide)
        return nt_dot(high, repeat) + nt_dot(middle, repeat) + nt_dot(low, repeat)

    lines = [in_latents[f : f + 1, :] for f in range(2)] + [in_noise[0, f : f + 1, :] for f in range(2)]
    lat_own[...] = jnp.concatenate([unflatten(line) for line in lines], axis=1)

    def share(pieces):
        own = pieces.at[p.s]
        return [copies.start(own, own, t) for t in (p.cpeer, p.zpeer, p.zcpeer)]

    def whole(pieces):
        parts = [pieces[s, :, 32 * f : 32 * f + 32] for f in range(2) for s in range(4)]
        return jnp.concatenate(parts, axis=1)

    lat_ops = [
        copies.route(lat_own, lat_pieces.at[p.s], (p.worker, s), me)
        for s in (p.s, p.cpeer[1], p.zpeer[1], p.zcpeer[1])
    ]
    last_noise = jnp.concatenate(
        [unflatten(in_noise[1, f : f + 1, :]) for f in range(2)] + [jnp.zeros((16, 64), F32)], axis=1
    )

    levels = [level_index[0, step] for step in range(STEPS)]
    small = jnp.concatenate(
        [in_embed[...], in_velocity[...], in_table[levels[0]], in_table[levels[1]], jnp.zeros((4, WIDTH), F32)],
        axis=0,
    )
    for i, part in enumerate(thirds(small)):
        features[48 * i : 48 * i + 40, :] = part
        features[48 * i + 40 : 48 * i + 48, :] = jnp.zeros((8, WIDTH), BF)
    new = lax.broadcasted_iota(jnp.int32, (1, WIDTH), 1)
    late = new - MAIN
    piece = jnp.where(new < MAIN, new >> 4, late >> 1)
    within = jnp.where(new < MAIN, new & 15, 16 + (late & 1))
    owner = (piece & 48) + ((piece & 3) << 2) + ((piece >> 2) & 3)
    old = owner * 18 + within
    features_new[...] = jnp.zeros((144, WIDTH), F32)

    def reorder(i, carry):
        row = lax.broadcasted_iota(jnp.int32, (128, WIDTH), 0) + i * 128
        move = jnp.where(row == old, 1.0, 0.0).astype(BF)
        features_new[...] += dot(features[:, pl.ds(pl.multiple_of(i * 128, 128), 128)], move)
        return carry

    lax.fori_loop(0, 9, reorder, 0)
    parts = [features_new[48 * i : 48 * i + 16, :] for i in range(3)]
    embed_six[...] = jnp.concatenate([parts[i] for i in (0, 1, 0, 1, 2, 0)], axis=0).astype(BF)
    out_three[...] = jnp.concatenate(
        [features_new[48 * i + 16 : 48 * i + 32, :] for i in range(3)], axis=0
    ).astype(BF)
    mods = features_new[32:36, :] + features_new[80:84, :] + features_new[128:132, :]
    for step in range(STEPS):
        size_line = jnp.full((1, WIDTH), step_sizes[levels[step]], F32)
        lines = [mods[2 * step : 2 * step + 2], size_line, jnp.zeros((5, WIDTH), F32)]
        mods_own[step] = jnp.concatenate(lines, axis=0)
    mods_ops = [
        copies.route(mods_own.at[step], mods_here.at[step], (target, p.s), me)
        for step, target in enumerate((p.worker, p.worker_before))
    ]

    row, column = iotas((HEAD_COLUMNS, HEAD_COLUMNS))
    same = jnp.zeros((HEAD_COLUMNS, HEAD_COLUMNS), F32)
    for h in range(4):
        low, high = HEAD_DIM * h, HEAD_DIM * (h + 1)
        inside = (row >= low) & (row < high) & (column >= low) & (column < high)
        same = jnp.where(inside, 1.0, same)
    same_head[...] = same.astype(BF)

    def embed(lat):
        high, middle, low = (part.astype(F32) for part in thirds(lat))
        stack = jnp.concatenate([high, high, middle, middle, high, low], axis=0)
        hidden[...] = dot(stack.T.astype(BF), embed_six[...])

    def normalise(step, frames=(0, 1)):
        shift, scale = mods_here[step, 0:1, :], 1.0 + mods_here[step, 1:2, :]

        def rows_of(i, carry):
            rows = pl.ds(pl.multiple_of(i * 32, 32), 32)
            h = hidden[rows, :]
            inverse = lax.rsqrt(jnp.mean(h * h, axis=-1, keepdims=True) + 1e-06)
            normed[rows, :] = (h * inverse * scale + shift).astype(BF)
            return carry

        lax.fori_loop(4 * frames[0], 4 * frames[-1] + 4, rows_of, 0, unroll=True)

    def project_kv(weights, half, rows=slice(0, 256)):
        kv[half, rows, :] = dot(normed[rows, :], weights[:, 256:896]).astype(BF)

    def project_query(weights):
        query[...] = dot(normed[...], weights[:, :384])

    def attend_frame(half, frame, mix):
        rows = slice(128 * frame, 128 * frame + 128)
        masks = head_masks(128)
        q = query[rows, :HEAD_COLUMNS].astype(BF).astype(F32)
        both = kv[half, rows, :].astype(F32)
        k = both[:, 32 : 32 + HEAD_COLUMNS].astype(BF)
        v = both[:, 320 : 320 + HEAD_COLUMNS]
        q_heads = jnp.concatenate([jnp.where(m, q, 0.0).astype(BF) for m in masks], axis=0)
        v_heads = jnp.concatenate([jnp.where(m, v, 0.0).astype(BF) for m in masks], axis=0)
        scores = nt_dot(q_heads, k) * INVERSE
        scores = jnp.exp(scores - jnp.max(scores, axis=-1, keepdims=True))
        probs = (scores / jnp.sum(scores, axis=-1, keepdims=True)).astype(BF)
        probs = jnp.concatenate([probs[128 * h : 128 * h + 128] for h in range(4)], axis=1)
        mixed = dot(probs, v_heads)
        mixed = jnp.concatenate([mixed, jnp.zeros((128, LANES - HEAD_COLUMNS), F32)], axis=1)
        mix[rows, :LANES] = mixed.astype(BF)

    def start_mix(mix, frame):
        part = lambda slot: mix.at[pl.ds(128 * frame, 128), pl.ds(LANES * slot, LANES)]
        by_z = copies.start(part(0), part(1), p.zpeer)
        by_core = copies.start(part(0), part(2), p.cpeer)
        return by_z, by_core, part

    def finish_mix(started):
        last = []
        for by_z, _, part in started:
            by_z.wait_recv()
            last.append(copies.start(part(1), part(3), p.cpeer))

        def wait(frame):
            started[frame][1].wait_recv()
            last[frame].wait_recv()

        return wait

    def spatial_out(mix, frame, turned=False):
        rows = slice(128 * frame, 128 * frame + 128)
        if turned:
            hidden[rows, :] += dot(mix[rows, :], out_turned[...])
        else:
            hidden[rows, :] += nt_dot(mix[rows, :], out_s[...])

    def start_halo(half, frame):
        rows = kv.at[half, pl.ds(128 * frame, 128)]
        if frame == 1:
            return copies.start(rows, before.at[half], p.next)
        return copies.start(rows, after.at[half], p.previous)

    def temporal(half, halo, first_place, last_place, prepare):
        prepare()

        def keys_values(ref_value):
            both = ref_value.astype(F32)
            return both[:, 32 : 32 + HEAD_COLUMNS], both[:, 320 : 320 + HEAD_COLUMNS]

        def score(q, k):
            high, low = halves(q * k)
            same_now = same_head[...]
            return (dot(high, same_now) + dot(low, same_now)) * INVERSE

        q0 = query[:128, :HEAD_COLUMNS].astype(BF).astype(F32)
        q1 = query[128:, :HEAD_COLUMNS].astype(BF).astype(F32)
        k0, v0 = keys_values(kv[half, :128])
        k1, v1 = keys_values(kv[half, 128:])
        s00, s01, s10, s11 = score(q0, k0), score(q0, k1), score(q1, k0), score(q1, k1)

        def blend(sa, sb, sc, va, vb, vc):
            top = jnp.maximum(jnp.maximum(sa, sb), sc)
            ea, eb, ec = jnp.exp(sa - top), jnp.exp(sb - top), jnp.exp(sc - top)
            total = ea + eb + ec
            rounded = lambda e: (e / total).astype(BF).astype(F32)
            mixed = rounded(ea) * va + rounded(eb) * vb + rounded(ec) * vc
            return jnp.concatenate([jnp.zeros((128, LANES - HEAD_COLUMNS), F32), mixed], axis=1).astype(BF)

        halo[0].wait_recv()
        ka, va = keys_values(after[half])
        sa = jnp.where(position == last_place, -1e30, score(q1, ka))
        yield 1, blend(s10, s11, sa, v0, v1, va)
        halo[1].wait_recv()
        kb, vb = keys_values(before[half])
        sb = jnp.where(position == first_place, -1e30, score(q0, kb))
        yield 0, blend(sb, s00, s01, vb, v0, v1)

    def velocity(ref, rows):
        def rows_of(i, carry):
            part = pl.ds(pl.multiple_of(i * 32, 32), 32)
            h = ref[part, :]
            h = h * lax.rsqrt(jnp.mean(h * h, axis=-1, keepdims=True) + 1e-06)
            normed[part, :], lower[part, :] = halves(h)
            return carry

        lax.fori_loop(0, rows // 32, rows_of, 0, unroll=True)
        both = nt_dot(out_three[...], normed[:rows, :]) + nt_dot(out_three[...], lower[:rows, :])
        return both[:16] + both[16:32] + both[32:48]

    def selected(j, t):
        target = lax.broadcasted_iota(jnp.int32, (REST, MAIN), 0)
        source = lax.broadcasted_iota(jnp.int32, (REST, MAIN), 1)
        choose = jnp.where(source == 8 * target - 4 * (target % 2) + 8 * t + j, 1.0, 0.0).astype(BF)
        return dot(choose, first[:MAIN, 768:1152])[:, 96:]

    own = pl.multiple_of(p.s * 32, 32)

    def exchange_tokens(mix, last, mixed_frames):
        ops = []
        for frame, mixed in mixed_frames:
            mix[128 * frame : 128 * frame + 128, :LANES] = mixed
            for slot, peer in ((1, p.zpeer), (3, p.zcpeer), (2, p.cpeer)):
                theirs = pl.multiple_of(128 * frame + peer[1] * 32, 32)
                ops.append(
                    copies.start(
                        mix.at[pl.ds(theirs, 32), pl.ds(0, LANES)],
                        last.at[pl.ds(32 * frame, 32), pl.ds(LANES * slot, LANES)],
                        peer,
                    )
                )
            mine = pl.ds(pl.multiple_of(128 * frame + own, 32), 32)
            last[32 * frame : 32 * frame + 32, :LANES] = mix[mine, :LANES]
        return ops

    def move_tokens(last):
        h = jnp.concatenate([hidden[pl.ds(own, 32), :], hidden[pl.ds(own + 128, 32), :]], axis=0)
        hidden[:64, :] = h + nt_dot(last[...], second[:, 768:])
        return velocity(hidden, 64)

    a.v1()
    c.z()
    for op in lat_ops:
        op.wait_recv()
    embed(whole(lat_pieces))
    a.v2()
    a.w_forward(0)
    b.v1()
    for op in mods_ops:
        op.wait_recv()
    normalise(0)
    a.v3()
    b.v2()
    a.w_forward(1, 2)
    b.w_forward(0)
    b.v3()
    a.w_forward(3)
    b.w_forward(1, 2)
    c.v1()
    spread_s.block(0)
    a.end()

    blocks = [selected(j, 0) for j in range(3)]
    pad = jnp.zeros((REST, 96), F32)
    first[MAIN:, :896] = jnp.concatenate(blocks + [pad[:, :32]], axis=1).astype(BF)
    b.w_forward(3)
    spread_s.block(3)
    spread_s.block(1)
    c.v2()
    c.w_forward(0)
    project_kv(first, 0)
    project_query(first)
    b.end()
    spread_s.block(2)
    c.v3()
    out_s[MAIN:, :LANES] = jnp.concatenate([selected(3, 0), pad], axis=1).astype(BF)
    spread_s.rest()
    cores_s = [spread_s.core(0)]
    mix = mixes.at[0]
    attend_frame(0, 0, mix)
    started = [start_mix(mix, 0)]
    c.w_forward(1, 2)
    attend_frame(0, 1, mix)
    started.append(start_mix(mix, 1))
    c.w_forward(3)
    spread_t.block(0)
    spread_t.block(3)
    spread_t.block(1)
    spread_s.wait()
    cores_s.append(spread_s.core(1))
    wait_mix = finish_mix(started)
    blocks = [selected(j, 1) for j in range(4)]
    second[MAIN:, :1152] = jnp.concatenate(blocks, axis=1).astype(BF)
    for op in cores_s:
        op.wait_recv()
    halo = []
    for frame in range(2):
        wait_mix(frame)
        spatial_out(mix, frame)
        normalise(0, (frame,))
        if frame == 0:
            c.end()
        project_kv(second, 1, slice(128 * frame, 128 * frame + 128))
        halo.append(start_halo(1, frame))
    cores_t = []

    def meanwhile():
        spread_t.rest()
        spread_t.block(2)
        cores_t.append(spread_t.core(0))
        project_query(second)
        out_turned[...] = out_s[...].T

    ops = exchange_tokens(mixes.at[1], mix_last.at[0], temporal(1, halo, 0, 63, meanwhile))
    spread_t.wait()
    cores_t.append(spread_t.core(1))
    for op in ops + cores_t:
        op.wait_recv()
    moved = lat_pieces[p.s, :, :64] - mods_here[0, 2:3, :64] * move_tokens(mix_last.at[0])
    moved = jnp.where(position == 63, lat_pieces[p.s, :, 64:], moved)
    lat_second[p.s] = jnp.concatenate([moved, jnp.zeros((16, 64), F32)], axis=1)
    for op in share(lat_second):
        op.wait_recv()

    embed(whole(lat_second))
    normalise(1)
    project_kv(first, 2)
    project_query(first)
    mix = mixes.at[2]
    started = []
    for frame in range(2):
        attend_frame(2, frame, mix)
        started.append(start_mix(mix, frame))
    wait_mix = finish_mix(started)
    halo = []
    for frame in range(2):
        wait_mix(frame)
        spatial_out(mix, frame, True)
        normalise(1, (frame,))
        project_kv(second, 3, slice(128 * frame, 128 * frame + 128))
        halo.append(start_halo(3, frame))
    ops = exchange_tokens(
        mixes.at[3], mix_last.at[1], temporal(3, halo, 63, 62, lambda: project_query(second))
    )
    for op in ops:
        op.wait_recv()
    moved = lat_second[p.s, :, :64] - mods_here[1, 2:3, :64] * move_tokens(mix_last.at[1])
    last_send[...] = jnp.concatenate([moved, jnp.zeros((16, 64), F32)], axis=1)
    shifted = copies.route(last_send, lat_last, (p.final, p.s), me)
    shifted.wait_recv()
    final = jnp.where(p.q == 0, last_noise, lat_last[...])
    for f in range(2):
        high, middle, low = thirds(final[:, 32 * f : 32 * f + 32])
        wide = dot(high, repeat) + dot(middle, repeat) + dot(low, repeat)
        out[f : f + 1, :] = jnp.sum(jnp.where(diagonal, wide, 0.0), axis=0, keepdims=True)
    copies.drain()


def per_device(*operands):
    operands = [operand.T if i in (7, 9, 10) else operand for i, operand in enumerate(operands)]
    smem, whole = pl.BlockSpec(memory_space=pltpu.SMEM), pl.BlockSpec(memory_space=pl.ANY)
    specs = [smem if i in (2, 3) else whole for i in range(len(operands))]
    return pl.pallas_call(
        kernel,
        out_shape=jax.ShapeDtypeStruct((2, 512), F32),
        in_specs=specs,
        out_specs=pl.BlockSpec(memory_space=pltpu.VMEM),
        scratch_shapes=[
            pltpu.VMEM((2, 512), F32),
            pltpu.VMEM((2, 2, 512), F32),
            pltpu.VMEM((30, 2, WIDTH), F32),
            pltpu.VMEM((16, WIDTH), F32),
            pltpu.VMEM((2, 18, 3, HEAD_COLUMNS), BF),
            pltpu.VMEM((2, 18, HEAD_COLUMNS), BF),
            pltpu.VMEM((16, WIDTH), F32),
            pltpu.VMEM((WIDTH, 1152), BF),
            pltpu.VMEM((WIDTH, 4 * LANES), BF),
            pltpu.VMEM((WIDTH, 768 + 4 * LANES), BF),
            pltpu.VMEM((16, 128), F32),
            pltpu.VMEM((4, 16, 128), F32),
            pltpu.VMEM((4, 16, 128), F32),
            pltpu.VMEM((16, 128), F32),
            pltpu.VMEM((16, 128), F32),
            pltpu.VMEM((2, 8, WIDTH), F32),
            pltpu.VMEM((2, 8, WIDTH), F32),
            pltpu.VMEM((144, WIDTH), BF),
            pltpu.VMEM((144, WIDTH), F32),
            pltpu.VMEM((96, WIDTH), BF),
            pltpu.VMEM((48, WIDTH), BF),
            pltpu.VMEM((256, WIDTH), F32),
            pltpu.VMEM((256, WIDTH), BF),
            pltpu.VMEM((256, WIDTH), BF),
            pltpu.VMEM((256, LANES), F32),
            pltpu.VMEM((4, 256, 640), BF),
            pltpu.VMEM((4, 128, 640), BF),
            pltpu.VMEM((4, 128, 640), BF),
            pltpu.VMEM((4, 256, 4 * LANES), BF),
            pltpu.VMEM((2, 64, 4 * LANES), BF),
            pltpu.VMEM((HEAD_COLUMNS, HEAD_COLUMNS), BF),
            pltpu.VMEM((4 * LANES, WIDTH), BF),
            pltpu.SemaphoreType.DMA((9,)),
            pltpu.SemaphoreType.DMA((COPIES,)),
            pltpu.SemaphoreType.DMA((COPIES,)),
        ],
        compiler_params=pltpu.CompilerParams(
            collective_id=0, has_side_effects=True, vmem_limit_bytes=56 * 2**20
        ),
        name="denoise",
    )(*operands)


def solution(mesh):
    placed = (
        P("queue", "space"),
        P(None, None, "space"),
        P("queue", None),
        P(),
        P(),
        P(),
        P("queue", None, "space"),
        P("space", "queue"),
        P("queue", None, "space"),
        P("space", "queue"),
        P(),
    )
    return jax.shard_map(
        per_device, mesh=mesh, in_specs=placed, out_specs=P("queue", "space"), check_vma=False
    )
```

```python
import functools

import jax
import jax.numpy as jnp
from jax import lax
from jax.experimental import pallas as pl
from jax.experimental.pallas import tpu as pltpu
from jax.sharding import PartitionSpec as P

STEPS = 2
BF = jnp.bfloat16
F32 = jnp.float32


MESH = pl.DeviceIdType.MESH
MAIN, REST = 1024, 128
WIDTH = MAIN + REST
HEAD_COLUMNS = 288
HEAD_DIM = 72
INVERSE = 1.0 / HEAD_DIM**0.5
LANES = 384
COPIES = 160


def device_of(n):
    n = (n + 2) % 64
    r, j = n // 4, n % 4
    x, i = r // 4, r % 4
    zh = i + (x % 2) * (3 - 2 * i)
    y = j + (r % 2) * (3 - 2 * j)
    return (x * 4 + zh) * 4 + y


def span_of(x, zh, y):
    r = x * 4 + zh + (x % 2) * (3 - 2 * zh)
    return (r * 4 + y + (r % 2) * (3 - 2 * y) + 62) % 64


class Place:
    def __init__(self):
        q, s = lax.axis_index("queue"), lax.axis_index("space")
        self.q, self.s = q, s
        self.x, self.zh, self.y = q // 16, (q // 4) % 4, q % 4
        self.zl, self.c = s // 2, s % 2
        self.v = (1 - self.c) * self.y + self.c * self.x
        self.w = (1 - self.c) * self.x + self.c * self.y
        self.zpeer = (q, (1 - self.zl) * 2 + self.c)
        self.cpeer = (q, self.zl * 2 + 1 - self.c)
        self.zcpeer = (q, (1 - self.zl) * 2 + 1 - self.c)
        self.n = span_of(self.x, self.zh, self.y)
        self.next = (device_of(self.n + 1), s)
        self.previous = (device_of(self.n + 63), s)
        self.worker, self.holder = device_of(q), self.n
        self.worker_before, self.holder_after = device_of(q + 63), (self.n + 1) % 64
        self.final, self.final_source = (self.n + 2) % 64, device_of(q + 62)

    def cell(self, v, w):
        x = self.c * v + (1 - self.c) * w
        y = (1 - self.c) * v + self.c * w
        return x * 4 + y

    def ring(self, v, w):
        x = self.c * v + (1 - self.c) * w
        y = (1 - self.c) * v + self.c * w
        return ((x * 4 + self.zh) * 4 + y, self.s)

    def up(self, dz):
        return ((self.x * 4 + (self.zh + dz) % 4) * 4 + self.y, self.s)

    def beside(self, dz):
        z = (self.zh * 2 + self.zl + dz) % 8
        return ((self.x * 4 + z // 2) * 4 + self.y, (z % 2) * 2 + self.c)


class Copies:
    def __init__(self, send, recv):
        self.send, self.recv, self.started = send, recv, []

    def start(self, src, dst, target):
        i = len(self.started)
        assert i < COPIES
        op = pltpu.make_async_remote_copy(
            src_ref=src,
            dst_ref=dst,
            send_sem=self.send.at[i],
            recv_sem=self.recv.at[i],
            device_id=target,
            device_id_type=MESH,
        )
        op.start()
        self.started.append(op)
        return op

    def route(self, src, dst, target, me):
        same = (target[0] == me[0]) & (target[1] == me[1])
        op = Routed(src, dst, same)
        i = len(self.started)
        op.remote = pltpu.make_async_remote_copy(
            src_ref=src,
            dst_ref=dst,
            send_sem=self.send.at[i],
            recv_sem=self.recv.at[i],
            device_id=target,
            device_id_type=MESH,
        )
        pl.when(jnp.logical_not(same))(op.remote.start)
        pl.when(same)(op.keep)
        self.started.append(op)
        return op

    def drain(self):
        for op in self.started:
            op.wait_send()


class Routed:
    def __init__(self, src, dst, same):
        self.src, self.dst, self.same = src, dst, same

    def keep(self):
        self.dst[...] = self.src[...]

    def wait_recv(self):
        pl.when(jnp.logical_not(self.same))(self.remote.wait_recv)

    def wait_send(self):
        pl.when(jnp.logical_not(self.same))(self.remote.wait_send)


def greet(partners, perhaps, me):
    barrier = pltpu.get_barrier_semaphore()
    count = len(partners)
    for partner in partners:
        pl.semaphore_signal(barrier, inc=1, device_id=partner, device_id_type=MESH)
    for partner in perhaps:
        other = (partner[0] != me[0]) | (partner[1] != me[1])

        @pl.when(other)
        def _():
            pl.semaphore_signal(barrier, inc=1, device_id=partner, device_id_type=MESH)

        count = count + jnp.where(other, 1, 0)
    pl.semaphore_wait(barrier, count)


class Stream:
    def __init__(self, place, copies, buf, columns):
        self.p, self.copies, self.buf, self.columns = place, copies, buf, columns
        self.ops = {}

    def copy(self, key, rows, count, target):
        part = self.buf.at[pl.ds(pl.multiple_of(rows, 16), count), pl.ds(*self.columns)]
        self.ops[key] = self.copies.start(part, part, target)

    def place(self, piece):
        p = self.p
        self.row = pl.multiple_of((p.cell(p.v, p.w) * 4 + p.zh) * 16, 16)
        self.buf[pl.ds(self.row, 16), pl.ds(*self.columns)] = piece

    def z(self):
        for d in (2, 1, 3):
            self.copy(("z", d), self.row, 16, self.p.up(d))

    def both(self, key, v, w, right, left):
        rows = self.p.cell(v, w) * 64
        self.copy((key, "R"), rows, 64, right)
        self.copy((key, "L"), rows, 64, left)

    def w_sends(self, k):
        p = self.p
        v = (p.v + (0, 3, 1, 2)[k]) % 4
        self.both(("w", k), v, p.w, p.ring(p.v, (p.w + 1) % 4), p.ring(p.v, (p.w + 3) % 4))

    def v1(self):
        p = self.p
        for d in (1, 3, 2):
            self.ops["z", d].wait_recv()
        self.both("v", p.v, p.w, p.ring((p.v + 1) % 4, p.w), p.ring((p.v + 3) % 4, p.w))
        self.w_sends(0)

    def v2(self):
        p = self.p
        self.ops["v", "R"].wait_recv()
        self.copy("vfR", p.cell((p.v + 3) % 4, p.w) * 64, 32, p.ring((p.v + 1) % 4, p.w))
        self.w_sends(1)
        self.ops["v", "L"].wait_recv()
        self.copy("vfL", p.cell((p.v + 1) % 4, p.w) * 64 + 32, 32, p.ring((p.v + 3) % 4, p.w))
        self.w_sends(2)

    def w_forward(self, *blocks):
        p = self.p
        for k in blocks:
            v = (p.v + (0, 3, 1, 2)[k]) % 4
            self.ops[("w", k), "R"].wait_recv()
            self.copy(("wfR", k), p.cell(v, (p.w + 3) % 4) * 64, 32, p.ring(p.v, (p.w + 1) % 4))
            self.ops[("w", k), "L"].wait_recv()
            self.copy(("wfL", k), p.cell(v, (p.w + 1) % 4) * 64 + 32, 32, p.ring(p.v, (p.w + 3) % 4))

    def v3(self):
        self.ops["vfR"].wait_recv()
        self.ops["vfL"].wait_recv()
        self.w_sends(3)

    def end(self):
        for k in range(4):
            self.ops["wfR", k].wait_recv()
            self.ops["wfL", k].wait_recv()


class Spread:
    def __init__(self, place, copies, buf, first):
        self.p, self.copies, self.buf, self.first = place, copies, buf, first
        self.ops = []

    def part(self, slot, rows, count):
        return self.buf.at[pl.ds(pl.multiple_of(rows, 16), count), pl.ds(self.first + LANES * slot, LANES)]

    def block(self, dw):
        p = self.p
        for v in range(4):
            rows = p.cell(v, (p.w + dw) % 4) * 64
            to = p.beside(1 if v < 2 else 7)
            self.ops.append(self.copies.start(self.part(0, rows, 64), self.part(1, rows, 64), to))

    def rest(self):
        self.ops.append(
            self.copies.start(self.part(0, MAIN, REST), self.part(1, MAIN, REST), self.p.zpeer)
        )

    def core(self, slot):
        return self.copies.start(
            self.part(slot, 0, WIDTH), self.part(slot + 2, 0, WIDTH), self.p.cpeer
        )

    def wait(self):
        for op in self.ops:
            op.wait_recv()


def nt_dot(a, b):
    return lax.dot_general(a, b, (((1,), (1,)), ((), ())), preferred_element_type=F32)


def dot(a, b):
    return jnp.dot(a, b, preferred_element_type=F32)


def halves(array):
    high = array.astype(BF)
    return high, (array - high.astype(F32)).astype(BF)


def thirds(array):
    high = array.astype(BF)
    rest = array - high.astype(F32)
    middle = rest.astype(BF)
    return high, middle, (rest - middle.astype(F32)).astype(BF)


def iotas(shape):
    return [lax.broadcasted_iota(jnp.int32, shape, axis) for axis in (0, 1)]


def head_masks(rows):
    lane = lax.broadcasted_iota(jnp.int32, (rows, HEAD_COLUMNS), 1)
    return [(lane >= HEAD_DIM * h) & (lane < HEAD_DIM * (h + 1)) for h in range(4)]


def kernel(
    latents,
    fresh_noise,
    level_index,
    step_sizes,
    time_table,
    embed_in,
    spatial_qkv,
    spatial_out,
    temporal_qkv,
    temporal_out,
    embed_out,
    out,
    in_latents,
    in_noise,
    in_table,
    in_embed,
    in_qkv,
    in_out,
    in_velocity,
    first,
    out_s,
    second,
    lat_own,
    lat_pieces,
    lat_second,
    lat_last,
    last_send,
    mods_own,
    mods_here,
    features,
    features_new,
    embed_six,
    out_three,
    hidden,
    normed,
    lower,
    query,
    kv,
    before,
    after,
    mixes,
    mix_last,
    same_head,
    out_turned,
    local,
    send,
    recv,
):
    p = Place()
    copies = Copies(send, recv)
    fetches = [
        pltpu.make_async_copy(src, dst, local.at[i])
        for i, (src, dst) in enumerate(
            (
                (spatial_qkv, in_qkv.at[0]),
                (temporal_qkv, in_qkv.at[1]),
                (spatial_out, in_out.at[0]),
                (temporal_out, in_out.at[1]),
                (latents, in_latents),
                (fresh_noise, in_noise),
                (embed_in, in_embed),
                (embed_out, in_velocity),
                (time_table, in_table),
            )
        )
    ]
    for fetch in fetches:
        fetch.start()
    partners = [p.up(d) for d in (1, 2, 3)]
    partners += [p.ring((p.v + d) % 4, p.w) for d in (1, 3)]
    partners += [p.ring(p.v, (p.w + d) % 4) for d in (1, 3)]
    partners += [p.beside(1), p.beside(7), p.cpeer, p.zcpeer]
    partners += [p.next, p.previous]
    me = (p.q, p.s)
    perhaps = [(q, s) for q in (p.worker, p.holder) for s in range(4)]
    perhaps += [(q, p.s) for q in (p.worker_before, p.holder_after, p.final, p.final_source)]
    greet(partners, perhaps, me)
    a = Stream(p, copies, first, (0, 1152))
    b = Stream(p, copies, out_s, (0, LANES))
    c = Stream(p, copies, second, (0, 1152))
    spread_s = Spread(p, copies, out_s, 0)
    spread_t = Spread(p, copies, second, 768)
    position = p.n

    for fetch in fetches[:4]:
        fetch.wait()
    to, source = iotas((16, 18))
    leading = jnp.where(to == source, 1.0, 0.0).astype(BF)
    rest = jnp.zeros((16, HEAD_COLUMNS), F32)
    blocks = []
    for t in range(2):
        for j in range(4):
            chosen = (source >= 16) & (to == 8 * t + 4 * (source - 16) + j)
            chosen = jnp.where(chosen, 1.0, 0.0).astype(BF)
            block = in_qkv[t, :, j, :] if j < 3 else in_out[t]
            blocks.append(dot(leading, block))
            rest = rest + dot(chosen, block)
    a.place(jnp.concatenate(blocks[:3] + [rest], axis=1).astype(BF))
    a.z()
    pad = jnp.zeros((16, LANES - HEAD_COLUMNS), F32)
    b.place(jnp.concatenate([blocks[3], pad], axis=1).astype(BF))
    b.z()
    c.place(jnp.concatenate(blocks[4:], axis=1).astype(BF))

    for fetch in fetches[4:]:
        fetch.wait()
    sub, lane = iotas((16, 512))
    diagonal = (lane & 15) == sub
    token, lane = iotas((32, 512))
    repeat = jnp.where((lane >> 4) == token, 1.0, 0.0).astype(BF)

    def unflatten(line):
        wide = jnp.where(diagonal, jnp.broadcast_to(line, (16, 512)), 0.0)
        high, middle, low = thirds(wide)
        return nt_dot(high, repeat) + nt_dot(middle, repeat) + nt_dot(low, repeat)

    lines = [in_latents[f : f + 1, :] for f in range(2)] + [in_noise[0, f : f + 1, :] for f in range(2)]
    lat_own[...] = jnp.concatenate([unflatten(line) for line in lines], axis=1)

    def share(pieces):
        own = pieces.at[p.s]
        return [copies.start(own, own, t) for t in (p.cpeer, p.zpeer, p.zcpeer)]

    def whole(pieces):
        parts = [pieces[s, :, 32 * f : 32 * f + 32] for f in range(2) for s in range(4)]
        return jnp.concatenate(parts, axis=1)

    lat_ops = [
        copies.route(lat_own, lat_pieces.at[p.s], (p.worker, s), me)
        for s in (p.s, p.cpeer[1], p.zpeer[1], p.zcpeer[1])
    ]
    last_noise = jnp.concatenate(
        [unflatten(in_noise[1, f : f + 1, :]) for f in range(2)] + [jnp.zeros((16, 64), F32)], axis=1
    )

    levels = [level_index[0, step] for step in range(STEPS)]
    small = jnp.concatenate(
        [in_embed[...], in_velocity[...], in_table[levels[0]], in_table[levels[1]], jnp.zeros((4, WIDTH), F32)],
        axis=0,
    )
    for i, part in enumerate(thirds(small)):
        features[48 * i : 48 * i + 40, :] = part
        features[48 * i + 40 : 48 * i + 48, :] = jnp.zeros((8, WIDTH), BF)
    new = lax.broadcasted_iota(jnp.int32, (1, WIDTH), 1)
    late = new - MAIN
    piece = jnp.where(new < MAIN, new >> 4, late >> 1)
    within = jnp.where(new < MAIN, new & 15, 16 + (late & 1))
    owner = (piece & 48) + ((piece & 3) << 2) + ((piece >> 2) & 3)
    old = owner * 18 + within
    features_new[...] = jnp.zeros((144, WIDTH), F32)

    def reorder(i, carry):
        row = lax.broadcasted_iota(jnp.int32, (128, WIDTH), 0) + i * 128
        move = jnp.where(row == old, 1.0, 0.0).astype(BF)
        features_new[...] += dot(features[:, pl.ds(pl.multiple_of(i * 128, 128), 128)], move)
        return carry

    lax.fori_loop(0, 9, reorder, 0)
    parts = [features_new[48 * i : 48 * i + 16, :] for i in range(3)]
    embed_six[...] = jnp.concatenate([parts[i] for i in (0, 1, 0, 1, 2, 0)], axis=0).astype(BF)
    out_three[...] = jnp.concatenate(
        [features_new[48 * i + 16 : 48 * i + 32, :] for i in range(3)], axis=0
    ).astype(BF)
    mods = features_new[32:36, :] + features_new[80:84, :] + features_new[128:132, :]
    for step in range(STEPS):
        size_line = jnp.full((1, WIDTH), step_sizes[levels[step]], F32)
        lines = [mods[2 * step : 2 * step + 2], size_line, jnp.zeros((5, WIDTH), F32)]
        mods_own[step] = jnp.concatenate(lines, axis=0)
    mods_ops = [
        copies.route(mods_own.at[step], mods_here.at[step], (target, p.s), me)
        for step, target in enumerate((p.worker, p.worker_before))
    ]

    row, column = iotas((HEAD_COLUMNS, HEAD_COLUMNS))
    same = jnp.zeros((HEAD_COLUMNS, HEAD_COLUMNS), F32)
    for h in range(4):
        low, high = HEAD_DIM * h, HEAD_DIM * (h + 1)
        inside = (row >= low) & (row < high) & (column >= low) & (column < high)
        same = jnp.where(inside, 1.0, same)
    same_head[...] = same.astype(BF)

    def embed(lat):
        high, middle, low = (part.astype(F32) for part in thirds(lat))
        stack = jnp.concatenate([high, high, middle, middle, high, low], axis=0)
        hidden[...] = dot(stack.T.astype(BF), embed_six[...])

    def normalise(step, frames=(0, 1)):
        shift, scale = mods_here[step, 0:1, :], 1.0 + mods_here[step, 1:2, :]

        def rows_of(i, carry):
            rows = pl.ds(pl.multiple_of(i * 32, 32), 32)
            h = hidden[rows, :]
            inverse = lax.rsqrt(jnp.mean(h * h, axis=-1, keepdims=True) + 1e-06)
            normed[rows, :] = (h * inverse * scale + shift).astype(BF)
            return carry

        lax.fori_loop(4 * frames[0], 4 * frames[-1] + 4, rows_of, 0, unroll=True)

    def project_kv(weights, half, rows=slice(0, 256)):
        kv[half, rows, :] = dot(normed[rows, :], weights[:, 256:896]).astype(BF)

    def project_query(weights):
        query[...] = dot(normed[...], weights[:, :384])

    def attend_frame(half, frame, mix):
        rows = slice(128 * frame, 128 * frame + 128)
        masks = head_masks(128)
        q = query[rows, :HEAD_COLUMNS].astype(BF).astype(F32)
        both = kv[half, rows, :].astype(F32)
        k = both[:, 32 : 32 + HEAD_COLUMNS].astype(BF)
        v = both[:, 320 : 320 + HEAD_COLUMNS]
        q_heads = jnp.concatenate([jnp.where(m, q, 0.0).astype(BF) for m in masks], axis=0)
        v_heads = jnp.concatenate([jnp.where(m, v, 0.0).astype(BF) for m in masks], axis=0)
        scores = nt_dot(q_heads, k) * INVERSE
        scores = jnp.exp(scores - jnp.max(scores, axis=-1, keepdims=True))
        probs = (scores / jnp.sum(scores, axis=-1, keepdims=True)).astype(BF)
        probs = jnp.concatenate([probs[128 * h : 128 * h + 128] for h in range(4)], axis=1)
        mixed = dot(probs, v_heads)
        mixed = jnp.concatenate([mixed, jnp.zeros((128, LANES - HEAD_COLUMNS), F32)], axis=1)
        mix[rows, :LANES] = mixed.astype(BF)

    def start_mix(mix, frame):
        part = lambda slot: mix.at[pl.ds(128 * frame, 128), pl.ds(LANES * slot, LANES)]
        by_z = copies.start(part(0), part(1), p.zpeer)
        by_core = copies.start(part(0), part(2), p.cpeer)
        return by_z, by_core, part

    def finish_mix(started):
        last = []
        for by_z, _, part in started:
            by_z.wait_recv()
            last.append(copies.start(part(1), part(3), p.cpeer))

        def wait(frame):
            started[frame][1].wait_recv()
            last[frame].wait_recv()

        return wait

    def spatial_out(mix, frame, turned=False):
        rows = slice(128 * frame, 128 * frame + 128)
        if turned:
            hidden[rows, :] += dot(mix[rows, :], out_turned[...])
        else:
            hidden[rows, :] += nt_dot(mix[rows, :], out_s[...])

    def start_halo(half, frame):
        rows = kv.at[half, pl.ds(128 * frame, 128)]
        if frame == 1:
            return copies.start(rows, before.at[half], p.next)
        return copies.start(rows, after.at[half], p.previous)

    def temporal(half, halo, first_place, last_place, prepare):
        prepare()

        def keys_values(ref_value):
            both = ref_value.astype(F32)
            return both[:, 32 : 32 + HEAD_COLUMNS], both[:, 320 : 320 + HEAD_COLUMNS]

        def score(q, k):
            high, low = halves(q * k)
            same_now = same_head[...]
            return (dot(high, same_now) + dot(low, same_now)) * INVERSE

        q0 = query[:128, :HEAD_COLUMNS].astype(BF).astype(F32)
        q1 = query[128:, :HEAD_COLUMNS].astype(BF).astype(F32)
        k0, v0 = keys_values(kv[half, :128])
        k1, v1 = keys_values(kv[half, 128:])
        s00, s01, s10, s11 = score(q0, k0), score(q0, k1), score(q1, k0), score(q1, k1)

        def blend(sa, sb, sc, va, vb, vc):
            top = jnp.maximum(jnp.maximum(sa, sb), sc)
            ea, eb, ec = jnp.exp(sa - top), jnp.exp(sb - top), jnp.exp(sc - top)
            total = ea + eb + ec
            rounded = lambda e: (e / total).astype(BF).astype(F32)
            mixed = rounded(ea) * va + rounded(eb) * vb + rounded(ec) * vc
            return jnp.concatenate([jnp.zeros((128, LANES - HEAD_COLUMNS), F32), mixed], axis=1).astype(BF)

        halo[0].wait_recv()
        ka, va = keys_values(after[half])
        sa = jnp.where(position == last_place, -1e30, score(q1, ka))
        yield 1, blend(s10, s11, sa, v0, v1, va)
        halo[1].wait_recv()
        kb, vb = keys_values(before[half])
        sb = jnp.where(position == first_place, -1e30, score(q0, kb))
        yield 0, blend(sb, s00, s01, vb, v0, v1)

    def velocity(ref, rows):
        def rows_of(i, carry):
            part = pl.ds(pl.multiple_of(i * 32, 32), 32)
            h = ref[part, :]
            h = h * lax.rsqrt(jnp.mean(h * h, axis=-1, keepdims=True) + 1e-06)
            normed[part, :], lower[part, :] = halves(h)
            return carry

        lax.fori_loop(0, rows // 32, rows_of, 0, unroll=True)
        both = nt_dot(out_three[...], normed[:rows, :]) + nt_dot(out_three[...], lower[:rows, :])
        return both[:16] + both[16:32] + both[32:48]

    def selected(j, t):
        target = lax.broadcasted_iota(jnp.int32, (REST, MAIN), 0)
        source = lax.broadcasted_iota(jnp.int32, (REST, MAIN), 1)
        choose = jnp.where(source == 8 * target - 4 * (target % 2) + 8 * t + j, 1.0, 0.0).astype(BF)
        return dot(choose, first[:MAIN, 768:1152])[:, 96:]

    own = pl.multiple_of(p.s * 32, 32)

    def exchange_tokens(mix, last, mixed_frames):
        ops = []
        for frame, mixed in mixed_frames:
            mix[128 * frame : 128 * frame + 128, :LANES] = mixed
            for slot, peer in ((1, p.zpeer), (3, p.zcpeer), (2, p.cpeer)):
                theirs = pl.multiple_of(128 * frame + peer[1] * 32, 32)
                ops.append(
                    copies.start(
                        mix.at[pl.ds(theirs, 32), pl.ds(0, LANES)],
                        last.at[pl.ds(32 * frame, 32), pl.ds(LANES * slot, LANES)],
                        peer,
                    )
                )
            mine = pl.ds(pl.multiple_of(128 * frame + own, 32), 32)
            last[32 * frame : 32 * frame + 32, :LANES] = mix[mine, :LANES]
        return ops

    def move_tokens(last):
        h = jnp.concatenate([hidden[pl.ds(own, 32), :], hidden[pl.ds(own + 128, 32), :]], axis=0)
        hidden[:64, :] = h + nt_dot(last[...], second[:, 768:])
        return velocity(hidden, 64)

    a.v1()
    c.z()
    for op in lat_ops:
        op.wait_recv()
    embed(whole(lat_pieces))
    a.v2()
    a.w_forward(0)
    b.v1()
    for op in mods_ops:
        op.wait_recv()
    normalise(0)
    a.v3()
    b.v2()
    a.w_forward(1, 2)
    b.w_forward(0)
    b.v3()
    a.w_forward(3)
    b.w_forward(1, 2)
    c.v1()
    spread_s.block(0)
    a.end()

    blocks = [selected(j, 0) for j in range(3)]
    pad = jnp.zeros((REST, 96), F32)
    first[MAIN:, :896] = jnp.concatenate(blocks + [pad[:, :32]], axis=1).astype(BF)
    b.w_forward(3)
    spread_s.block(3)
    spread_s.block(1)
    c.v2()
    c.w_forward(0)
    project_kv(first, 0)
    project_query(first)
    b.end()
    spread_s.block(2)
    c.v3()
    out_s[MAIN:, :LANES] = jnp.concatenate([selected(3, 0), pad], axis=1).astype(BF)
    spread_s.rest()
    cores_s = [spread_s.core(0)]
    mix = mixes.at[0]
    attend_frame(0, 0, mix)
    started = [start_mix(mix, 0)]
    c.w_forward(1, 2)
    attend_frame(0, 1, mix)
    started.append(start_mix(mix, 1))
    c.w_forward(3)
    spread_t.block(0)
    spread_t.block(3)
    spread_t.block(1)
    spread_s.wait()
    cores_s.append(spread_s.core(1))
    wait_mix = finish_mix(started)
    blocks = [selected(j, 1) for j in range(4)]
    second[MAIN:, :1152] = jnp.concatenate(blocks, axis=1).astype(BF)
    for op in cores_s:
        op.wait_recv()
    halo = []
    for frame in range(2):
        wait_mix(frame)
        spatial_out(mix, frame)
        normalise(0, (frame,))
        if frame == 0:
            c.end()
        project_kv(second, 1, slice(128 * frame, 128 * frame + 128))
        halo.append(start_halo(1, frame))
    cores_t = []

    def meanwhile():
        spread_t.rest()
        spread_t.block(2)
        cores_t.append(spread_t.core(0))
        project_query(second)
        out_turned[...] = out_s[...].T

    ops = exchange_tokens(mixes.at[1], mix_last.at[0], temporal(1, halo, 0, 63, meanwhile))
    spread_t.wait()
    cores_t.append(spread_t.core(1))
    for op in ops + cores_t:
        op.wait_recv()
    moved = lat_pieces[p.s, :, :64] - mods_here[0, 2:3, :64] * move_tokens(mix_last.at[0])
    moved = jnp.where(position == 63, lat_pieces[p.s, :, 64:], moved)
    lat_second[p.s] = jnp.concatenate([moved, jnp.zeros((16, 64), F32)], axis=1)
    for op in share(lat_second):
        op.wait_recv()

    embed(whole(lat_second))
    normalise(1)
    project_kv(first, 2)
    project_query(first)
    mix = mixes.at[2]
    started = []
    for frame in range(2):
        attend_frame(2, frame, mix)
        started.append(start_mix(mix, frame))
    wait_mix = finish_mix(started)
    halo = []
    for frame in range(2):
        wait_mix(frame)
        spatial_out(mix, frame, True)
        normalise(1, (frame,))
        project_kv(second, 3, slice(128 * frame, 128 * frame + 128))
        halo.append(start_halo(3, frame))
    ops = exchange_tokens(
        mixes.at[3], mix_last.at[1], temporal(3, halo, 63, 62, lambda: project_query(second))
    )
    for op in ops:
        op.wait_recv()
    moved = lat_second[p.s, :, :64] - mods_here[1, 2:3, :64] * move_tokens(mix_last.at[1])
    last_send[...] = jnp.concatenate([moved, jnp.zeros((16, 64), F32)], axis=1)
    shifted = copies.route(last_send, lat_last, (p.final, p.s), me)
    shifted.wait_recv()
    final = jnp.where(p.q == 0, last_noise, lat_last[...])
    for f in range(2):
        high, middle, low = thirds(final[:, 32 * f : 32 * f + 32])
        wide = dot(high, repeat) + dot(middle, repeat) + dot(low, repeat)
        out[f : f + 1, :] = jnp.sum(jnp.where(diagonal, wide, 0.0), axis=0, keepdims=True)
    copies.drain()


def per_device(*operands):
    operands = [operand.T if i in (7, 9, 10) else operand for i, operand in enumerate(operands)]
    smem, whole = pl.BlockSpec(memory_space=pltpu.SMEM), pl.BlockSpec(memory_space=pl.ANY)
    specs = [smem if i in (2, 3) else whole for i in range(len(operands))]
    return pl.pallas_call(
        kernel,
        out_shape=jax.ShapeDtypeStruct((2, 512), F32),
        in_specs=specs,
        out_specs=pl.BlockSpec(memory_space=pltpu.VMEM),
        scratch_shapes=[
            pltpu.VMEM((2, 512), F32),
            pltpu.VMEM((2, 2, 512), F32),
            pltpu.VMEM((30, 2, WIDTH), F32),
            pltpu.VMEM((16, WIDTH), F32),
            pltpu.VMEM((2, 18, 3, HEAD_COLUMNS), BF),
            pltpu.VMEM((2, 18, HEAD_COLUMNS), BF),
            pltpu.VMEM((16, WIDTH), F32),
            pltpu.VMEM((WIDTH, 1152), BF),
            pltpu.VMEM((WIDTH, 4 * LANES), BF),
            pltpu.VMEM((WIDTH, 768 + 4 * LANES), BF),
            pltpu.VMEM((16, 128), F32),
            pltpu.VMEM((4, 16, 128), F32),
            pltpu.VMEM((4, 16, 128), F32),
            pltpu.VMEM((16, 128), F32),
            pltpu.VMEM((16, 128), F32),
            pltpu.VMEM((2, 8, WIDTH), F32),
            pltpu.VMEM((2, 8, WIDTH), F32),
            pltpu.VMEM((144, WIDTH), BF),
            pltpu.VMEM((144, WIDTH), F32),
            pltpu.VMEM((96, WIDTH), BF),
            pltpu.VMEM((48, WIDTH), BF),
            pltpu.VMEM((256, WIDTH), F32),
            pltpu.VMEM((256, WIDTH), BF),
            pltpu.VMEM((256, WIDTH), BF),
            pltpu.VMEM((256, LANES), F32),
            pltpu.VMEM((4, 256, 640), BF),
            pltpu.VMEM((4, 128, 640), BF),
            pltpu.VMEM((4, 128, 640), BF),
            pltpu.VMEM((4, 256, 4 * LANES), BF),
            pltpu.VMEM((2, 64, 4 * LANES), BF),
            pltpu.VMEM((HEAD_COLUMNS, HEAD_COLUMNS), BF),
            pltpu.VMEM((4 * LANES, WIDTH), BF),
            pltpu.SemaphoreType.DMA((9,)),
            pltpu.SemaphoreType.DMA((COPIES,)),
            pltpu.SemaphoreType.DMA((COPIES,)),
        ],
        compiler_params=pltpu.CompilerParams(
            collective_id=0, has_side_effects=True, vmem_limit_bytes=56 * 2**20
        ),
        name="denoise",
    )(*operands)


def solution(mesh):
    placed = (
        P("queue", "space"),
        P(None, None, "space"),
        P("queue", None),
        P(),
        P(),
        P(),
        P("queue", None, "space"),
        P("space", "queue"),
        P("queue", None, "space"),
        P("space", "queue"),
        P(),
    )
    return jax.shard_map(
        per_device, mesh=mesh, in_specs=placed, out_specs=P("queue", "space"), check_vma=False
    )
```
